512 devices in a mesh: dap: 128 (over x, y, z_hi, core), rep: 4 (over z_lo).
Axes of the slice: x: 4, y: 8, z: 8 (z_hi: 2, z_lo: 4; z = z_hi * 4 + z_lo), core: 2. Of those that a mesh axis runs over, the one named last changes fastest.
Arguments:
- alignment_source_tensor: float32 [256, 512, 256], P('dap'), may hold values from -6 to 6
- couple_source_tensor: float32 [512, 512, 128], P('dap', 'rep'), may hold values from -6 to 6
- horizontal_scale_factor: float32 [256], replicated, may hold values from 0.3 to 3
- horizontal_projection_matrix: bfloat16 [256, 1024], replicated, may hold values from -12 to 12
- couple_scale_factor: float32 [128], replicated, may hold values from 0.3 to 3
- couple_offset_matrix: bfloat16 [128, 8], replicated, may hold values from -0.5 to 0.5
- horizontal_final_matrix: bfloat16 [256, 256], replicated, may hold values from -1.5 to 1.5
- vertical_scale_factor: float32 [256], replicated, may hold values from 0.3 to 3
- vertical_projection_matrix: bfloat16 [256, 1024], replicated, may hold values from -12 to 12
- vertical_final_matrix: bfloat16 [256, 256], replicated, may hold values from -1.5 to 1.5
- tensorial_scale_factor: float32 [256], replicated, may hold values from 0.3 to 3
- tensorial_factor_matrix: bfloat16 [256, 64], replicated, may hold values from -0.375 to 0.375
- tensorial_final_matrix: bfloat16 [1024, 128], replicated, may hold values from -1 to 1
Outputs:
- alignment_target_tensor: float32 [256, 512, 256], P(None, 'dap')
- couple_target_tensor: float32 [512, 512, 128], P('dap', 'rep')
The draws below stay inside these ranges and needn't reach their ends.
All inputs are finite; a program needn't handle non-finite values.
Results may differ from the reference program's by a relative error of at most 0.02.
Values may be sent and summed in bfloat16 or wider, within the bound.
A program may use at most 64 MiB of HBM per device.

```python
import math
import jax
import jax.numpy as jnp
from jax import lax

ALIGNMENT_FEAT = 256
CZ = 128
HEADS = 8
HEAD_DIM = 32
FACTOR_WIDTH = 32
ALIGNED_CHAINS = 256
AMINO_TOTAL = 512
ROW_GROUPS = 4


def projection(key):
    reference_result = jnp.clip(jax.random.normal(key, (ALIGNMENT_FEAT, 4 * ALIGNMENT_FEAT), jnp.float32), -4.0, 4.0)
    return reference_result * ALIGNMENT_FEAT ** (-0.5)


def draw_alignment_source_tensor(key, part):
    key = jax.random.fold_in(key, 1)
    reference_result = jax.random.normal(key, (ALIGNED_CHAINS, AMINO_TOTAL, ALIGNMENT_FEAT), jnp.float32)
    return jnp.clip(reference_result, -6.0, 6.0)


def draw_horizontal_projection_matrix(key, part):
    key = jax.random.fold_in(key, 2)
    weight = projection(key)
    return weight.astype(jnp.bfloat16)


def draw_vertical_projection_matrix(key, part):
    key = jax.random.fold_in(key, 3)
    weight = projection(key)
    return weight.astype(jnp.bfloat16)


def block_scale(rng, shape, cuts, smallest, high):
    gain, own = 1.0, jax.random.fold_in(rng, 6)
    for position, parts in cuts:
        draws = jnp.exp(jax.random.uniform(jax.random.fold_in(own, position), (parts,), jnp.float32, smallest / len(cuts), high / len(cuts)))
        gain = gain * jnp.repeat(draws, shape[position] // parts).reshape([-1 if axis == position else 1 for axis in range(len(shape))])
    return gain


def normal_values(key, extent, width, reach, cuts=(), kind=jnp.bfloat16):
    result = width * jax.random.normal(key, extent, jnp.float32)
    if cuts:
        result = result * block_scale(key, extent, cuts, -0.22, 0.18)
    return jnp.clip(result, -reach, reach).astype(kind)


def setup_inputs(seed: int = 0) -> dict:
    key_of = jax.random.split(jax.random.key(seed), 14)
    alignment_source_tensor = draw_alignment_source_tensor(jax.random.fold_in(key_of[13], 71), 0)
    couple_source_tensor = normal_values(key_of[1], (AMINO_TOTAL, AMINO_TOTAL, CZ), 1.0, 6.0, ((0, 128), (1, 4)), jnp.float32)
    horizontal_scale_factor = jnp.clip(jnp.exp(jax.random.uniform(key_of[2], (ALIGNMENT_FEAT,), jnp.float32, math.log(0.3), math.log(3.0))), 0.3, 3.0)
    horizontal_projection_matrix = draw_horizontal_projection_matrix(jax.random.fold_in(key_of[13], 71), 0)
    couple_scale_factor = jnp.clip(jnp.exp(jax.random.uniform(key_of[4], (CZ,), jnp.float32, math.log(0.3), math.log(3.0))), 0.3, 3.0)
    couple_offset_matrix = normal_values(key_of[5], (CZ, HEADS), CZ ** -0.5, 0.5)
    horizontal_final_matrix = normal_values(key_of[6], (ALIGNMENT_FEAT, ALIGNMENT_FEAT), 16 ** -0.5, 1.5)
    vertical_scale_factor = jnp.clip(jnp.exp(jax.random.uniform(key_of[7], (ALIGNMENT_FEAT,), jnp.float32, math.log(0.3), math.log(3.0))), 0.3, 3.0)
    vertical_projection_matrix = draw_vertical_projection_matrix(jax.random.fold_in(key_of[13], 71), 0)
    vertical_final_matrix = normal_values(key_of[9], (ALIGNMENT_FEAT, ALIGNMENT_FEAT), 16 ** -0.5, 1.5)
    tensorial_scale_factor = jnp.clip(jnp.exp(jax.random.uniform(key_of[10], (ALIGNMENT_FEAT,), jnp.float32, math.log(0.3), math.log(3.0))), 0.3, 3.0)
    tensorial_factor_matrix = normal_values(key_of[11], (ALIGNMENT_FEAT, 2 * FACTOR_WIDTH), ALIGNMENT_FEAT ** -0.5, 0.375)
    tensorial_final_matrix = normal_values(key_of[12], (FACTOR_WIDTH * FACTOR_WIDTH, CZ), FACTOR_WIDTH ** -0.5, 1.0)
    return dict(alignment_source_tensor=alignment_source_tensor, couple_source_tensor=couple_source_tensor, horizontal_scale_factor=horizontal_scale_factor, horizontal_projection_matrix=horizontal_projection_matrix, couple_scale_factor=couple_scale_factor, couple_offset_matrix=couple_offset_matrix, horizontal_final_matrix=horizontal_final_matrix, vertical_scale_factor=vertical_scale_factor, vertical_projection_matrix=vertical_projection_matrix, vertical_final_matrix=vertical_final_matrix, tensorial_scale_factor=tensorial_scale_factor, tensorial_factor_matrix=tensorial_factor_matrix, tensorial_final_matrix=tensorial_final_matrix)


def standardize_features(inputs, norm_gain):
    average = lax.optimization_barrier(jnp.mean(inputs, axis=-1, keepdims=True))
    centred = inputs - average
    variance = lax.optimization_barrier(jnp.mean(centred * centred, axis=-1, keepdims=True))
    return centred * lax.rsqrt(variance + 1e-05) * norm_gain.astype(jnp.float32)

def attend(queries_in, keys_in, values_in, gates_in, bias_heads):
    q_len = queries_in.shape[0]
    k_len = keys_in.shape[0]
    queries = queries_in.astype(jnp.float32).reshape(q_len, HEADS, HEAD_DIM)
    key_heads = keys_in.astype(jnp.float32).reshape(k_len, HEADS, HEAD_DIM)
    value_heads = values_in.astype(jnp.float32).reshape(k_len, HEADS, HEAD_DIM)
    logits = jnp.einsum('qhd,khd->hqk', queries, key_heads) * HEAD_DIM ** (-0.5)
    if bias_heads is not None:
        logits = logits + bias_heads.astype(jnp.float32)
    maximum = lax.optimization_barrier(jnp.max(logits, axis=-1, keepdims=True))
    exponent = jnp.exp(logits - maximum)
    weights = (exponent / lax.optimization_barrier(jnp.sum(exponent, axis=-1, keepdims=True))).astype(jnp.bfloat16)
    attended = jnp.einsum('hqk,khd->qhd', weights.astype(jnp.float32), value_heads).reshape(q_len, HEADS * HEAD_DIM)
    return (attended * jax.nn.sigmoid(gates_in.astype(jnp.float32))).astype(jnp.bfloat16)

def split_attend(projected, bias_heads):
    feature_width = HEADS * HEAD_DIM
    return attend(projected[:, :feature_width], projected[:, feature_width:2 * feature_width], projected[:, 2 * feature_width:3 * feature_width], projected[:, 3 * feature_width:], bias_heads)

def reference(alignment_source_tensor, couple_source_tensor, horizontal_scale_factor, horizontal_projection_matrix, couple_scale_factor, couple_offset_matrix, horizontal_final_matrix, vertical_scale_factor, vertical_projection_matrix, vertical_final_matrix, tensorial_scale_factor, tensorial_factor_matrix, tensorial_final_matrix):
    ln_pair = standardize_features(couple_source_tensor, couple_scale_factor).astype(jnp.bfloat16)
    pair_bias = jnp.einsum('ijc,ch->hij', ln_pair.astype(jnp.float32), couple_offset_matrix.astype(jnp.float32)).astype(jnp.bfloat16)
    horizontal_standardized = standardize_features(alignment_source_tensor, horizontal_scale_factor).astype(jnp.bfloat16)
    horizontal_result = jnp.dot(horizontal_standardized.reshape(ALIGNED_CHAINS * AMINO_TOTAL, ALIGNMENT_FEAT), horizontal_projection_matrix, preferred_element_type=jnp.float32).astype(jnp.bfloat16).reshape(ALIGNED_CHAINS, AMINO_TOTAL, 4 * ALIGNMENT_FEAT)

    def row_one(projected):
        return split_attend(projected, pair_bias)
    horizontal_sigmoid_masked = lax.map(row_one, horizontal_result)
    alignment_intermediate = alignment_source_tensor + jnp.dot(horizontal_sigmoid_masked.reshape(ALIGNED_CHAINS * AMINO_TOTAL, ALIGNMENT_FEAT), horizontal_final_matrix, preferred_element_type=jnp.float32).reshape(ALIGNED_CHAINS, AMINO_TOTAL, ALIGNMENT_FEAT)
    vertical_standardized = standardize_features(alignment_intermediate, vertical_scale_factor).astype(jnp.bfloat16)
    vertical_result = jnp.dot(vertical_standardized.reshape(ALIGNED_CHAINS * AMINO_TOTAL, ALIGNMENT_FEAT), vertical_projection_matrix, preferred_element_type=jnp.float32).astype(jnp.bfloat16).reshape(ALIGNED_CHAINS, AMINO_TOTAL, 4 * ALIGNMENT_FEAT)

    def col_one(projected):
        return split_attend(projected, None)
    vertical_sigmoid_masked = jnp.swapaxes(lax.map(col_one, jnp.swapaxes(vertical_result, 0, 1)), 0, 1)
    alignment_target_tensor = alignment_intermediate + jnp.dot(vertical_sigmoid_masked.reshape(ALIGNED_CHAINS * AMINO_TOTAL, ALIGNMENT_FEAT), vertical_final_matrix, preferred_element_type=jnp.float32).reshape(ALIGNED_CHAINS, AMINO_TOTAL, ALIGNMENT_FEAT)
    tensorial_standardized = standardize_features(alignment_target_tensor, tensorial_scale_factor).astype(jnp.bfloat16)
    tensorial_result = jnp.dot(tensorial_standardized.reshape(ALIGNED_CHAINS * AMINO_TOTAL, ALIGNMENT_FEAT), tensorial_factor_matrix, preferred_element_type=jnp.float32).astype(jnp.bfloat16).reshape(ALIGNED_CHAINS, AMINO_TOTAL, 2 * FACTOR_WIDTH)
    alignments_each_slice = ALIGNED_CHAINS // ROW_GROUPS
    left_side = tensorial_result[:, :, :FACTOR_WIDTH].reshape(ROW_GROUPS, alignments_each_slice, AMINO_TOTAL, FACTOR_WIDTH)
    right_side = tensorial_result[:, :, FACTOR_WIDTH:].reshape(ROW_GROUPS, alignments_each_slice, AMINO_TOTAL, FACTOR_WIDTH)

    def one_residue(residue):
        update = jnp.zeros((AMINO_TOTAL, CZ), jnp.float32)
        for group_index in range(ROW_GROUPS):
            column = lax.dynamic_index_in_dim(left_side[group_index], residue, 1, keepdims=False)
            outer_prod = jnp.einsum('sc,sje->jce', column.astype(jnp.float32), right_side[group_index].astype(jnp.float32)) * (1.0 / ALIGNED_CHAINS)
            flattened = outer_prod.astype(jnp.bfloat16).reshape(AMINO_TOTAL, FACTOR_WIDTH * FACTOR_WIDTH)
            update = update + jnp.dot(flattened, tensorial_final_matrix, preferred_element_type=jnp.float32)
        return update
    pair_update = lax.map(one_residue, jnp.arange(AMINO_TOTAL, dtype=jnp.int32))
    couple_target_tensor = couple_source_tensor + pair_update
    return (alignment_target_tensor, couple_target_tensor)
```

```python
import math

import jax
import jax.numpy as jnp
from jax import lax
from jax.experimental import pallas as pl
from jax.experimental.pallas import tpu as pltpu
from jax.sharding import PartitionSpec as P

HEADS = 8
HEAD_DIM = 32
FEAT = HEADS * HEAD_DIM
CZ = 128
ROWS = 256
RES = 512
FACTOR = 32
LOG2E = math.log2(math.e)
LOGIT_SCALE = HEAD_DIM ** (-0.5) * LOG2E
MESH = pl.DeviceIdType.MESH
F32 = jnp.float32
BF16 = jnp.bfloat16

BIAS1, BIAS_Y, BIAS_X, BIAS_C, MSA1, MSA2, LEFT, FINAL, RIGHT1, RIGHT_Y, RIGHT_X, RIGHT_C = range(12)
PHASES = 12


def layer_norm(values, gain):
    average = jnp.mean(values, axis=-1, keepdims=True)
    centred = values - average
    variance = jnp.mean(centred * centred, axis=-1, keepdims=True)
    return (centred * lax.rsqrt(variance + 1e-05) * gain).astype(BF16)


def dot(a, b):
    return lax.dot_general(a, b, (((1,), (0,)), ((), ())), preferred_element_type=F32)


def dot_nt(a, b):
    return lax.dot_general(a, b, (((1,), (1,)), ((), ())), preferred_element_type=F32)


def head_mask():
    head = lax.broadcasted_iota(jnp.int32, (HEADS, FEAT), 0)
    channel = lax.broadcasted_iota(jnp.int32, (HEADS, FEAT), 1) // HEAD_DIM
    return (head == channel).astype(F32)


def expand_heads(queries):
    n = queries.shape[0]
    spread = jnp.broadcast_to(queries[:, None, :], (n, HEADS, FEAT))
    return (spread * head_mask()[None]).reshape(n * HEADS, FEAT).astype(BF16)


def merge_heads(attended, inverse):
    n = attended.shape[0] // HEADS
    scaled = (attended * inverse).reshape(n, HEADS, FEAT) * head_mask()[None]
    return jnp.sum(scaled, axis=1)


def kernel(
    msa, pair, g_row, w_row, g_pair, w_bias, wo_row, g_col, w_col, wo_col, g_opm, w_fac, w_fin,
    out_msa, out_pair,
    bias_src, bias_in, bias, queries, gates, keys, values, logits, weights, denom, staged, msa_src, msa_in,
    unpacked, col_src, col_in, col_logits, col_weights, col_denom, natural, final, left_src, left, right_src, right,
    right_f, final_f, final_w, outer, update, msa_halves, spread,
    send, recv,
):
    dap = lax.axis_index("dap")
    rep = lax.axis_index("rep")
    x = dap // 32
    y = (dap // 4) % 8
    xy = dap // 4
    zc = dap % 4
    zh = zc // 2
    core = zc % 2
    member = core * 2 + zh

    def device(xy_, zh_, core_):
        return xy_ * 4 + zh_ * 2 + core_

    barrier = pltpu.get_barrier_semaphore()

    def greet(dap_, rep_):
        pl.semaphore_signal(barrier, inc=1, device_id=(dap_, rep_), device_id_type=MESH)

    def greet_xy(step, _):
        greet(device((xy + step) % 32, zh, core), rep)
        return 0

    lax.fori_loop(1, 32, greet_xy, 0)
    for step in range(1, 8):
        other = (zh * 4 + rep + step) % 8
        greet(device(xy, other // 4, core), other % 4)
    greet(device(xy, zh, 1 - core), rep)
    greet(device(xy, 1 - zh, 1 - core), rep)
    mirror = rep * 8 + y
    greet(device(mirror, 1 - zh, core), x)

    @pl.when(x != rep)
    def _():
        greet(device(mirror, zh, core), x)

    def push(src, dst, phase, dap_, rep_):
        pltpu.make_async_remote_copy(
            src_ref=src, dst_ref=dst, send_sem=send.at[phase], recv_sem=recv.at[phase],
            device_id=(dap_, rep_), device_id_type=MESH,
        ).start()

    def arrived(shaped, phase):
        pltpu.make_async_copy(shaped, shaped, recv.at[phase]).wait()

    def drained(shaped, phase):
        pltpu.make_async_copy(shaped, shaped, send.at[phase]).wait()

    def push_y(buffer, phase):
        for step in range(1, 8):
            block = buffer.at[x, y, core]
            push(block, block, phase, device(x * 8 + (y + step) % 8, zh, core), rep)

    def push_x(buffer, phase):
        for step in range(1, 4):
            block = buffer.at[x, :, core]
            push(block, block, phase, device(((x + step) % 4) * 8 + y, zh, core), rep)

    def push_c(buffer, phase):
        block = buffer.at[:, :, core]
        push(block, block, phase, device(xy, zh, 1 - core), rep)

    ln_pair = layer_norm(pair[...].reshape(4 * 128, CZ), g_pair[...])
    head_bias = dot_nt(w_bias[...], ln_pair) * LOG2E
    for a in range(4):
        bias_src[a] = head_bias[:, a * 128 : (a + 1) * 128]

    pl.semaphore_wait(barrier, 41 + jnp.where(x != rep, 1, 0))

    for step in range(1, 8):
        other = (zh * 4 + rep + step) % 8
        push(bias_src.at[other % 4], bias_in.at[zh * 4 + rep], BIAS1, device(xy, other // 4, core), other % 4)
    bias_in[zh * 4 + rep] = bias_src[rep]

    for s in range(2):
        tokens = layer_norm(msa[s], g_row[...])
        projected = dot(tokens, w_row[:, FEAT : 3 * FEAT]).astype(BF16)
        keys[s] = projected[:, :FEAT]
        values[s] = projected[:, FEAT:]
        for half in range(2):
            msa_halves[s, half] = msa[s, :, half * 128 : (half + 1) * 128]
            for h_ in range(2):
                for c_ in range(2):
                    queries[s, half, pl.ds(c_ * 2 + h_, 32, stride=4), :] = msa_halves[
                        s, half, pl.ds(8 * h_ + 4 * c_ + rep, 32, stride=16), :
                    ]

    arrived(bias_in.at[pl.ds(0, 7)], BIAS1)
    block = jnp.concatenate(
        [jnp.concatenate([bias_in[h_ * 4 + r_] for r_ in range(4)], axis=1) for h_ in range(2)], axis=0
    )
    bias[x, y, core] = block.astype(BF16)
    push_y(bias, BIAS_Y)

    def row_logits(s):
        tokens = layer_norm(jnp.concatenate([queries[s, 0], queries[s, 1]], axis=1), g_row[...])
        wide = dot(tokens, w_row[:, :FEAT]) * LOGIT_SCALE
        gates[s] = jax.nn.sigmoid(dot(tokens, w_row[:, 3 * FEAT :]))
        logits[s] = dot_nt(expand_heads(wide), keys[s]).reshape(32, 2, 16, RES)

    row_logits(0)
    arrived(bias.at[0, pl.ds(0, 7), 0], BIAS_Y)
    push_x(bias, BIAS_X)
    row_logits(1)
    final_f[...] = w_fin[...].astype(F32)
    for e in range(FACTOR):
        final_w[pl.ds(e * FACTOR, FACTOR), :] = final_f[pl.ds(e, FACTOR, stride=FACTOR), :].astype(BF16)
    arrived(bias.at[pl.ds(0, 3), :, 0], BIAS_X)
    push_c(bias, BIAS_C)

    def row_softmax(group, which):
        rows = pl.ds(group * 4, 4)
        offset = bias[group // 2, pl.ds((group % 2) * 4, 4), which].astype(F32).reshape(64, RES)
        for s in range(2):
            raw = logits[s, rows, which].reshape(64, RES) + offset
            top = jnp.max(raw, axis=-1, keepdims=True)
            powers = jnp.exp2(raw - top)
            total = jnp.sum(powers, axis=-1, keepdims=True)
            weights[s, rows, which] = powers.astype(BF16).reshape(4, 16, RES)
            denom[s, rows, which] = jnp.broadcast_to(1.0 / total, (64, 128)).reshape(4, 16, 128)
        return which

    lax.fori_loop(0, 8, row_softmax, core)
    arrived(bias.at[:, :, 0], BIAS_C)
    lax.fori_loop(0, 8, row_softmax, 1 - core)
    for s in range(2):
        attended = dot(weights[s].reshape(1024, RES), values[s])
        merged = merge_heads(attended, denom[s].reshape(1024, 128)[:, :1])
        gated = (merged * gates[s]).astype(BF16)
        change = dot(gated, wo_row[...])
        for half in range(2):
            staged[pl.ds(s * 2 + half, 128, stride=4), :] = queries[s, half] + change[:, half * 128 : (half + 1) * 128]
    msa_src[...] = staged[...].astype(BF16).reshape(32, 16, 128)

    def push_msa(step, _):
        other = (xy + step) % 32
        push(msa_src.at[other], msa_in.at[xy], MSA1, device(other, zh, core), rep)
        return 0

    lax.fori_loop(1, 32, push_msa, 0)
    msa_in[xy] = msa_src[xy]
    arrived(msa_in.at[pl.ds(0, 31)], MSA1)
    unpacked[...] = msa_in[...].astype(F32).reshape(512, 128)
    for target in range(4):
        parts = [
            jnp.concatenate(
                [unpacked[pl.ds(target * 4 + s * 2 + half, 32, stride=16), :] for half in range(2)], axis=1
            )
            for s in range(2)
        ]
        col_src[target] = jnp.concatenate(parts, axis=0).astype(BF16)
    for step in range(1, 4):
        other = (member + step) % 4
        push(col_src.at[other], col_in.at[member], MSA2, device(xy, other % 2, other // 2), rep)
    col_in[member] = col_src[member]
    arrived(col_in.at[pl.ds(0, 3)], MSA2)

    middle = col_in[...].astype(F32).reshape(ROWS, FEAT)
    tokens = layer_norm(middle, g_col[...])
    projected = dot(tokens, w_col[...])
    wide = expand_heads(projected[:, :FEAT] * LOGIT_SCALE)
    col_keys = projected[:, FEAT : 2 * FEAT].astype(BF16)
    col_values = projected[:, 2 * FEAT : 3 * FEAT].astype(BF16)
    col_gates = jax.nn.sigmoid(projected[:, 3 * FEAT :])
    col_logits[...] = dot_nt(wide, col_keys)

    def col_softmax(group, _):
        rows = pl.ds(pl.multiple_of(group * 128, 128), 128)
        raw = col_logits[rows, :]
        top = jnp.max(raw, axis=-1, keepdims=True)
        powers = jnp.exp2(raw - top)
        total = jnp.sum(powers, axis=-1, keepdims=True)
        col_weights[rows, :] = powers.astype(BF16)
        col_denom[rows, :] = jnp.broadcast_to(1.0 / total, (128, 128))
        return 0

    lax.fori_loop(0, 16, col_softmax, 0)
    attended = dot(col_weights[...], col_values)
    merged = merge_heads(attended, col_denom[...][:, :1])
    gated = (merged * col_gates).astype(BF16)
    target_rows = middle + dot(gated, wo_col[...])

    ln_opm = layer_norm(target_rows, g_opm[...])
    factors = dot_nt(w_fac[...], ln_opm)
    right_src[...] = factors[FACTOR:].astype(BF16)
    left_src[...] = (factors[:FACTOR] * (1.0 / ROWS)).astype(BF16)
    push(right_src, right.at[rep, y, core, zh], RIGHT1, device(mirror, 1 - zh, core), x)

    @pl.when(x != rep)
    def _():
        push(right_src, right.at[rep, y, core, zh], RIGHT1, device(mirror, zh, core), x)

    @pl.when(x == rep)
    def _():
        right[rep, y, core, zh] = right_src[...]

    for step in range(1, 4):
        push(left_src, left.at[rep], LEFT, dap, (rep + step) % 4)
    left[rep] = left_src[...]
    for m_ in range(4):
        for s in range(2):
            start = (m_ * 2 + s) * 32
            for half in range(2):
                natural[half, pl.ds((m_ % 2) * 4 + (m_ // 2) * 2 + s, 32, stride=8), :] = target_rows[
                    start : start + 32, half * 128 : (half + 1) * 128
                ]
    final[rep] = jnp.concatenate([natural[0], natural[1]], axis=1).astype(BF16)
    for step in range(1, 4):
        push(final.at[rep], final.at[rep], FINAL, dap, (rep + step) % 4)

    @pl.when(x != rep)
    def _():
        arrived(right.at[0, 0, 0], RIGHT1)

    @pl.when(x == rep)
    def _():
        arrived(right_src, RIGHT1)

    push_y(right, RIGHT_Y)
    arrived(right.at[0, pl.ds(0, 7), 0], RIGHT_Y)
    push_x(right, RIGHT_X)
    arrived(right.at[pl.ds(0, 3), :, 0], RIGHT_X)
    push_c(right, RIGHT_C)
    arrived(left.at[pl.ds(0, 3)], LEFT)
    left_all = left[...].reshape(4 * FACTOR, ROWS)
    arrived(right.at[:, :, 0], RIGHT_C)

    for half in range(2):
        right_f[half] = right[..., half * 128 : (half + 1) * 128].astype(F32).reshape(128 * FACTOR, 128)
    for e in range(FACTOR):
        operand = jnp.concatenate(
            [right_f[half, pl.ds(e, 128, stride=FACTOR), :] for half in range(2)], axis=1
        ).astype(BF16)
        product = dot_nt(left_all, operand).astype(BF16)
        for i in range(4):
            outer[pl.ds(e * FACTOR, FACTOR), i * 128 : (i + 1) * 128] = product[i * FACTOR : (i + 1) * FACTOR]
    flat = lax.dot_general(final_w[...], outer[...], (((0,), (0,)), ((), ())), preferred_element_type=F32)
    for i in range(4):
        update[i] = flat[:, i * 128 : (i + 1) * 128].T
        for x_ in range(4):
            for m_ in range(4):
                here = pl.ds(8 * (m_ % 2) + 4 * (m_ // 2) + x_, 8, stride=16)
                out_pair[i, here, :] = pair[i, here, :] + update[i, pl.ds(x_ * 32 + m_, 8, stride=4), :]

    arrived(final.at[pl.ds(0, 3)], FINAL)
    for half in range(2):
        for r_ in range(4):
            spread[half, pl.ds(r_, ROWS, stride=4), :] = final[r_, :, half * 128 : (half + 1) * 128].astype(F32)
        out_msa[:, half * 128 : (half + 1) * 128] = spread[half]

    drained(bias_in.at[pl.ds(0, 7)], BIAS1)
    drained(bias.at[0, pl.ds(0, 7), 0], BIAS_Y)
    drained(bias.at[pl.ds(0, 3), :, 0], BIAS_X)
    drained(bias.at[:, :, 0], BIAS_C)
    drained(msa_in.at[pl.ds(0, 31)], MSA1)
    drained(col_in.at[pl.ds(0, 3)], MSA2)
    drained(left.at[pl.ds(0, 3)], LEFT)
    drained(final.at[pl.ds(0, 3)], FINAL)

    @pl.when(x != rep)
    def _():
        drained(right.at[0, 0, 0], RIGHT1)

    @pl.when(x == rep)
    def _():
        drained(right_src, RIGHT1)

    drained(right.at[0, pl.ds(0, 7), 0], RIGHT_Y)
    drained(right.at[pl.ds(0, 3), :, 0], RIGHT_X)
    drained(right.at[:, :, 0], RIGHT_C)


def shards(
    alignment_source_tensor,
    couple_source_tensor,
    horizontal_scale_factor,
    horizontal_projection_matrix,
    couple_scale_factor,
    couple_offset_matrix,
    horizontal_final_matrix,
    vertical_scale_factor,
    vertical_projection_matrix,
    vertical_final_matrix,
    tensorial_scale_factor,
    tensorial_factor_matrix,
    tensorial_final_matrix,
):
    vmem = pl.BlockSpec(memory_space=pltpu.VMEM)
    scratch = [
        pltpu.VMEM((4, 8, 128), F32),
        pltpu.VMEM((8, 8, 128), F32),
        pltpu.VMEM((4, 8, 2, 16, RES), BF16),
        pltpu.VMEM((2, 2, 128, 128), F32),
        pltpu.VMEM((2, 128, FEAT), F32),
        pltpu.VMEM((2, RES, FEAT), BF16),
        pltpu.VMEM((2, RES, FEAT), BF16),
        pltpu.VMEM((2, 32, 2, 16, RES), F32),
        pltpu.VMEM((2, 32, 2, 16, RES), BF16),
        pltpu.VMEM((2, 32, 2, 16, 128), F32),
        pltpu.VMEM((512, 128), F32),
        pltpu.VMEM((32, 16, 128), BF16),
        pltpu.VMEM((32, 16, 128), BF16),
        pltpu.VMEM((512, 128), F32),
        pltpu.VMEM((4, 64, FEAT), BF16),
        pltpu.VMEM((4, 64, FEAT), BF16),
        pltpu.VMEM((ROWS * HEADS, ROWS), F32),
        pltpu.VMEM((ROWS * HEADS, ROWS), BF16),
        pltpu.VMEM((ROWS * HEADS, 128), F32),
        pltpu.VMEM((2, ROWS, 128), F32),
        pltpu.VMEM((4, ROWS, FEAT), BF16),
        pltpu.VMEM((FACTOR, ROWS), BF16),
        pltpu.VMEM((4, FACTOR, ROWS), BF16),
        pltpu.VMEM((FACTOR, ROWS), BF16),
        pltpu.VMEM((4, 8, 2, 2, FACTOR, ROWS), BF16),
        pltpu.VMEM((2, 128 * FACTOR, 128), F32),
        pltpu.VMEM((FACTOR * FACTOR, CZ), F32),
        pltpu.VMEM((FACTOR * FACTOR, CZ), BF16),
        pltpu.VMEM((FACTOR * FACTOR, 512), BF16),
        pltpu.VMEM((4, 128, CZ), F32),
        pltpu.VMEM((2, 2, RES, 128), F32),
        pltpu.VMEM((2, ROWS * 4, 128), F32),
        pltpu.SemaphoreType.DMA((PHASES,)),
        pltpu.SemaphoreType.DMA((PHASES,)),
    ]
    out_msa, out_pair = pl.pallas_call(
        kernel,
        out_shape=(
            jax.ShapeDtypeStruct((ROWS * 4, FEAT), F32),
            jax.ShapeDtypeStruct((4, 128, CZ), F32),
        ),
        in_specs=[vmem] * 13,
        out_specs=(vmem, vmem),
        scratch_shapes=scratch,
        compiler_params=pltpu.CompilerParams(
            collective_id=0, has_side_effects=True, vmem_limit_bytes=48 * 1024 * 1024
        ),
    )(
        alignment_source_tensor,
        couple_source_tensor,
        horizontal_scale_factor.reshape(1, FEAT),
        horizontal_projection_matrix,
        couple_scale_factor.reshape(1, CZ),
        couple_offset_matrix.T,
        horizontal_final_matrix,
        vertical_scale_factor.reshape(1, FEAT),
        vertical_projection_matrix,
        vertical_final_matrix,
        tensorial_scale_factor.reshape(1, FEAT),
        tensorial_factor_matrix.T,
        tensorial_final_matrix,
    )
    return out_msa.reshape(ROWS, 4, FEAT), out_pair


def solution(mesh):
    return jax.shard_map(
        shards,
        mesh=mesh,
        in_specs=(P("dap", None, None), P("dap", "rep", None)) + (P(),) * 11,
        out_specs=(P(None, "dap", None), P("dap", "rep", None)),
        check_vma=False,
    )
```

```python
import math

import jax
import jax.numpy as jnp
from jax import lax
from jax.experimental import pallas as pl
from jax.experimental.pallas import tpu as pltpu
from jax.sharding import PartitionSpec as P

HEADS = 8
HEAD_DIM = 32
FEAT = HEADS * HEAD_DIM
CZ = 128
ROWS = 256
RES = 512
FACTOR = 32
LOG2E = math.log2(math.e)
LOGIT_SCALE = HEAD_DIM ** (-0.5) * LOG2E
MESH = pl.DeviceIdType.MESH
F32 = jnp.float32
BF16 = jnp.bfloat16

BIAS1, BIAS_Y, BIAS_X, BIAS_C, MSA1, MSA2, LEFT, LEFT_X, LEFT_C, FINAL, RIGHT1, RIGHT_Y, RESULT = range(13)
PHASES = 13


def layer_norm(values, gain):
    average = jnp.mean(values, axis=-1, keepdims=True)
    centred = values - average
    variance = jnp.mean(centred * centred, axis=-1, keepdims=True)
    return (centred * lax.rsqrt(variance + 1e-05) * gain).astype(BF16)


def dot(a, b):
    return lax.dot_general(a, b, (((1,), (0,)), ((), ())), preferred_element_type=F32)


def dot_nt(a, b):
    return lax.dot_general(a, b, (((1,), (1,)), ((), ())), preferred_element_type=F32)


def head_mask():
    head = lax.broadcasted_iota(jnp.int32, (HEADS, FEAT), 0)
    channel = lax.broadcasted_iota(jnp.int32, (HEADS, FEAT), 1) // HEAD_DIM
    return (head == channel).astype(F32)


def expand_heads(queries):
    n = queries.shape[0]
    spread = jnp.broadcast_to(queries[:, None, :], (n, HEADS, FEAT))
    return (spread * head_mask()[None]).reshape(n * HEADS, FEAT).astype(BF16)


def merge_heads(attended, inverse):
    n = attended.shape[0] // HEADS
    scaled = (attended * inverse).reshape(n, HEADS, FEAT) * head_mask()[None]
    return jnp.sum(scaled, axis=1)


def kernel(*refs):
    given, (out_msa, out_pair), held, rest = refs[:13], refs[13:15], refs[15:28], refs[28:]
    msa, pair, g_row, w_row, g_pair, w_bias, wo_row, g_col, w_col, wo_col, g_opm, w_fac, w_fin = held
    (
        bias_src, bias_in, bias, queries, gates, keys, values, logits, weights, denom, staged, msa_src, msa_in,
        unpacked, col_src, col_in, col_logits, col_weights, col_denom, natural, final, left_src, left, right_src, right,
        left_f, left_t, outer, update, result_src, result_in, msa_halves, spread,
        send, recv, load,
    ) = rest
    loads = [pltpu.make_async_copy(given[k], held[k], load.at[k]) for k in range(13)]
    for k in (1, 5, 4, 0, 2, 3, 6, 12, 7, 8, 9, 10, 11):
        loads[k].start()

    def loaded(*which):
        for k in which:
            loads[k].wait()

    dap = lax.axis_index("dap")
    rep = lax.axis_index("rep")
    x = dap // 32
    y = (dap // 4) % 8
    xy = dap // 4
    zc = dap % 4
    zh = zc // 2
    core = zc % 2
    member = core * 2 + zh

    def device(xy_, zh_, core_):
        return xy_ * 4 + zh_ * 2 + core_

    barrier = pltpu.get_barrier_semaphore()

    def greet(dap_, rep_):
        pl.semaphore_signal(barrier, inc=1, device_id=(dap_, rep_), device_id_type=MESH)

    def greet_xy(step, _):
        greet(device((xy + step) % 32, zh, core), rep)
        return 0

    lax.fori_loop(1, 32, greet_xy, 0)
    for step in range(1, 8):
        other = (zh * 4 + rep + step) % 8
        greet(device(xy, other // 4, core), other % 4)
    for step in range(4):
        greet(device(((x + step) % 4) * 8 + y, zh, 1 - core), rep)
    greet(device(xy, 1 - zh, 1 - core), rep)
    mirror = rep * 8 + y
    greet(device(mirror, 1 - zh, core), x)

    @pl.when(x != rep)
    def _():
        greet(device(mirror, zh, core), x)

    def push(src, dst, phase, dap_, rep_):
        pltpu.make_async_remote_copy(
            src_ref=src, dst_ref=dst, send_sem=send.at[phase], recv_sem=recv.at[phase],
            device_id=(dap_, rep_), device_id_type=MESH,
        ).start()

    def arrived(shaped, phase):
        pltpu.make_async_copy(shaped, shaped, recv.at[phase]).wait()

    def drained(shaped, phase):
        pltpu.make_async_copy(shaped, shaped, send.at[phase]).wait()

    leaving = []

    def finish():
        for shaped, phase in leaving:
            if shaped is not None:
                drained(shaped, phase)
                continue

            @pl.when(x != rep)
            def _():
                drained(right.at[0], RIGHT1)

            @pl.when(x == rep)
            def _():
                drained(right_src, RIGHT1)

    def push_y(buffer, phase):
        for step in range(1, 8):
            block = buffer.at[x, y, core]
            push(block, block, phase, device(x * 8 + (y + step) % 8, zh, core), rep)
        leaving.append((buffer.at[0, pl.ds(0, 7), 0], phase))

    def push_x(buffer, phase):
        for step in range(1, 4):
            block = buffer.at[x, :, core]
            push(block, block, phase, device(((x + step) % 4) * 8 + y, zh, core), rep)
        leaving.append((buffer.at[pl.ds(0, 3), :, 0], phase))

    def push_c(buffer, phase):
        block = buffer.at[:, :, core]
        push(block, block, phase, device(xy, zh, 1 - core), rep)
        leaving.append((buffer.at[:, :, 0], phase))

    loaded(1, 4, 5)
    ln_pair = layer_norm(pair[...].reshape(4 * 128, CZ), g_pair[...])
    head_bias = dot_nt(w_bias[...], ln_pair) * LOG2E
    for a in range(4):
        bias_src[a] = head_bias[:, a * 128 : (a + 1) * 128]

    pl.semaphore_wait(barrier, 44 + jnp.where(x != rep, 1, 0))

    for step in range(1, 8):
        other = (zh * 4 + rep + step) % 8
        push(bias_src.at[other % 4], bias_in.at[zh * 4 + rep], BIAS1, device(xy, other // 4, core), other % 4)
    leaving.append((bias_in.at[pl.ds(0, 7)], BIAS1))
    bias_in[zh * 4 + rep] = bias_src[rep]

    loaded(0, 2, 3)
    for s in range(2):
        tokens = layer_norm(msa[s], g_row[...])
        projected = dot(tokens, w_row[:, FEAT : 3 * FEAT]).astype(BF16)
        keys[s] = projected[:, :FEAT]
        values[s] = projected[:, FEAT:]
        for half in range(2):
            msa_halves[s, half] = msa[s, :, half * 128 : (half + 1) * 128]
            for h_ in range(2):
                for c_ in range(2):
                    queries[s, half, pl.ds(c_ * 2 + h_, 32, stride=4), :] = msa_halves[
                        s, half, pl.ds(8 * h_ + 4 * c_ + rep, 32, stride=16), :
                    ]

    arrived(bias_in.at[pl.ds(0, 7)], BIAS1)
    block = jnp.concatenate(
        [jnp.concatenate([bias_in[h_ * 4 + r_] for r_ in range(4)], axis=1) for h_ in range(2)], axis=0
    )
    bias[x, y, core] = block.astype(BF16)
    push_y(bias, BIAS_Y)

    def row_logits(s):
        tokens = layer_norm(jnp.concatenate([queries[s, 0], queries[s, 1]], axis=1), g_row[...])
        wide = dot(tokens, w_row[:, :FEAT]) * LOGIT_SCALE
        gates[s] = jax.nn.sigmoid(dot(tokens, w_row[:, 3 * FEAT :]))
        logits[s] = dot_nt(expand_heads(wide), keys[s]).reshape(32, 2, 16, RES)

    row_logits(0)
    arrived(bias.at[0, pl.ds(0, 7), 0], BIAS_Y)
    push_x(bias, BIAS_X)
    row_logits(1)
    arrived(bias.at[pl.ds(0, 3), :, 0], BIAS_X)
    push_c(bias, BIAS_C)

    def row_softmax(group, which):
        rows = pl.ds(group * 4, 4)
        offset = bias[group // 2, pl.ds((group % 2) * 4, 4), which].astype(F32).reshape(64, RES)
        for s in range(2):
            raw = logits[s, rows, which].reshape(64, RES) + offset
            top = jnp.max(raw, axis=-1, keepdims=True)
            powers = jnp.exp2(raw - top)
            total = jnp.sum(powers, axis=-1, keepdims=True)
            weights[s, rows, which] = powers.astype(BF16).reshape(4, 16, RES)
            denom[s, rows, which] = jnp.broadcast_to(1.0 / total, (64, 128)).reshape(4, 16, 128)
        return which

    lax.fori_loop(0, 8, row_softmax, core)
    arrived(bias.at[:, :, 0], BIAS_C)
    lax.fori_loop(0, 8, row_softmax, 1 - core)
    loaded(6)
    for s in range(2):
        attended = dot(weights[s].reshape(1024, RES), values[s])
        merged = merge_heads(attended, denom[s].reshape(1024, 128)[:, :1])
        gated = (merged * gates[s]).astype(BF16)
        change = dot(gated, wo_row[...])
        for half in range(2):
            staged[pl.ds(s * 2 + half, 128, stride=4), :] = queries[s, half] + change[:, half * 128 : (half + 1) * 128]
    msa_src[...] = staged[...].astype(BF16).reshape(32, 16, 128)

    def push_msa(step, _):
        other = (xy + step) % 32
        push(msa_src.at[other], msa_in.at[xy], MSA1, device(other, zh, core), rep)
        return 0

    lax.fori_loop(1, 32, push_msa, 0)
    leaving.append((msa_in.at[pl.ds(0, 31)], MSA1))
    msa_in[xy] = msa_src[xy]
    arrived(msa_in.at[pl.ds(0, 31)], MSA1)
    unpacked[...] = msa_in[...].astype(F32).reshape(512, 128)
    for target in range(4):
        parts = [
            jnp.concatenate(
                [unpacked[pl.ds(target * 4 + s * 2 + half, 32, stride=16), :] for half in range(2)], axis=1
            )
            for s in range(2)
        ]
        col_src[target] = jnp.concatenate(parts, axis=0).astype(BF16)
    for step in range(1, 4):
        other = (member + step) % 4
        push(col_src.at[other], col_in.at[member], MSA2, device(xy, other % 2, other // 2), rep)
    leaving.append((col_in.at[pl.ds(0, 3)], MSA2))
    col_in[member] = col_src[member]
    arrived(col_in.at[pl.ds(0, 3)], MSA2)

    loaded(7, 8, 9, 10, 11, 12)
    middle = col_in[...].astype(F32).reshape(ROWS, FEAT)
    tokens = layer_norm(middle, g_col[...])
    projected = dot(tokens, w_col[...])
    wide = expand_heads(projected[:, :FEAT] * LOGIT_SCALE)
    col_keys = projected[:, FEAT : 2 * FEAT].astype(BF16)
    col_values = projected[:, 2 * FEAT : 3 * FEAT].astype(BF16)
    col_gates = jax.nn.sigmoid(projected[:, 3 * FEAT :])
    col_logits[...] = dot_nt(wide, col_keys)

    def col_softmax(group, _):
        rows = pl.ds(pl.multiple_of(group * 128, 128), 128)
        raw = col_logits[rows, :]
        top = jnp.max(raw, axis=-1, keepdims=True)
        powers = jnp.exp2(raw - top)
        total = jnp.sum(powers, axis=-1, keepdims=True)
        col_weights[rows, :] = powers.astype(BF16)
        col_denom[rows, :] = jnp.broadcast_to(1.0 / total, (128, 128))
        return 0

    lax.fori_loop(0, 16, col_softmax, 0)
    attended = dot(col_weights[...], col_values)
    merged = merge_heads(attended, col_denom[...][:, :1])
    gated = (merged * col_gates).astype(BF16)
    target_rows = middle + dot(gated, wo_col[...])

    ln_opm = layer_norm(target_rows, g_opm[...])
    factors = dot_nt(w_fac[...], ln_opm)
    right_src[...] = factors[FACTOR:].astype(BF16)
    left_src[...] = (factors[:FACTOR] * (1.0 / ROWS)).astype(BF16)
    push(right_src, right.at[y, zh], RIGHT1, device(mirror, 1 - zh, core), x)

    @pl.when(x != rep)
    def _():
        push(right_src, right.at[y, zh], RIGHT1, device(mirror, zh, core), x)

    @pl.when(x == rep)
    def _():
        right[y, zh] = right_src[...]

    for step in range(1, 4):
        push(left_src, left.at[x, core, rep], LEFT, dap, (rep + step) % 4)
    leaving.append((None, RIGHT1))
    leaving.append((left.at[0, 0, pl.ds(0, 3)], LEFT))
    left[x, core, rep] = left_src[...]
    for m_ in range(4):
        for s in range(2):
            start = (m_ * 2 + s) * 32
            for half in range(2):
                natural[half, pl.ds((m_ % 2) * 4 + (m_ // 2) * 2 + s, 32, stride=8), :] = target_rows[
                    start : start + 32, half * 128 : (half + 1) * 128
                ]
    final[rep] = jnp.concatenate([natural[0], natural[1]], axis=1).astype(BF16)
    for step in range(1, 4):
        push(final.at[rep], final.at[rep], FINAL, dap, (rep + step) % 4)
    leaving.append((final.at[pl.ds(0, 3)], FINAL))

    @pl.when(x != rep)
    def _():
        arrived(right.at[0], RIGHT1)

    @pl.when(x == rep)
    def _():
        arrived(right_src, RIGHT1)

    for step in range(1, 8):
        push(right.at[y], right.at[y], RIGHT_Y, device(x * 8 + (y + step) % 8, zh, core), rep)
    leaving.append((right.at[pl.ds(0, 7)], RIGHT_Y))
    arrived(left.at[0, 0, pl.ds(0, 3)], LEFT)
    for step in range(1, 4):
        block = left.at[x, core]
        push(block, block, LEFT_X, device(((x + step) % 4) * 8 + y, zh, core), rep)
    leaving.append((left.at[pl.ds(0, 3), 0], LEFT_X))
    arrived(left.at[pl.ds(0, 3), 0], LEFT_X)
    block = left.at[:, core]
    push(block, block, LEFT_C, device(xy, zh, 1 - core), rep)
    leaving.append((left.at[:, 0], LEFT_C))
    arrived(left.at[:, 0], LEFT_C)

    for half in range(2):
        left_f[half] = left[..., half * 128 : (half + 1) * 128].astype(F32).reshape(32 * FACTOR, 128)
    for channel in range(FACTOR):
        left_t[pl.ds(channel * 32, 32), :] = jnp.concatenate(
            [left_f[half, pl.ds(channel, 32, stride=FACTOR), :] for half in range(2)], axis=1
        ).astype(BF16)
    arrived(right.at[pl.ds(0, 7)], RIGHT_Y)
    quarter = lax.broadcasted_iota(jnp.int32, (FACTOR, 128), 1) // 32
    right_all = right[...].reshape(16 * FACTOR, ROWS)
    for part in range(4):
        product = dot_nt(right_all, left_t[pl.ds(part * 256, 256), :])
        for tile in range(2):
            lanes = slice(tile * 128, (tile + 1) * 128)
            for four in range(4):
                blocks = [product[(four * 4 + jq) * FACTOR : (four * 4 + jq + 1) * FACTOR, lanes] for jq in range(4)]
                for cq in range(4):
                    moved = [
                        blocks[jq] if jq == cq else pltpu.roll(blocks[jq], (32 * (jq - cq)) % 128, 1) for jq in range(4)
                    ]
                    joined = jnp.where(
                        quarter < 2,
                        jnp.where(quarter == 0, moved[0], moved[1]),
                        jnp.where(quarter == 2, moved[2], moved[3]),
                    )
                    channel = part * 8 + tile * 4 + cq
                    outer[pl.ds(channel * FACTOR, FACTOR), four * 128 : (four + 1) * 128] = joined.astype(BF16)
    flat = lax.dot_general(w_fin[...], outer[...], (((0,), (0,)), ((), ())), preferred_element_type=F32)
    for four in range(4):
        update[pl.ds(four * 128, 128), :] = flat[:, four * 128 : (four + 1) * 128].T

    for target in range(8):
        for r_ in range(4):
            result_src[target, r_] = update[pl.ds(target * 4 + r_, 16, stride=32), :].astype(BF16)
    mine = x * 2 + core
    for step in range(1, 8):
        other = (mine + step) % 8
        push(result_src.at[other], result_in.at[mine], RESULT, device((other // 2) * 8 + y, zh, other % 2), rep)
    leaving.append((result_in.at[pl.ds(0, 7)], RESULT))
    result_in[mine] = result_src[mine]

    arrived(final.at[pl.ds(0, 3)], FINAL)
    for half in range(2):
        for r_ in range(4):
            spread[half, pl.ds(r_, ROWS, stride=4), :] = final[r_, :, half * 128 : (half + 1) * 128].astype(F32)
        out_msa[:, half * 128 : (half + 1) * 128] = spread[half]

    arrived(result_in.at[pl.ds(0, 7)], RESULT)
    for source in range(8):
        for a in range(4):
            here = pl.ds(4 * (source % 2) + source // 2, 16, stride=8)
            out_pair[a, here, :] = pair[a, here, :] + result_in[source, a].astype(F32)

    finish()


def shards(
    alignment_source_tensor,
    couple_source_tensor,
    horizontal_scale_factor,
    horizontal_projection_matrix,
    couple_scale_factor,
    couple_offset_matrix,
    horizontal_final_matrix,
    vertical_scale_factor,
    vertical_projection_matrix,
    vertical_final_matrix,
    tensorial_scale_factor,
    tensorial_factor_matrix,
    tensorial_final_matrix,
):
    operands = [
        alignment_source_tensor,
        couple_source_tensor,
        horizontal_scale_factor.reshape(1, FEAT),
        horizontal_projection_matrix,
        couple_scale_factor.reshape(1, CZ),
        couple_offset_matrix.T,
        horizontal_final_matrix,
        vertical_scale_factor.reshape(1, FEAT),
        vertical_projection_matrix,
        vertical_final_matrix,
        tensorial_scale_factor.reshape(1, FEAT),
        tensorial_factor_matrix.T,
        tensorial_final_matrix,
    ]
    vmem = pl.BlockSpec(memory_space=pltpu.VMEM)
    scratch = [pltpu.VMEM(a.shape, a.dtype) for a in operands] + [
        pltpu.VMEM((4, 8, 128), F32),
        pltpu.VMEM((8, 8, 128), F32),
        pltpu.VMEM((4, 8, 2, 16, RES), BF16),
        pltpu.VMEM((2, 2, 128, 128), F32),
        pltpu.VMEM((2, 128, FEAT), F32),
        pltpu.VMEM((2, RES, FEAT), BF16),
        pltpu.VMEM((2, RES, FEAT), BF16),
        pltpu.VMEM((2, 32, 2, 16, RES), F32),
        pltpu.VMEM((2, 32, 2, 16, RES), BF16),
        pltpu.VMEM((2, 32, 2, 16, 128), F32),
        pltpu.VMEM((512, 128), F32),
        pltpu.VMEM((32, 16, 128), BF16),
        pltpu.VMEM((32, 16, 128), BF16),
        pltpu.VMEM((512, 128), F32),
        pltpu.VMEM((4, 64, FEAT), BF16),
        pltpu.VMEM((4, 64, FEAT), BF16),
        pltpu.VMEM((ROWS * HEADS, ROWS), F32),
        pltpu.VMEM((ROWS * HEADS, ROWS), BF16),
        pltpu.VMEM((ROWS * HEADS, 128), F32),
        pltpu.VMEM((2, ROWS, 128), F32),
        pltpu.VMEM((4, ROWS, FEAT), BF16),
        pltpu.VMEM((FACTOR, ROWS), BF16),
        pltpu.VMEM((4, 2, 4, FACTOR, ROWS), BF16),
        pltpu.VMEM((FACTOR, ROWS), BF16),
        pltpu.VMEM((8, 2, FACTOR, ROWS), BF16),
        pltpu.VMEM((2, 32 * FACTOR, 128), F32),
        pltpu.VMEM((32 * FACTOR, ROWS), BF16),
        pltpu.VMEM((FACTOR * FACTOR, 512), BF16),
        pltpu.VMEM((512, CZ), F32),
        pltpu.VMEM((8, 4, 16, CZ), BF16),
        pltpu.VMEM((8, 4, 16, CZ), BF16),
        pltpu.VMEM((2, 2, RES, 128), F32),
        pltpu.VMEM((2, ROWS * 4, 128), F32),
        pltpu.SemaphoreType.DMA((PHASES,)),
        pltpu.SemaphoreType.DMA((PHASES,)),
        pltpu.SemaphoreType.DMA((len(operands),)),
    ]
    out_msa, out_pair = pl.pallas_call(
        kernel,
        out_shape=(
            jax.ShapeDtypeStruct((ROWS * 4, FEAT), F32),
            jax.ShapeDtypeStruct((4, 128, CZ), F32),
        ),
        in_specs=[pl.BlockSpec(memory_space=pltpu.HBM)] * len(operands),
        out_specs=(vmem, vmem),
        scratch_shapes=scratch,
        compiler_params=pltpu.CompilerParams(
            collective_id=0, has_side_effects=True, vmem_limit_bytes=60 * 1024 * 1024
        ),
    )(*operands)
    return out_msa.reshape(ROWS, 4, FEAT), out_pair


def solution(mesh):
    return jax.shard_map(
        shards,
        mesh=mesh,
        in_specs=(P("dap", None, None), P("dap", "rep", None)) + (P(),) * 11,
        out_specs=(P(None, "dap", None), P("dap", "rep", None)),
        check_vma=False,
    )
```

```python
import math

import jax
import jax.numpy as jnp
from jax import lax
from jax.experimental import pallas as pl
from jax.experimental.pallas import tpu as pltpu
from jax.sharding import PartitionSpec as P

HEADS = 8
HEAD_DIM = 32
FEAT = HEADS * HEAD_DIM
CZ = 128
ROWS = 256
RES = 512
FACTOR = 32
LOG2E = math.log2(math.e)
LOGIT_SCALE = HEAD_DIM ** (-0.5) * LOG2E
MESH = pl.DeviceIdType.MESH
F32 = jnp.float32
BF16 = jnp.bfloat16

BIAS1, BIAS_Y, BIAS_X, BIAS_C, MSA1, MSA2, LEFT, LEFT_X, LEFT_C, FINAL, RIGHT1, RIGHT_Y, RESULT = range(13)
PHASES = 13


def layer_norm(values, gain):
    average = jnp.mean(values, axis=-1, keepdims=True)
    centred = values - average
    variance = jnp.mean(centred * centred, axis=-1, keepdims=True)
    return (centred * lax.rsqrt(variance + 1e-05) * gain).astype(BF16)


def dot(a, b):
    return lax.dot_general(a, b, (((1,), (0,)), ((), ())), preferred_element_type=F32)


def dot_nt(a, b):
    return lax.dot_general(a, b, (((1,), (1,)), ((), ())), preferred_element_type=F32)


def head_mask():
    head = lax.broadcasted_iota(jnp.int32, (HEADS, FEAT), 0)
    channel = lax.broadcasted_iota(jnp.int32, (HEADS, FEAT), 1) // HEAD_DIM
    return (head == channel).astype(F32)


def expand_heads(queries):
    n = queries.shape[0]
    spread = jnp.broadcast_to(queries[:, None, :], (n, HEADS, FEAT))
    return (spread * head_mask()[None]).reshape(n * HEADS, FEAT).astype(BF16)


def merge_heads(attended, inverse):
    n = attended.shape[0] // HEADS
    scaled = (attended * inverse).reshape(n, HEADS, FEAT) * head_mask()[None]
    return jnp.sum(scaled, axis=1)


def kernel(*refs):
    given, (out_msa, out_pair), held, rest = refs[:13], refs[13:15], refs[15:28], refs[28:]
    msa, pair, g_row, w_row, g_pair, w_bias, wo_row, g_col, w_col, wo_col, g_opm, w_fac, w_fin = held
    (
        bias_src, bias_in, bias, queries, gates, keys, values, logits, weights, denom, staged, msa_src, msa_in,
        unpacked, col_src, col_in, col_logits, col_weights, col_denom, natural, final, left_src, left, right_src, right,
        left_f, left_t, outer, update, result_src, result_in, msa_halves, spread,
        send, recv, load, recv_by, recv_bx, recv_r1,
    ) = rest
    loads = [pltpu.make_async_copy(given[k], held[k], load.at[k]) for k in range(13)]
    for k in (1, 5, 4, 0, 2, 3, 6, 12, 7, 8, 9, 10, 11):
        loads[k].start()

    def loaded(*which):
        for k in which:
            loads[k].wait()

    dap = lax.axis_index("dap")
    rep = lax.axis_index("rep")
    x = dap // 32
    y = (dap // 4) % 8
    xy = dap // 4
    zc = dap % 4
    zh = zc // 2
    core = zc % 2
    member = core * 2 + zh

    def device(xy_, zh_, core_):
        return xy_ * 4 + zh_ * 2 + core_

    barrier = pltpu.get_barrier_semaphore()

    def greet(dap_, rep_):
        pl.semaphore_signal(barrier, inc=1, device_id=(dap_, rep_), device_id_type=MESH)

    def greet_xy(step, _):
        greet(device((xy + step) % 32, zh, core), rep)
        return 0

    lax.fori_loop(1, 32, greet_xy, 0)
    for step in range(1, 8):
        other = (zh * 4 + rep + step) % 8
        greet(device(xy, other // 4, core), other % 4)
    for step in range(4):
        greet(device(((x + step) % 4) * 8 + y, zh, 1 - core), rep)
    greet(device(xy, 1 - zh, 1 - core), rep)
    mirror = rep * 8 + y
    greet(device(mirror, 1 - zh, core), x)

    @pl.when(x != rep)
    def _():
        greet(device(mirror, zh, core), x)

    def push(src, dst, phase, dap_, rep_, into=None):
        pltpu.make_async_remote_copy(
            src_ref=src, dst_ref=dst, send_sem=send.at[phase], recv_sem=recv.at[phase] if into is None else into,
            device_id=(dap_, rep_), device_id_type=MESH,
        ).start()

    def arrived(shaped, phase):
        landed(shaped, recv.at[phase])

    def landed(shaped, sem):
        pltpu.make_async_copy(shaped, shaped, sem).wait()

    def drained(shaped, phase):
        pltpu.make_async_copy(shaped, shaped, send.at[phase]).wait()

    leaving = []

    def finish():
        for shaped, phase in leaving:
            if shaped is not None:
                drained(shaped, phase)
                continue

            @pl.when(x != rep)
            def _():
                drained(right.at[0], RIGHT1)

            @pl.when(x == rep)
            def _():
                drained(right_src, RIGHT1)

    def bias_along_x(y_):
        block = bias.at[x, y_, core]
        for step in range(1, 4):
            push(block, block, BIAS_X, device(((x + step) % 4) * 8 + y, zh, core), rep, recv_bx.at[x * 8 + y_])

    def bias_to_core(y_):
        block = bias.at[:, y_, core]
        push(block, block, BIAS_C, device(xy, zh, 1 - core), rep)

    loaded(1, 4, 5)
    ln_pair = layer_norm(pair[...].reshape(4 * 128, CZ), g_pair[...])
    head_bias = dot_nt(w_bias[...], ln_pair) * LOG2E
    for a in range(4):
        bias_src[a] = head_bias[:, a * 128 : (a + 1) * 128]

    pl.semaphore_wait(barrier, 44 + jnp.where(x != rep, 1, 0))

    for step in range(1, 8):
        other = (zh * 4 + rep + step) % 8
        push(bias_src.at[other % 4], bias_in.at[zh * 4 + rep], BIAS1, device(xy, other // 4, core), other % 4)
    leaving.append((bias_in.at[pl.ds(0, 7)], BIAS1))
    bias_in[zh * 4 + rep] = bias_src[rep]

    loaded(0, 2, 3)
    for s in range(2):
        tokens = layer_norm(msa[s], g_row[...])
        projected = dot(tokens, w_row[:, FEAT : 3 * FEAT]).astype(BF16)
        keys[s] = projected[:, :FEAT]
        values[s] = projected[:, FEAT:]
        for half in range(2):
            msa_halves[s, half] = msa[s, :, half * 128 : (half + 1) * 128]
            for h_ in range(2):
                for c_ in range(2):
                    queries[s, half, pl.ds(c_ * 2 + h_, 32, stride=4), :] = msa_halves[
                        s, half, pl.ds(8 * h_ + 4 * c_ + rep, 32, stride=16), :
                    ]

    arrived(bias_in.at[pl.ds(0, 7)], BIAS1)
    block = jnp.concatenate(
        [jnp.concatenate([bias_in[h_ * 4 + r_] for r_ in range(4)], axis=1) for h_ in range(2)], axis=0
    )
    bias[x, y, core] = block.astype(BF16)
    for step in (4, 3, 5, 2, 6, 1, 7):
        block = bias.at[x, y, core]
        push(block, block, BIAS_Y, device(x * 8 + (y + step) % 8, zh, core), rep, recv_by.at[y])
    bias_along_x(y)

    def row_logits(s):
        tokens = layer_norm(jnp.concatenate([queries[s, 0], queries[s, 1]], axis=1), g_row[...])
        wide = dot(tokens, w_row[:, :FEAT]) * LOGIT_SCALE
        gates[s] = jax.nn.sigmoid(dot(tokens, w_row[:, 3 * FEAT :]))
        logits[s] = dot_nt(expand_heads(wide), keys[s]).reshape(32, 2, 16, RES)

    row_logits(0)
    for step in (1, 7, 2, 6, 3, 5, 4):
        source = (y + step) % 8
        landed(bias.at[0, 0, 0], recv_by.at[source])
        bias_along_x(source)
    row_logits(1)
    for step in (0, 1, 7, 2, 6, 3, 5, 4):
        source = (y + step) % 8
        for other in range(1, 4):
            landed(bias.at[0, 0, 0], recv_bx.at[((x + other) % 4) * 8 + source])
        bias_to_core(source)
    leaving.append((bias.at[0, pl.ds(0, 7), 0], BIAS_Y))
    leaving.append((bias.at[pl.ds(0, 3), :, 0], BIAS_X))
    leaving.append((bias.at[:, :, 0], BIAS_C))

    def row_softmax(group, which):
        rows = pl.ds(group * 4, 4)
        offset = bias[group // 2, pl.ds((group % 2) * 4, 4), which].astype(F32).reshape(64, RES)
        for s in range(2):
            raw = logits[s, rows, which].reshape(64, RES) + offset
            top = jnp.max(raw, axis=-1, keepdims=True)
            powers = jnp.exp2(raw - top)
            total = jnp.sum(powers, axis=-1, keepdims=True)
            weights[s, rows, which] = powers.astype(BF16).reshape(4, 16, RES)
            denom[s, rows, which] = jnp.broadcast_to(1.0 / total, (64, 128)).reshape(4, 16, 128)
        return which

    lax.fori_loop(0, 8, row_softmax, core)
    arrived(bias.at[:, :, 0], BIAS_C)
    lax.fori_loop(0, 8, row_softmax, 1 - core)
    loaded(6)
    for s in range(2):
        attended = dot(weights[s].reshape(1024, RES), values[s])
        merged = merge_heads(attended, denom[s].reshape(1024, 128)[:, :1])
        gated = (merged * gates[s]).astype(BF16)
        change = dot(gated, wo_row[...])
        for half in range(2):
            staged[pl.ds(s * 2 + half, 128, stride=4), :] = queries[s, half] + change[:, half * 128 : (half + 1) * 128]
    msa_src[...] = staged[...].astype(BF16).reshape(32, 16, 128)

    def push_msa(step, _):
        other = (xy + step) % 32
        push(msa_src.at[other], msa_in.at[xy], MSA1, device(other, zh, core), rep)
        return 0

    lax.fori_loop(1, 32, push_msa, 0)
    leaving.append((msa_in.at[pl.ds(0, 31)], MSA1))
    msa_in[xy] = msa_src[xy]
    arrived(msa_in.at[pl.ds(0, 31)], MSA1)
    unpacked[...] = msa_in[...].astype(F32).reshape(512, 128)
    for target in range(4):
        parts = [
            jnp.concatenate(
                [unpacked[pl.ds(target * 4 + s * 2 + half, 32, stride=16), :] for half in range(2)], axis=1
            )
            for s in range(2)
        ]
        col_src[target] = jnp.concatenate(parts, axis=0).astype(BF16)
    for step in range(1, 4):
        other = (member + step) % 4
        push(col_src.at[other], col_in.at[member], MSA2, device(xy, other % 2, other // 2), rep)
    leaving.append((col_in.at[pl.ds(0, 3)], MSA2))
    col_in[member] = col_src[member]
    arrived(col_in.at[pl.ds(0, 3)], MSA2)

    loaded(7, 8, 9, 10, 11, 12)
    middle = col_in[...].astype(F32).reshape(ROWS, FEAT)
    tokens = layer_norm(middle, g_col[...])
    projected = dot(tokens, w_col[...])
    wide = expand_heads(projected[:, :FEAT] * LOGIT_SCALE)
    col_keys = projected[:, FEAT : 2 * FEAT].astype(BF16)
    col_values = projected[:, 2 * FEAT : 3 * FEAT].astype(BF16)
    col_gates = jax.nn.sigmoid(projected[:, 3 * FEAT :])
    col_logits[...] = dot_nt(wide, col_keys)

    def col_softmax(group, _):
        rows = pl.ds(pl.multiple_of(group * 128, 128), 128)
        raw = col_logits[rows, :]
        top = jnp.max(raw, axis=-1, keepdims=True)
        powers = jnp.exp2(raw - top)
        total = jnp.sum(powers, axis=-1, keepdims=True)
        col_weights[rows, :] = powers.astype(BF16)
        col_denom[rows, :] = jnp.broadcast_to(1.0 / total, (128, 128))
        return 0

    lax.fori_loop(0, 16, col_softmax, 0)
    attended = dot(col_weights[...], col_values)
    merged = merge_heads(attended, col_denom[...][:, :1])
    gated = (merged * col_gates).astype(BF16)
    target_rows = middle + dot(gated, wo_col[...])

    ln_opm = layer_norm(target_rows, g_opm[...])
    factors = dot_nt(w_fac[...], ln_opm)
    right_src[...] = factors[FACTOR:].astype(BF16)
    left_src[...] = (factors[:FACTOR] * (1.0 / ROWS)).astype(BF16)
    push(right_src, right.at[y, zh], RIGHT1, device(mirror, 1 - zh, core), x, recv_r1.at[zh])

    @pl.when(x != rep)
    def _():
        push(right_src, right.at[y, zh], RIGHT1, device(mirror, zh, core), x, recv_r1.at[zh])

    @pl.when(x == rep)
    def _():
        right[y, zh] = right_src[...]

    for step in range(1, 4):
        push(left_src, left.at[x, core, rep], LEFT, dap, (rep + step) % 4)
    leaving.append((None, RIGHT1))
    leaving.append((left.at[0, 0, pl.ds(0, 3)], LEFT))
    left[x, core, rep] = left_src[...]
    for m_ in range(4):
        for s in range(2):
            start = (m_ * 2 + s) * 32
            for half in range(2):
                natural[half, pl.ds((m_ % 2) * 4 + (m_ // 2) * 2 + s, 32, stride=8), :] = target_rows[
                    start : start + 32, half * 128 : (half + 1) * 128
                ]
    final[rep] = jnp.concatenate([natural[0], natural[1]], axis=1).astype(BF16)
    def right_along_y(zh_):
        for step in (4, 3, 5, 2, 6, 1, 7):
            block = right.at[y, zh_]
            push(block, block, RIGHT_Y, device(x * 8 + (y + step) % 8, zh, core), rep)

    @pl.when(x != rep)
    def _():
        landed(right_src, recv_r1.at[zh])

    right_along_y(zh)
    arrived(left.at[0, 0, pl.ds(0, 3)], LEFT)
    for step in (2, 1, 3):
        block = left.at[x, core]
        push(block, block, LEFT_X, device(((x + step) % 4) * 8 + y, zh, core), rep)
    leaving.append((left.at[pl.ds(0, 3), 0], LEFT_X))
    landed(right_src, recv_r1.at[1 - zh])
    right_along_y(1 - zh)
    leaving.append((right.at[pl.ds(0, 7)], RIGHT_Y))
    for step in range(1, 4):
        push(final.at[rep], final.at[rep], FINAL, dap, (rep + step) % 4)
    leaving.append((final.at[pl.ds(0, 3)], FINAL))
    arrived(left.at[pl.ds(0, 3), 0], LEFT_X)
    block = left.at[:, core]
    push(block, block, LEFT_C, device(xy, zh, 1 - core), rep)
    leaving.append((left.at[:, 0], LEFT_C))
    arrived(left.at[:, 0], LEFT_C)

    for half in range(2):
        left_f[half] = left[..., half * 128 : (half + 1) * 128].astype(F32).reshape(32 * FACTOR, 128)
    for channel in range(FACTOR):
        left_t[pl.ds(channel * 32, 32), :] = jnp.concatenate(
            [left_f[half, pl.ds(channel, 32, stride=FACTOR), :] for half in range(2)], axis=1
        ).astype(BF16)
    arrived(right.at[pl.ds(0, 7)], RIGHT_Y)
    quarter = lax.broadcasted_iota(jnp.int32, (FACTOR, 128), 1) // 32
    right_all = right[...].reshape(16 * FACTOR, ROWS)
    for part in range(4):
        product = dot_nt(right_all, left_t[pl.ds(part * 256, 256), :])
        for tile in range(2):
            lanes = slice(tile * 128, (tile + 1) * 128)
            for four in range(4):
                blocks = [product[(four * 4 + jq) * FACTOR : (four * 4 + jq + 1) * FACTOR, lanes] for jq in range(4)]
                for cq in range(4):
                    moved = [
                        blocks[jq] if jq == cq else pltpu.roll(blocks[jq], (32 * (jq - cq)) % 128, 1) for jq in range(4)
                    ]
                    joined = jnp.where(
                        quarter < 2,
                        jnp.where(quarter == 0, moved[0], moved[1]),
                        jnp.where(quarter == 2, moved[2], moved[3]),
                    )
                    channel = part * 8 + tile * 4 + cq
                    outer[pl.ds(channel * FACTOR, FACTOR), four * 128 : (four + 1) * 128] = joined.astype(BF16)
    flat = lax.dot_general(w_fin[...], outer[...], (((0,), (0,)), ((), ())), preferred_element_type=F32)
    for four in range(4):
        update[pl.ds(four * 128, 128), :] = flat[:, four * 128 : (four + 1) * 128].T

    for target in range(8):
        for r_ in range(4):
            result_src[target, r_] = update[pl.ds(target * 4 + r_, 16, stride=32), :].astype(BF16)
    mine = x * 2 + core
    for step in range(1, 8):
        other = (mine + step) % 8
        push(result_src.at[other], result_in.at[mine], RESULT, device((other // 2) * 8 + y, zh, other % 2), rep)
    leaving.append((result_in.at[pl.ds(0, 7)], RESULT))
    result_in[mine] = result_src[mine]

    arrived(final.at[pl.ds(0, 3)], FINAL)
    for half in range(2):
        for r_ in range(4):
            spread[half, pl.ds(r_, ROWS, stride=4), :] = final[r_, :, half * 128 : (half + 1) * 128].astype(F32)
        out_msa[:, half * 128 : (half + 1) * 128] = spread[half]

    arrived(result_in.at[pl.ds(0, 7)], RESULT)
    for source in range(8):
        for a in range(4):
            here = pl.ds(4 * (source % 2) + source // 2, 16, stride=8)
            out_pair[a, here, :] = pair[a, here, :] + result_in[source, a].astype(F32)

    finish()


def shards(
    alignment_source_tensor,
    couple_source_tensor,
    horizontal_scale_factor,
    horizontal_projection_matrix,
    couple_scale_factor,
    couple_offset_matrix,
    horizontal_final_matrix,
    vertical_scale_factor,
    vertical_projection_matrix,
    vertical_final_matrix,
    tensorial_scale_factor,
    tensorial_factor_matrix,
    tensorial_final_matrix,
):
    operands = [
        alignment_source_tensor,
        couple_source_tensor,
        horizontal_scale_factor.reshape(1, FEAT),
        horizontal_projection_matrix,
        couple_scale_factor.reshape(1, CZ),
        couple_offset_matrix.T,
        horizontal_final_matrix,
        vertical_scale_factor.reshape(1, FEAT),
        vertical_projection_matrix,
        vertical_final_matrix,
        tensorial_scale_factor.reshape(1, FEAT),
        tensorial_factor_matrix.T,
        tensorial_final_matrix,
    ]
    vmem = pl.BlockSpec(memory_space=pltpu.VMEM)
    scratch = [pltpu.VMEM(a.shape, a.dtype) for a in operands] + [
        pltpu.VMEM((4, 8, 128), F32),
        pltpu.VMEM((8, 8, 128), F32),
        pltpu.VMEM((4, 8, 2, 16, RES), BF16),
        pltpu.VMEM((2, 2, 128, 128), F32),
        pltpu.VMEM((2, 128, FEAT), F32),
        pltpu.VMEM((2, RES, FEAT), BF16),
        pltpu.VMEM((2, RES, FEAT), BF16),
        pltpu.VMEM((2, 32, 2, 16, RES), F32),
        pltpu.VMEM((2, 32, 2, 16, RES), BF16),
        pltpu.VMEM((2, 32, 2, 16, 128), F32),
        pltpu.VMEM((512, 128), F32),
        pltpu.VMEM((32, 16, 128), BF16),
        pltpu.VMEM((32, 16, 128), BF16),
        pltpu.VMEM((512, 128), F32),
        pltpu.VMEM((4, 64, FEAT), BF16),
        pltpu.VMEM((4, 64, FEAT), BF16),
        pltpu.VMEM((ROWS * HEADS, ROWS), F32),
        pltpu.VMEM((ROWS * HEADS, ROWS), BF16),
        pltpu.VMEM((ROWS * HEADS, 128), F32),
        pltpu.VMEM((2, ROWS, 128), F32),
        pltpu.VMEM((4, ROWS, FEAT), BF16),
        pltpu.VMEM((FACTOR, ROWS), BF16),
        pltpu.VMEM((4, 2, 4, FACTOR, ROWS), BF16),
        pltpu.VMEM((FACTOR, ROWS), BF16),
        pltpu.VMEM((8, 2, FACTOR, ROWS), BF16),
        pltpu.VMEM((2, 32 * FACTOR, 128), F32),
        pltpu.VMEM((32 * FACTOR, ROWS), BF16),
        pltpu.VMEM((FACTOR * FACTOR, 512), BF16),
        pltpu.VMEM((512, CZ), F32),
        pltpu.VMEM((8, 4, 16, CZ), BF16),
        pltpu.VMEM((8, 4, 16, CZ), BF16),
        pltpu.VMEM((2, 2, RES, 128), F32),
        pltpu.VMEM((2, ROWS * 4, 128), F32),
        pltpu.SemaphoreType.DMA((PHASES,)),
        pltpu.SemaphoreType.DMA((PHASES,)),
        pltpu.SemaphoreType.DMA((len(operands),)),
        pltpu.SemaphoreType.DMA((8,)),
        pltpu.SemaphoreType.DMA((32,)),
        pltpu.SemaphoreType.DMA((2,)),
    ]
    out_msa, out_pair = pl.pallas_call(
        kernel,
        out_shape=(
            jax.ShapeDtypeStruct((ROWS * 4, FEAT), F32),
            jax.ShapeDtypeStruct((4, 128, CZ), F32),
        ),
        in_specs=[pl.BlockSpec(memory_space=pltpu.HBM)] * len(operands),
        out_specs=(vmem, vmem),
        scratch_shapes=scratch,
        compiler_params=pltpu.CompilerParams(
            collective_id=0, has_side_effects=True, vmem_limit_bytes=60 * 1024 * 1024
        ),
    )(*operands)
    return out_msa.reshape(ROWS, 4, FEAT), out_pair


def solution(mesh):
    return jax.shard_map(
        shards,
        mesh=mesh,
        in_specs=(P("dap", None, None), P("dap", "rep", None)) + (P(),) * 11,
        out_specs=(P(None, "dap", None), P("dap", "rep", None)),
        check_vma=False,
    )
```

```python
import math

import jax
import jax.numpy as jnp
from jax import lax
from jax.experimental import pallas as pl
from jax.experimental.pallas import tpu as pltpu
from jax.sharding import PartitionSpec as P

HEADS = 8
HEAD_DIM = 32
FEAT = HEADS * HEAD_DIM
CZ = 128
ROWS = 256
RES = 512
FACTOR = 32
LOG2E = math.log2(math.e)
LOGIT_SCALE = HEAD_DIM ** (-0.5) * LOG2E
MESH = pl.DeviceIdType.MESH
F32 = jnp.float32
BF16 = jnp.bfloat16

BIAS1, BIAS_Y, BIAS_X, BIAS_C, MSA1, MSA2, LEFT, LEFT_X, LEFT_C, FINAL, RIGHT1, RIGHT_Y, RESULT = range(13)
PHASES = 13


def layer_norm(values, gain):
    average = jnp.mean(values, axis=-1, keepdims=True)
    centred = values - average
    variance = jnp.mean(centred * centred, axis=-1, keepdims=True)
    return (centred * lax.rsqrt(variance + 1e-05) * gain).astype(BF16)


def dot(a, b):
    return lax.dot_general(a, b, (((1,), (0,)), ((), ())), preferred_element_type=F32)


def dot_nt(a, b):
    return lax.dot_general(a, b, (((1,), (1,)), ((), ())), preferred_element_type=F32)


def head_mask():
    head = lax.broadcasted_iota(jnp.int32, (HEADS, FEAT), 0)
    channel = lax.broadcasted_iota(jnp.int32, (HEADS, FEAT), 1) // HEAD_DIM
    return (head == channel).astype(F32)


def expand_heads(queries):
    n = queries.shape[0]
    spread = jnp.broadcast_to(queries[:, None, :], (n, HEADS, FEAT))
    return (spread * head_mask()[None]).reshape(n * HEADS, FEAT).astype(BF16)


def merge_heads(attended, inverse):
    n = attended.shape[0] // HEADS
    scaled = (attended * inverse).reshape(n, HEADS, FEAT) * head_mask()[None]
    return jnp.sum(scaled, axis=1)


def kernel(*refs):
    given, (out_msa, out_pair), held, rest = refs[:13], refs[13:15], refs[15:28], refs[28:]
    msa, pair, g_row, w_row, g_pair, w_bias, wo_row, g_col, w_col, wo_col, g_opm, w_fac, w_fin = held
    (
        bias_src, bias_in, bias, queries, gates, keys, values, logits, weights, denom, staged, msa_src, msa_in,
        unpacked, col_src, col_in, col_logits, col_weights, col_denom, natural, final, left_src, left, right_src, right,
        left_f, left_t, outer, update, result_src, result_in, msa_halves,
        send, recv, load, recv_by, recv_bx, recv_bc, recv_r1,
    ) = rest
    loads = [pltpu.make_async_copy(given[k], held[k], load.at[k]) for k in range(13)]
    for k in (1, 5, 4):
        loads[k].start()

    def loaded(*which):
        for k in which:
            loads[k].wait()

    dap = lax.axis_index("dap")
    rep = lax.axis_index("rep")
    x = dap // 32
    y = (dap // 4) % 8
    xy = dap // 4
    zc = dap % 4
    zh = zc // 2
    core = zc % 2

    def device(xy_, zh_, core_):
        return xy_ * 4 + zh_ * 2 + core_

    barrier = pltpu.get_barrier_semaphore()

    def greet(dap_, rep_):
        pl.semaphore_signal(barrier, inc=1, device_id=(dap_, rep_), device_id_type=MESH)

    def far_first(turn):
        return (xy + (turn + 11) % 31 + 1) % 32

    def greet_xy(turn, _):
        greet(device(far_first(turn), zh, core), rep)
        return 0

    mirror = rep * 8 + y
    greet(device(mirror, 1 - zh, core), x)

    @pl.when(x != rep)
    def _():
        greet(device(mirror, zh, core), x)

    lax.fori_loop(0, 31, greet_xy, 0)
    for step in (4, 3, 5, 2, 6, 1, 7):
        other = (zh * 4 + rep + step) % 8
        greet(device(xy, other // 4, core), other % 4)
    for step in range(4):
        greet(device(((x + step) % 4) * 8 + y, zh, 1 - core), rep)
    greet(device(xy, 1 - zh, 1 - core), rep)
    for k in (0, 2, 3, 6, 12, 7, 8, 9, 10, 11):
        loads[k].start()

    def push(src, dst, phase, dap_, rep_, into=None):
        pltpu.make_async_remote_copy(
            src_ref=src, dst_ref=dst, send_sem=send.at[phase], recv_sem=recv.at[phase] if into is None else into,
            device_id=(dap_, rep_), device_id_type=MESH,
        ).start()

    def arrived(shaped, phase):
        landed(shaped, recv.at[phase])

    def landed(shaped, sem):
        pltpu.make_async_copy(shaped, shaped, sem).wait()

    def drained(shaped, phase):
        pltpu.make_async_copy(shaped, shaped, send.at[phase]).wait()

    leaving = []

    def finish():
        for shaped, phase in leaving:
            if shaped is not None:
                drained(shaped, phase)
                continue

            @pl.when(x != rep)
            def _():
                drained(right.at[0], RIGHT1)

            @pl.when(x == rep)
            def _():
                drained(right_src, RIGHT1)

    def bias_along_x(y_):
        block = bias.at[x, y_, core]
        for step in range(1, 4):
            push(block, block, BIAS_X, device(((x + step) % 4) * 8 + y, zh, core), rep, recv_bx.at[x * 8 + y_])

    def bias_to_core(y_):
        block = bias.at[:, y_, core]
        push(block, block, BIAS_C, device(xy, zh, 1 - core), rep, recv_bc.at[y_])

    loaded(1, 4, 5)
    ln_pair = layer_norm(pair[...].reshape(4 * 128, CZ), g_pair[...])
    head_bias = dot_nt(w_bias[...], ln_pair) * LOG2E
    for a in range(4):
        bias_src[a] = head_bias[:, a * 128 : (a + 1) * 128]

    pl.semaphore_wait(barrier, 44 + jnp.where(x != rep, 1, 0))

    for step in (4, 3, 5, 2, 6, 1, 7):
        other = (zh * 4 + rep + step) % 8
        push(bias_src.at[other % 4], bias_in.at[zh * 4 + rep], BIAS1, device(xy, other // 4, core), other % 4)
    leaving.append((bias_in.at[pl.ds(0, 7)], BIAS1))
    bias_in[zh * 4 + rep] = bias_src[rep]

    loaded(0, 2, 3)
    for s in range(2):
        tokens = layer_norm(msa[s], g_row[...])
        projected = dot(tokens, w_row[:, FEAT : 3 * FEAT]).astype(BF16)
        keys[s] = projected[:, :FEAT]
        values[s] = projected[:, FEAT:]
        for half in range(2):
            msa_halves[s, half] = msa[s, :, half * 128 : (half + 1) * 128]
            for h_ in range(2):
                for c_ in range(2):
                    queries[s, c_, half, pl.ds(h_, 32, stride=2), :] = msa_halves[
                        s, half, pl.ds(8 * h_ + 4 * c_ + rep, 32, stride=16), :
                    ]

    arrived(bias_in.at[pl.ds(0, 7)], BIAS1)
    block = jnp.concatenate(
        [jnp.concatenate([bias_in[h_ * 4 + r_] for r_ in range(4)], axis=1) for h_ in range(2)], axis=0
    )
    bias[x, y, core] = block.astype(BF16)
    for step in (4, 3, 5, 2, 6, 1, 7):
        block = bias.at[x, y, core]
        push(block, block, BIAS_Y, device(x * 8 + (y + step) % 8, zh, core), rep, recv_by.at[y])
    bias_along_x(y)

    def row_logits(s):
        halves = [jnp.concatenate([queries[s, 0, half], queries[s, 1, half]], axis=0) for half in range(2)]
        tokens = layer_norm(jnp.concatenate(halves, axis=1), g_row[...])
        wide = dot(tokens, w_row[:, :FEAT]) * LOGIT_SCALE
        gates[s] = jax.nn.sigmoid(dot(tokens, w_row[:, 3 * FEAT :])).reshape(2, 64, FEAT)
        logits[s] = dot_nt(expand_heads(wide), keys[s]).reshape(2, 4, 8, 16, RES)

    def nearest(turn):
        away = (turn + 1) // 2
        return (y + jnp.where(turn % 2 == 1, away, 8 - away)) % 8

    def row_softmax(y_, which):
        offset = bias[:, y_, which].astype(F32).reshape(64, RES)
        for s in range(2):
            raw = logits[s, which, :, y_].reshape(64, RES) + offset
            top = jnp.max(raw, axis=-1, keepdims=True)
            powers = jnp.exp2(raw - top)
            total = jnp.sum(powers, axis=-1, keepdims=True)
            weights[s, which, :, y_] = powers.astype(BF16).reshape(4, 16, RES)
            denom[s, which, :, y_] = jnp.broadcast_to(1.0 / total, (64, 128)).reshape(4, 16, 128)

    def row_finish(which):
        for s in range(2):
            attended = dot(weights[s, which].reshape(512, RES), values[s])
            merged = merge_heads(attended, denom[s, which].reshape(512, 128)[:, :1])
            gated = (merged * gates[s, which]).astype(BF16)
            change = dot(gated, wo_row[...])
            for half in range(2):
                staged[pl.ds(which * 4 + s * 2 + half, 64, stride=8), :] = (
                    queries[s, which, half] + change[:, half * 128 : (half + 1) * 128]
                )

    row_logits(0)
    for step in (1, 7, 2, 6, 3, 5, 4):
        source = (y + step) % 8
        landed(bias.at[0, 0, 0], recv_by.at[source])
        bias_along_x(source)
    row_logits(1)

    def own_queries(turn, _):
        source = nearest(turn)
        for other in range(1, 4):
            landed(bias.at[0, 0, 0], recv_bx.at[((x + other) % 4) * 8 + source])
        bias_to_core(source)
        row_softmax(source, core)
        return 0

    def other_queries(turn, _):
        source = nearest(turn)
        landed(bias.at[:, 0, 0], recv_bc.at[source])
        row_softmax(source, 1 - core)
        return 0

    loaded(6)
    lax.fori_loop(0, 8, own_queries, 0)
    row_finish(core)
    lax.fori_loop(0, 8, other_queries, 0)
    row_finish(1 - core)
    leaving.append((bias.at[0, pl.ds(0, 7), 0], BIAS_Y))
    leaving.append((bias.at[pl.ds(0, 3), :, 0], BIAS_X))
    leaving.append((bias.at[:, :, 0], BIAS_C))
    msa_src[...] = staged[...].astype(BF16).reshape(32, 16, 128)

    def push_msa(turn, _):
        other = far_first(turn)
        push(msa_src.at[other], msa_in.at[xy], MSA1, device(other, zh, core), rep)
        return 0

    lax.fori_loop(0, 31, push_msa, 0)
    leaving.append((msa_in.at[pl.ds(0, 31)], MSA1))
    msa_in[xy] = msa_src[xy]
    arrived(msa_in.at[pl.ds(0, 31)], MSA1)
    unpacked[...] = msa_in[...].astype(F32).reshape(512, 128)
    for target in range(4):
        parts = [
            jnp.concatenate(
                [unpacked[pl.ds(target * 4 + s * 2 + half, 32, stride=16), :] for half in range(2)], axis=1
            )
            for s in range(2)
        ]
        col_src[target] = jnp.concatenate(parts, axis=0).astype(BF16)
    for step in range(1, 4):
        other = (zc + step) % 4
        push(col_src.at[other], col_in.at[zc], MSA2, device(xy, other // 2, other % 2), rep)
    leaving.append((col_in.at[pl.ds(0, 3)], MSA2))
    col_in[zc] = col_src[zc]
    arrived(col_in.at[pl.ds(0, 3)], MSA2)

    loaded(7, 8, 9, 10, 11, 12)
    middle = col_in[...].astype(F32).reshape(ROWS, FEAT)
    tokens = layer_norm(middle, g_col[...])
    projected = dot(tokens, w_col[...])
    wide = expand_heads(projected[:, :FEAT] * LOGIT_SCALE)
    col_keys = projected[:, FEAT : 2 * FEAT].astype(BF16)
    col_values = projected[:, 2 * FEAT : 3 * FEAT].astype(BF16)
    col_gates = jax.nn.sigmoid(projected[:, 3 * FEAT :])
    col_logits[...] = dot_nt(wide, col_keys)

    def col_softmax(group, _):
        rows = pl.ds(pl.multiple_of(group * 128, 128), 128)
        raw = col_logits[rows, :]
        top = jnp.max(raw, axis=-1, keepdims=True)
        powers = jnp.exp2(raw - top)
        total = jnp.sum(powers, axis=-1, keepdims=True)
        col_weights[rows, :] = powers.astype(BF16)
        col_denom[rows, :] = jnp.broadcast_to(1.0 / total, (128, 128))
        return 0

    lax.fori_loop(0, 16, col_softmax, 0)
    attended = dot(col_weights[...], col_values)
    merged = merge_heads(attended, col_denom[...][:, :1])
    gated = (merged * col_gates).astype(BF16)
    target_rows = middle + dot(gated, wo_col[...])

    ln_opm = layer_norm(target_rows, g_opm[...])
    factors = dot_nt(w_fac[...], ln_opm)
    right_src[...] = factors[FACTOR:].astype(BF16)
    left_src[...] = (factors[:FACTOR] * (1.0 / ROWS)).astype(BF16)
    push(right_src, right.at[y, zh], RIGHT1, device(mirror, 1 - zh, core), x, recv_r1.at[zh])

    @pl.when(x != rep)
    def _():
        push(right_src, right.at[y, zh], RIGHT1, device(mirror, zh, core), x, recv_r1.at[zh])

    @pl.when(x == rep)
    def _():
        right[y, zh] = right_src[...]

    for step in range(1, 4):
        push(left_src, left.at[x, core, rep], LEFT, dap, (rep + step) % 4)
    leaving.append((None, RIGHT1))
    leaving.append((left.at[0, 0, pl.ds(0, 3)], LEFT))
    left[x, core, rep] = left_src[...]
    for m_ in range(4):
        for s in range(2):
            start = (m_ * 2 + s) * 32
            for half in range(2):
                natural[half, pl.ds(m_ * 2 + s, 32, stride=8), :] = target_rows[
                    start : start + 32, half * 128 : (half + 1) * 128
                ]
    final[rep] = jnp.concatenate([natural[0], natural[1]], axis=1).astype(BF16)
    def right_along_y(zh_):
        for step in (4, 3, 5, 2, 6, 1, 7):
            block = right.at[y, zh_]
            push(block, block, RIGHT_Y, device(x * 8 + (y + step) % 8, zh, core), rep)

    @pl.when(x != rep)
    def _():
        landed(right_src, recv_r1.at[zh])

    right_along_y(zh)
    arrived(left.at[0, 0, pl.ds(0, 3)], LEFT)
    for step in (2, 1, 3):
        block = left.at[x, core]
        push(block, block, LEFT_X, device(((x + step) % 4) * 8 + y, zh, core), rep)
    leaving.append((left.at[pl.ds(0, 3), 0], LEFT_X))
    landed(right_src, recv_r1.at[1 - zh])
    right_along_y(1 - zh)
    leaving.append((right.at[pl.ds(0, 7)], RIGHT_Y))
    for step in range(1, 4):
        push(final.at[rep], final.at[rep], FINAL, dap, (rep + step) % 4)
    leaving.append((final.at[pl.ds(0, 3)], FINAL))
    arrived(left.at[pl.ds(0, 3), 0], LEFT_X)
    block = left.at[:, core]
    push(block, block, LEFT_C, device(xy, zh, 1 - core), rep)
    leaving.append((left.at[:, 0], LEFT_C))
    arrived(left.at[:, 0], LEFT_C)

    for half in range(2):
        left_f[half] = left[..., half * 128 : (half + 1) * 128].astype(F32).reshape(32 * FACTOR, 128)
    for channel in range(FACTOR):
        left_t[pl.ds(channel * 32, 32), :] = jnp.concatenate(
            [left_f[half, pl.ds(channel, 32, stride=FACTOR), :] for half in range(2)], axis=1
        ).astype(BF16)
    arrived(right.at[pl.ds(0, 7)], RIGHT_Y)
    quarter = lax.broadcasted_iota(jnp.int32, (FACTOR, 128), 1) // 32
    right_all = right[...].reshape(16 * FACTOR, ROWS)
    for part in range(4):
        product = dot_nt(right_all, left_t[pl.ds(part * 256, 256), :])
        for tile in range(2):
            lanes = slice(tile * 128, (tile + 1) * 128)
            for four in range(4):
                blocks = [product[(four * 4 + jq) * FACTOR : (four * 4 + jq + 1) * FACTOR, lanes] for jq in range(4)]
                for cq in range(4):
                    moved = [
                        blocks[jq] if jq == cq else pltpu.roll(blocks[jq], (32 * (jq - cq)) % 128, 1) for jq in range(4)
                    ]
                    joined = jnp.where(
                        quarter < 2,
                        jnp.where(quarter == 0, moved[0], moved[1]),
                        jnp.where(quarter == 2, moved[2], moved[3]),
                    )
                    channel = part * 8 + tile * 4 + cq
                    outer[pl.ds(channel * FACTOR, FACTOR), four * 128 : (four + 1) * 128] = joined.astype(BF16)
    flat = lax.dot_general(w_fin[...], outer[...], (((0,), (0,)), ((), ())), preferred_element_type=F32)
    for four in range(4):
        update[pl.ds(four * 128, 128), :] = flat[:, four * 128 : (four + 1) * 128].T

    for target in range(8):
        for r_ in range(4):
            result_src[target, r_] = update[pl.ds(target * 4 + r_, 16, stride=32), :].astype(BF16)
    mine = x * 2 + core
    for step in range(1, 8):
        other = (mine + step) % 8
        push(result_src.at[other], result_in.at[mine], RESULT, device((other // 2) * 8 + y, zh, other % 2), rep)
    leaving.append((result_in.at[pl.ds(0, 7)], RESULT))
    result_in[mine] = result_src[mine]

    arrived(final.at[pl.ds(0, 3)], FINAL)
    for half in range(2):
        for r_ in range(4):
            out_msa[pl.ds(half * 4 + r_, ROWS, stride=8), :] = final[r_, :, half * 128 : (half + 1) * 128].astype(F32)

    arrived(result_in.at[pl.ds(0, 7)], RESULT)
    for source in range(8):
        for a in range(4):
            here = pl.ds(4 * (source % 2) + source // 2, 16, stride=8)
            out_pair[a, here, :] = pair[a, here, :] + result_in[source, a].astype(F32)

    finish()


def shards(
    alignment_source_tensor,
    couple_source_tensor,
    horizontal_scale_factor,
    horizontal_projection_matrix,
    couple_scale_factor,
    couple_offset_matrix,
    horizontal_final_matrix,
    vertical_scale_factor,
    vertical_projection_matrix,
    vertical_final_matrix,
    tensorial_scale_factor,
    tensorial_factor_matrix,
    tensorial_final_matrix,
):
    operands = [
        alignment_source_tensor,
        couple_source_tensor,
        horizontal_scale_factor.reshape(1, FEAT),
        horizontal_projection_matrix,
        couple_scale_factor.reshape(1, CZ),
        couple_offset_matrix.T,
        horizontal_final_matrix,
        vertical_scale_factor.reshape(1, FEAT),
        vertical_projection_matrix,
        vertical_final_matrix,
        tensorial_scale_factor.reshape(1, FEAT),
        tensorial_factor_matrix.T,
        tensorial_final_matrix,
    ]
    vmem = pl.BlockSpec(memory_space=pltpu.VMEM)
    scratch = [pltpu.VMEM(a.shape, a.dtype) for a in operands] + [
        pltpu.VMEM((4, 8, 128), F32),
        pltpu.VMEM((8, 8, 128), F32),
        pltpu.VMEM((4, 8, 2, 16, RES), BF16),
        pltpu.VMEM((2, 2, 2, 64, 128), F32),
        pltpu.VMEM((2, 2, 64, FEAT), F32),
        pltpu.VMEM((2, RES, FEAT), BF16),
        pltpu.VMEM((2, RES, FEAT), BF16),
        pltpu.VMEM((2, 2, 4, 8, 16, RES), F32),
        pltpu.VMEM((2, 2, 4, 8, 16, RES), BF16),
        pltpu.VMEM((2, 2, 4, 8, 16, 128), F32),
        pltpu.VMEM((512, 128), F32),
        pltpu.VMEM((32, 16, 128), BF16),
        pltpu.VMEM((32, 16, 128), BF16),
        pltpu.VMEM((512, 128), F32),
        pltpu.VMEM((4, 64, FEAT), BF16),
        pltpu.VMEM((4, 64, FEAT), BF16),
        pltpu.VMEM((ROWS * HEADS, ROWS), F32),
        pltpu.VMEM((ROWS * HEADS, ROWS), BF16),
        pltpu.VMEM((ROWS * HEADS, 128), F32),
        pltpu.VMEM((2, ROWS, 128), F32),
        pltpu.VMEM((4, ROWS, FEAT), BF16),
        pltpu.VMEM((FACTOR, ROWS), BF16),
        pltpu.VMEM((4, 2, 4, FACTOR, ROWS), BF16),
        pltpu.VMEM((FACTOR, ROWS), BF16),
        pltpu.VMEM((8, 2, FACTOR, ROWS), BF16),
        pltpu.VMEM((2, 32 * FACTOR, 128), F32),
        pltpu.VMEM((32 * FACTOR, ROWS), BF16),
        pltpu.VMEM((FACTOR * FACTOR, 512), BF16),
        pltpu.VMEM((512, CZ), F32),
        pltpu.VMEM((8, 4, 16, CZ), BF16),
        pltpu.VMEM((8, 4, 16, CZ), BF16),
        pltpu.VMEM((2, 2, RES, 128), F32),
        pltpu.SemaphoreType.DMA((PHASES,)),
        pltpu.SemaphoreType.DMA((PHASES,)),
        pltpu.SemaphoreType.DMA((len(operands),)),
        pltpu.SemaphoreType.DMA((8,)),
        pltpu.SemaphoreType.DMA((32,)),
        pltpu.SemaphoreType.DMA((8,)),
        pltpu.SemaphoreType.DMA((2,)),
    ]
    out_msa, out_pair = pl.pallas_call(
        kernel,
        out_shape=(
            jax.ShapeDtypeStruct((ROWS * 8, 128), F32),
            jax.ShapeDtypeStruct((4, 128, CZ), F32),
        ),
        in_specs=[pl.BlockSpec(memory_space=pltpu.HBM)] * len(operands),
        out_specs=(vmem, vmem),
        scratch_shapes=scratch,
        compiler_params=pltpu.CompilerParams(
            collective_id=0, has_side_effects=True, vmem_limit_bytes=60 * 1024 * 1024
        ),
    )(*operands)
    return jnp.swapaxes(out_msa.reshape(ROWS, 2, 4, 128), 1, 2).reshape(ROWS, 4, FEAT), out_pair


def solution(mesh):
    return jax.shard_map(
        shards,
        mesh=mesh,
        in_specs=(P("dap", None, None), P("dap", "rep", None)) + (P(),) * 11,
        out_specs=(P(None, "dap", None), P("dap", "rep", None)),
        check_vma=False,
    )
```

```python
import math

import jax
import jax.numpy as jnp
from jax import lax
from jax.experimental import pallas as pl
from jax.experimental.pallas import tpu as pltpu
from jax.sharding import PartitionSpec as P

HEADS = 8
HEAD_DIM = 32
FEAT = HEADS * HEAD_DIM
CZ = 128
ROWS = 256
RES = 512
FACTOR = 32
LOG2E = math.log2(math.e)
LOGIT_SCALE = HEAD_DIM ** (-0.5) * LOG2E
MESH = pl.DeviceIdType.MESH
F32 = jnp.float32
BF16 = jnp.bfloat16

BIAS1, BIAS_Y, BIAS_X, BIAS_C, MSA1, MSA2, LEFT, LEFT_X, LEFT_C, FINAL, RIGHT1, RIGHT_Y, RESULT = range(13)
PHASES = 13


def layer_norm(values, gain):
    average = jnp.mean(values, axis=-1, keepdims=True)
    centred = values - average
    variance = jnp.mean(centred * centred, axis=-1, keepdims=True)
    return (centred * lax.rsqrt(variance + 1e-05) * gain).astype(BF16)


def dot(a, b):
    return lax.dot_general(a, b, (((1,), (0,)), ((), ())), preferred_element_type=F32)


def dot_nt(a, b):
    return lax.dot_general(a, b, (((1,), (1,)), ((), ())), preferred_element_type=F32)


def head_mask():
    head = lax.broadcasted_iota(jnp.int32, (HEADS, FEAT), 0)
    channel = lax.broadcasted_iota(jnp.int32, (HEADS, FEAT), 1) // HEAD_DIM
    return (head == channel).astype(F32)


def expand_heads(queries):
    n = queries.shape[0]
    spread = jnp.broadcast_to(queries[:, None, :], (n, HEADS, FEAT))
    return (spread * head_mask()[None]).reshape(n * HEADS, FEAT).astype(BF16)


def merge_heads(attended, inverse):
    n = attended.shape[0] // HEADS
    scaled = (attended * inverse).reshape(n, HEADS, FEAT) * head_mask()[None]
    return jnp.sum(scaled, axis=1)


def kernel(*refs):
    given, (out_msa, out_pair), held, rest = refs[:13], refs[13:15], refs[15:28], refs[28:]
    msa, pair, g_row, w_row, g_pair, w_bias, wo_row, g_col, w_col, wo_col, g_opm, w_fac, w_fin = held
    (
        bias_src, bias_in, bias, queries, gates, keys, values, logits, weights, denom, staged, msa_src, msa_in,
        unpacked, col_src, col_in, col_logits, col_weights, col_denom, natural, final, left_src, left, right_src, right,
        left_f, left_t, final_t, outer, update, result_src, result_in, msa_halves,
        send, recv, load, recv_by, recv_bx, recv_bc, recv_r1, recv_ry,
    ) = rest
    loads = [pltpu.make_async_copy(given[k], held[k], load.at[k]) for k in range(13)]
    for k in (1, 5, 4):
        loads[k].start()

    def loaded(*which):
        for k in which:
            loads[k].wait()

    dap = lax.axis_index("dap")
    rep = lax.axis_index("rep")
    x = dap >> 5
    y = (dap >> 2) & 7
    xy = dap >> 2
    zc = dap & 3
    zh = zc >> 1
    core = zc & 1

    def device(xy_, zh_, core_):
        return xy_ * 4 + zh_ * 2 + core_

    barrier = pltpu.get_barrier_semaphore()

    def greet(dap_, rep_):
        pl.semaphore_signal(barrier, inc=1, device_id=(dap_, rep_), device_id_type=MESH)

    def far_first(turn):
        return (xy + turn + jnp.where(turn < 20, 12, -19)) & 31

    def greet_xy(turn, _):
        greet(device(far_first(turn), zh, core), rep)
        return 0

    mirror = rep * 8 + y
    greet(device(mirror, 1 - zh, core), x)

    @pl.when(x != rep)
    def _():
        greet(device(mirror, zh, core), x)

    lax.fori_loop(0, 31, greet_xy, 0)
    for step in (4, 3, 5, 2, 6, 1, 7):
        other = (zh * 4 + rep + step) & 7
        greet(device(xy, other >> 2, core), other & 3)
    for step in range(4):
        greet(device(((x + step) & 3) * 8 + y, zh, 1 - core), rep)
    greet(device(xy, 1 - zh, 1 - core), rep)
    for k in (0, 2, 3, 6, 12, 7, 8, 9, 10, 11):
        loads[k].start()

    def push(src, dst, phase, dap_, rep_, into=None):
        pltpu.make_async_remote_copy(
            src_ref=src, dst_ref=dst, send_sem=send.at[phase], recv_sem=recv.at[phase] if into is None else into,
            device_id=(dap_, rep_), device_id_type=MESH,
        ).start()

    def arrived(shaped, phase):
        landed(shaped, recv.at[phase])

    def landed(shaped, sem):
        pltpu.make_async_copy(shaped, shaped, sem).wait()

    def drained(shaped, phase):
        pltpu.make_async_copy(shaped, shaped, send.at[phase]).wait()

    leaving = []

    def finish():
        for shaped, phase in leaving:
            if shaped is not None:
                drained(shaped, phase)
                continue

            @pl.when(x != rep)
            def _():
                drained(right.at[0], RIGHT1)

            @pl.when(x == rep)
            def _():
                drained(right_src, RIGHT1)

    def bias_along_x(y_):
        block = bias.at[x, y_, core]
        for step in range(1, 4):
            push(block, block, BIAS_X, device(((x + step) & 3) * 8 + y, zh, core), rep, recv_bx.at[x * 8 + y_])

    def bias_to_core(y_):
        block = bias.at[:, y_, core]
        push(block, block, BIAS_C, device(xy, zh, 1 - core), rep, recv_bc.at[y_])

    loaded(1, 4, 5)
    ln_pair = layer_norm(pair[...].reshape(4 * 128, CZ), g_pair[...])
    head_bias = dot_nt(w_bias[...], ln_pair) * LOG2E
    for a in range(4):
        bias_src[a] = head_bias[:, a * 128 : (a + 1) * 128]

    pl.semaphore_wait(barrier, 44 + jnp.where(x != rep, 1, 0))

    for step in (4, 3, 5, 2, 6, 1, 7):
        other = (zh * 4 + rep + step) & 7
        push(bias_src.at[other & 3], bias_in.at[zh * 4 + rep], BIAS1, device(xy, other >> 2, core), other & 3)
    leaving.append((bias_in.at[pl.ds(0, 7)], BIAS1))
    bias_in[zh * 4 + rep] = bias_src[rep]

    loaded(0, 2, 3)
    for s in range(2):
        tokens = layer_norm(msa[s], g_row[...])
        projected = dot(tokens, w_row[:, FEAT : 3 * FEAT]).astype(BF16)
        keys[s] = projected[:, :FEAT]
        values[s] = projected[:, FEAT:]
        for half in range(2):
            msa_halves[s, half] = msa[s, :, half * 128 : (half + 1) * 128]
            for h_ in range(2):
                for c_ in range(2):
                    queries[s, c_, half, pl.ds(h_, 32, stride=2), :] = msa_halves[
                        s, half, pl.ds(8 * h_ + 4 * c_ + rep, 32, stride=16), :
                    ]

    arrived(bias_in.at[pl.ds(0, 7)], BIAS1)
    block = jnp.concatenate(
        [jnp.concatenate([bias_in[h_ * 4 + r_] for r_ in range(4)], axis=1) for h_ in range(2)], axis=0
    )
    bias[x, y, core] = block.astype(BF16)
    for step in (4, 3, 5, 2, 6, 1, 7):
        block = bias.at[x, y, core]
        push(block, block, BIAS_Y, device(x * 8 + ((y + step) & 7), zh, core), rep, recv_by.at[y])
    bias_along_x(y)

    def row_logits(s):
        halves = [jnp.concatenate([queries[s, 0, half], queries[s, 1, half]], axis=0) for half in range(2)]
        tokens = layer_norm(jnp.concatenate(halves, axis=1), g_row[...])
        wide = dot(tokens, w_row[:, :FEAT]) * LOGIT_SCALE
        gates[s] = jax.nn.sigmoid(dot(tokens, w_row[:, 3 * FEAT :])).reshape(2, 64, FEAT)
        logits[s] = dot_nt(expand_heads(wide), keys[s]).reshape(2, 4, 8, 16, RES)

    def nearest(turn):
        away = (turn + 1) >> 1
        return (y + jnp.where((turn & 1) == 1, away, 8 - away)) & 7

    def row_softmax(y_, which):
        offset = bias[:, y_, which].astype(F32).reshape(64, RES)
        for s in range(2):
            raw = logits[s, which, :, y_].reshape(64, RES) + offset
            top = jnp.max(raw, axis=-1, keepdims=True)
            powers = jnp.exp2(raw - top)
            total = jnp.sum(powers, axis=-1, keepdims=True)
            weights[s, which, :, y_] = powers.astype(BF16).reshape(4, 16, RES)
            denom[s, which, :, y_] = jnp.broadcast_to(1.0 / total, (64, 128)).reshape(4, 16, 128)

    def row_finish(which):
        for s in range(2):
            attended = dot(weights[s, which].reshape(512, RES), values[s])
            merged = merge_heads(attended, denom[s, which].reshape(512, 128)[:, :1])
            gated = (merged * gates[s, which]).astype(BF16)
            change = dot(gated, wo_row[...])
            for half in range(2):
                staged[pl.ds(which * 4 + s * 2 + half, 64, stride=8), :] = (
                    queries[s, which, half] + change[:, half * 128 : (half + 1) * 128]
                )

    row_logits(0)
    for step in (1, 7, 2, 6, 3, 5, 4):
        source = (y + step) & 7
        landed(bias.at[0, 0, 0], recv_by.at[source])
        bias_along_x(source)
    row_logits(1)
    loaded(12)
    final_t[...] = w_fin[...].astype(F32).T.astype(BF16)

    def own_arrived(turn):
        source = nearest(turn)
        for other in range(1, 4):
            landed(bias.at[0, 0, 0], recv_bx.at[((x + other) & 3) * 8 + source])
        bias_to_core(source)
        return source

    def other_arrived(turn):
        source = nearest(turn)
        landed(bias.at[:, 0, 0], recv_bc.at[source])
        return source

    def both_queries(turn, _):
        mine_, theirs = own_arrived(turn), other_arrived(turn - 1)
        row_softmax(mine_, core)
        row_softmax(theirs, 1 - core)
        return 0

    loaded(6)
    row_softmax(own_arrived(0), core)
    lax.fori_loop(1, 8, both_queries, 0)
    row_softmax(other_arrived(7), 1 - core)
    row_finish(core)
    row_finish(1 - core)
    leaving.append((bias.at[0, pl.ds(0, 7), 0], BIAS_Y))
    leaving.append((bias.at[pl.ds(0, 3), :, 0], BIAS_X))
    leaving.append((bias.at[:, :, 0], BIAS_C))
    msa_src[...] = staged[...].astype(BF16).reshape(32, 16, 128)

    def push_msa(turn, _):
        other = far_first(turn)
        push(msa_src.at[other], msa_in.at[xy], MSA1, device(other, zh, core), rep)
        return 0

    lax.fori_loop(0, 31, push_msa, 0)
    leaving.append((msa_in.at[pl.ds(0, 31)], MSA1))
    msa_in[xy] = msa_src[xy]
    arrived(msa_in.at[pl.ds(0, 31)], MSA1)
    unpacked[...] = msa_in[...].astype(F32).reshape(512, 128)
    for target in range(4):
        parts = [
            jnp.concatenate(
                [unpacked[pl.ds(target * 4 + s * 2 + half, 32, stride=16), :] for half in range(2)], axis=1
            )
            for s in range(2)
        ]
        col_src[target] = jnp.concatenate(parts, axis=0).astype(BF16)
    for step in range(1, 4):
        other = (zc + step) & 3
        push(col_src.at[other], col_in.at[zc], MSA2, device(xy, other >> 1, other & 1), rep)
    leaving.append((col_in.at[pl.ds(0, 3)], MSA2))
    col_in[zc] = col_src[zc]
    arrived(col_in.at[pl.ds(0, 3)], MSA2)

    loaded(7, 8, 9, 10, 11)
    middle = col_in[...].astype(F32).reshape(ROWS, FEAT)
    tokens = layer_norm(middle, g_col[...])
    projected = dot(tokens, w_col[...])
    wide = expand_heads(projected[:, :FEAT] * LOGIT_SCALE)
    col_keys = projected[:, FEAT : 2 * FEAT].astype(BF16)
    col_values = projected[:, 2 * FEAT : 3 * FEAT].astype(BF16)
    col_gates = jax.nn.sigmoid(projected[:, 3 * FEAT :])
    col_logits[...] = dot_nt(wide, col_keys)

    def col_softmax(group, _):
        rows = pl.ds(pl.multiple_of(group * 128, 128), 128)
        raw = col_logits[rows, :]
        top = jnp.max(raw, axis=-1, keepdims=True)
        powers = jnp.exp2(raw - top)
        total = jnp.sum(powers, axis=-1, keepdims=True)
        col_weights[rows, :] = powers.astype(BF16)
        col_denom[rows, :] = jnp.broadcast_to(1.0 / total, (128, 128))
        return 0

    lax.fori_loop(0, 16, col_softmax, 0, unroll=2)
    attended = dot(col_weights[...], col_values)
    merged = merge_heads(attended, col_denom[...][:, :1])
    gated = (merged * col_gates).astype(BF16)
    target_rows = middle + dot(gated, wo_col[...])

    ln_opm = layer_norm(target_rows, g_opm[...])
    factors = dot_nt(w_fac[...], ln_opm)
    right_src[...] = factors[FACTOR:].astype(BF16)
    left_src[...] = (factors[:FACTOR] * (1.0 / ROWS)).astype(BF16)
    push(right_src, right.at[y, zh], RIGHT1, device(mirror, 1 - zh, core), x, recv_r1.at[zh])

    @pl.when(x != rep)
    def _():
        push(right_src, right.at[y, zh], RIGHT1, device(mirror, zh, core), x, recv_r1.at[zh])

    @pl.when(x == rep)
    def _():
        right[y, zh] = right_src[...]

    for step in range(1, 4):
        push(left_src, left.at[x, core, rep], LEFT, dap, (rep + step) & 3)
    leaving.append((None, RIGHT1))
    leaving.append((left.at[0, 0, pl.ds(0, 3)], LEFT))
    left[x, core, rep] = left_src[...]
    for m_ in range(4):
        for s in range(2):
            start = (m_ * 2 + s) * 32
            for half in range(2):
                natural[half, pl.ds(m_ * 2 + s, 32, stride=8), :] = target_rows[
                    start : start + 32, half * 128 : (half + 1) * 128
                ]
    final[rep] = jnp.concatenate([natural[0], natural[1]], axis=1).astype(BF16)
    def right_along_y(zh_):
        for step in (4, 3, 5, 2, 6, 1, 7):
            block = right.at[y, zh_]
            push(block, block, RIGHT_Y, device(x * 8 + ((y + step) & 7), zh, core), rep, recv_ry.at[y])

    @pl.when(x != rep)
    def _():
        landed(right_src, recv_r1.at[zh])

    right_along_y(zh)
    arrived(left.at[0, 0, pl.ds(0, 3)], LEFT)
    for step in (2, 1, 3):
        block = left.at[x, core]
        push(block, block, LEFT_X, device(((x + step) & 3) * 8 + y, zh, core), rep)
    leaving.append((left.at[pl.ds(0, 3), 0], LEFT_X))
    landed(right_src, recv_r1.at[1 - zh])
    right_along_y(1 - zh)
    leaving.append((right.at[pl.ds(0, 7)], RIGHT_Y))
    for step in range(1, 4):
        push(final.at[rep], final.at[rep], FINAL, dap, (rep + step) & 3)
    leaving.append((final.at[pl.ds(0, 3)], FINAL))
    arrived(left.at[pl.ds(0, 3), 0], LEFT_X)
    block = left.at[:, core]
    push(block, block, LEFT_C, device(xy, zh, 1 - core), rep)
    leaving.append((left.at[:, 0], LEFT_C))
    arrived(left.at[:, 0], LEFT_C)

    for half in range(2):
        left_f[half] = left[..., half * 128 : (half + 1) * 128].astype(F32).reshape(32 * FACTOR, 128)
    for channel in range(FACTOR):
        left_t[pl.ds(channel * 32, 32), :] = jnp.concatenate(
            [left_f[half, pl.ds(channel, 32, stride=FACTOR), :] for half in range(2)], axis=1
        ).astype(BF16)
    quarter = lax.broadcasted_iota(jnp.int32, (FACTOR, 128), 1) // 32
    for four in range(4):
        sources = (nearest(2 * four), nearest(2 * four + 1))
        for source in sources if four else sources[1:]:
            landed(right.at[0], recv_ry.at[source])
        operand = jnp.concatenate([right[source].reshape(2 * FACTOR, ROWS) for source in sources], axis=0)
        product = dot_nt(operand, left_t[...])
        for tile in range(8):
            blocks = [
                product[jq * FACTOR : (jq + 1) * FACTOR, tile * 128 : (tile + 1) * 128] for jq in range(4)
            ]
            for cq in range(4):
                moved = [
                    blocks[jq] if jq == cq else pltpu.roll(blocks[jq], (32 * (jq - cq)) % 128, 1) for jq in range(4)
                ]
                joined = jnp.where(
                    quarter < 2,
                    jnp.where(quarter == 0, moved[0], moved[1]),
                    jnp.where(quarter == 2, moved[2], moved[3]),
                )
                outer[pl.ds((tile * 4 + cq) * FACTOR, FACTOR), :] = joined.astype(BF16)
        change = dot(final_t[...], outer[...]).T
        for half, source in enumerate(sources):
            update[pl.ds(pl.multiple_of(source * 64, 64), 64), :] = change[half * 64 : (half + 1) * 64]

    for target in range(8):
        for r_ in range(4):
            result_src[target, r_] = update[pl.ds(target * 4 + r_, 16, stride=32), :].astype(BF16)
    mine = x * 2 + core
    for step in range(1, 8):
        other = (mine + step) & 7
        push(result_src.at[other], result_in.at[mine], RESULT, device((other >> 1) * 8 + y, zh, other & 1), rep)
    leaving.append((result_in.at[pl.ds(0, 7)], RESULT))
    result_in[mine] = result_src[mine]

    arrived(final.at[pl.ds(0, 3)], FINAL)
    for half in range(2):
        for r_ in range(4):
            out_msa[pl.ds(half * 4 + r_, ROWS, stride=8), :] = final[r_, :, half * 128 : (half + 1) * 128].astype(F32)

    arrived(result_in.at[pl.ds(0, 7)], RESULT)
    for source in range(8):
        for a in range(4):
            here = pl.ds(4 * (source % 2) + source // 2, 16, stride=8)
            out_pair[a, here, :] = pair[a, here, :] + result_in[source, a].astype(F32)

    finish()


def hand_over(msa, pair, out_msa, out_pair, done):
    part = ROWS * 2
    copies = [
        pltpu.make_async_copy(msa.at[pl.ds(k * part, part)], out_msa.at[pl.ds(k * part, part)], done.at[k])
        for k in range(4)
    ]
    copies.append(pltpu.make_async_copy(pair, out_pair, done.at[4]))
    for copy in copies:
        copy.start()
    for copy in copies:
        copy.wait()


def shards(
    alignment_source_tensor,
    couple_source_tensor,
    horizontal_scale_factor,
    horizontal_projection_matrix,
    couple_scale_factor,
    couple_offset_matrix,
    horizontal_final_matrix,
    vertical_scale_factor,
    vertical_projection_matrix,
    vertical_final_matrix,
    tensorial_scale_factor,
    tensorial_factor_matrix,
    tensorial_final_matrix,
):
    operands = [
        alignment_source_tensor,
        couple_source_tensor,
        horizontal_scale_factor.reshape(1, FEAT),
        horizontal_projection_matrix,
        couple_scale_factor.reshape(1, CZ),
        couple_offset_matrix.T,
        horizontal_final_matrix,
        vertical_scale_factor.reshape(1, FEAT),
        vertical_projection_matrix,
        vertical_final_matrix,
        tensorial_scale_factor.reshape(1, FEAT),
        tensorial_factor_matrix.T,
        tensorial_final_matrix,
    ]
    vmem = pl.BlockSpec(memory_space=pltpu.VMEM)
    scratch = [pltpu.VMEM(a.shape, a.dtype) for a in operands] + [
        pltpu.VMEM((4, 8, 128), F32),
        pltpu.VMEM((8, 8, 128), F32),
        pltpu.VMEM((4, 8, 2, 16, RES), BF16),
        pltpu.VMEM((2, 2, 2, 64, 128), F32),
        pltpu.VMEM((2, 2, 64, FEAT), F32),
        pltpu.VMEM((2, RES, FEAT), BF16),
        pltpu.VMEM((2, RES, FEAT), BF16),
        pltpu.VMEM((2, 2, 4, 8, 16, RES), F32),
        pltpu.VMEM((2, 2, 4, 8, 16, RES), BF16),
        pltpu.VMEM((2, 2, 4, 8, 16, 128), F32),
        pltpu.VMEM((512, 128), F32),
        pltpu.VMEM((32, 16, 128), BF16),
        pltpu.VMEM((32, 16, 128), BF16),
        pltpu.VMEM((512, 128), F32),
        pltpu.VMEM((4, 64, FEAT), BF16),
        pltpu.VMEM((4, 64, FEAT), BF16),
        pltpu.VMEM((ROWS * HEADS, ROWS), F32),
        pltpu.VMEM((ROWS * HEADS, ROWS), BF16),
        pltpu.VMEM((ROWS * HEADS, 128), F32),
        pltpu.VMEM((2, ROWS, 128), F32),
        pltpu.VMEM((4, ROWS, FEAT), BF16),
        pltpu.VMEM((FACTOR, ROWS), BF16),
        pltpu.VMEM((4, 2, 4, FACTOR, ROWS), BF16),
        pltpu.VMEM((FACTOR, ROWS), BF16),
        pltpu.VMEM((8, 2, FACTOR, ROWS), BF16),
        pltpu.VMEM((2, 32 * FACTOR, 128), F32),
        pltpu.VMEM((32 * FACTOR, ROWS), BF16),
        pltpu.VMEM((CZ, FACTOR * FACTOR), BF16),
        pltpu.VMEM((FACTOR * FACTOR, 128), BF16),
        pltpu.VMEM((512, CZ), F32),
        pltpu.VMEM((8, 4, 16, CZ), BF16),
        pltpu.VMEM((8, 4, 16, CZ), BF16),
        pltpu.VMEM((2, 2, RES, 128), F32),
        pltpu.SemaphoreType.DMA((PHASES,)),
        pltpu.SemaphoreType.DMA((PHASES,)),
        pltpu.SemaphoreType.DMA((len(operands),)),
        pltpu.SemaphoreType.DMA((8,)),
        pltpu.SemaphoreType.DMA((32,)),
        pltpu.SemaphoreType.DMA((8,)),
        pltpu.SemaphoreType.DMA((2,)),
        pltpu.SemaphoreType.DMA((8,)),
    ]
    out_msa, out_pair = pl.pallas_call(
        kernel,
        out_shape=(
            jax.ShapeDtypeStruct((ROWS * 8, 128), F32),
            jax.ShapeDtypeStruct((4, 128, CZ), F32),
        ),
        in_specs=[pl.BlockSpec(memory_space=pltpu.HBM)] * len(operands),
        out_specs=(vmem, vmem),
        scratch_shapes=scratch,
        compiler_params=pltpu.CompilerParams(
            collective_id=0, has_side_effects=True, vmem_limit_bytes=60 * 1024 * 1024
        ),
    )(*operands)
    anywhere = pl.BlockSpec(memory_space=pl.ANY)
    out_msa, out_pair = pl.pallas_call(
        hand_over,
        out_shape=(
            jax.ShapeDtypeStruct((ROWS * 8, 128), F32),
            jax.ShapeDtypeStruct((4, 128, CZ), F32),
        ),
        in_specs=[anywhere] * 2,
        out_specs=(anywhere, anywhere),
        scratch_shapes=[pltpu.SemaphoreType.DMA((5,))],
        compiler_params=pltpu.CompilerParams(vmem_limit_bytes=60 * 1024 * 1024),
    )(out_msa, out_pair)
    return jnp.swapaxes(out_msa.reshape(ROWS, 2, 4, 128), 1, 2).reshape(ROWS, 4, FEAT), out_pair


def solution(mesh):
    return jax.shard_map(
        shards,
        mesh=mesh,
        in_specs=(P("dap", None, None), P("dap", "rep", None)) + (P(),) * 11,
        out_specs=(P(None, "dap", None), P("dap", "rep", None)),
        check_vma=False,
    )
```

```python
import math

import jax
import jax.numpy as jnp
from jax import lax
from jax.experimental import pallas as pl
from jax.experimental.pallas import tpu as pltpu
from jax.sharding import PartitionSpec as P

HEADS = 8
HEAD_DIM = 32
FEAT = HEADS * HEAD_DIM
CZ = 128
ROWS = 256
RES = 512
FACTOR = 32
LOG2E = math.log2(math.e)
LOGIT_SCALE = HEAD_DIM ** (-0.5) * LOG2E
MESH = pl.DeviceIdType.MESH
F32 = jnp.float32
BF16 = jnp.bfloat16

BIAS1, BIAS_Y, BIAS_X, BIAS_C, MSA1, MSA2, LEFT, LEFT_X, LEFT_C, FINAL, RIGHT1, RIGHT_Y, RESULT = range(13)
PHASES = 13


def layer_norm(values, gain):
    average = jnp.mean(values, axis=-1, keepdims=True)
    centred = values - average
    variance = jnp.mean(centred * centred, axis=-1, keepdims=True)
    return (centred * lax.rsqrt(variance + 1e-05) * gain).astype(BF16)


def dot(a, b):
    return lax.dot_general(a, b, (((1,), (0,)), ((), ())), preferred_element_type=F32)


def dot_nt(a, b):
    return lax.dot_general(a, b, (((1,), (1,)), ((), ())), preferred_element_type=F32)


def head_mask():
    head = lax.broadcasted_iota(jnp.int32, (HEADS, FEAT), 0)
    channel = lax.broadcasted_iota(jnp.int32, (HEADS, FEAT), 1) // HEAD_DIM
    return (head == channel).astype(F32)


def expand_heads(queries):
    n = queries.shape[0]
    spread = jnp.broadcast_to(queries[:, None, :], (n, HEADS, FEAT))
    return (spread * head_mask()[None]).reshape(n * HEADS, FEAT).astype(BF16)


def merge_heads(attended, inverse):
    n = attended.shape[0] // HEADS
    scaled = (attended * inverse).reshape(n, HEADS, FEAT) * head_mask()[None]
    return jnp.sum(scaled, axis=1)


def kernel(*refs):
    given, (out_msa, out_pair), held, rest = refs[:13], refs[13:15], refs[15:28], refs[28:]
    msa, pair, g_row, w_row, g_pair, w_bias, wo_row, g_col, w_col, wo_col, g_opm, w_fac, w_fin = held
    (
        bias_src, bias_in, bias, queries, gates, keys, values, logits, weights, denom, staged, msa_src, msa_in,
        unpacked, col_src, col_in, col_logits, col_weights, col_denom, natural, final, left_src, left, right_src, right,
        left_f, left_t, final_t, outer, update, result_src, result_in, msa_halves,
        send, recv, load, recv_by, recv_bx, recv_bc, recv_r1, recv_ry, recv_lx, recv_lc,
    ) = rest
    loads = [pltpu.make_async_copy(given[k], held[k], load.at[k]) for k in range(13)]
    for k in (1, 5, 4):
        loads[k].start()

    def loaded(*which):
        for k in which:
            loads[k].wait()

    dap = lax.axis_index("dap")
    rep = lax.axis_index("rep")
    x = dap >> 5
    y = (dap >> 2) & 7
    xy = dap >> 2
    zc = dap & 3
    zh = zc >> 1
    core = zc & 1

    def device(xy_, zh_, core_):
        return xy_ * 4 + zh_ * 2 + core_

    barrier = pltpu.get_barrier_semaphore()

    def greet(dap_, rep_):
        pl.semaphore_signal(barrier, inc=1, device_id=(dap_, rep_), device_id_type=MESH)

    def far_first(turn):
        return (xy + turn + jnp.where(turn < 20, 12, -19)) & 31

    def greet_xy(turn, _):
        greet(device(far_first(turn), zh, core), rep)
        return 0

    mirror = rep * 8 + y
    greet(device(mirror, 1 - zh, core), x)

    @pl.when(x != rep)
    def _():
        greet(device(mirror, zh, core), x)

    lax.fori_loop(0, 31, greet_xy, 0)
    for step in (4, 3, 5, 2, 6, 1, 7):
        other = (zh * 4 + rep + step) & 7
        greet(device(xy, other >> 2, core), other & 3)
    for step in range(4):
        greet(device(((x + step) & 3) * 8 + y, zh, 1 - core), rep)
    greet(device(xy, 1 - zh, 1 - core), rep)
    for k in (0, 2, 3, 6, 12, 7, 8, 9, 10, 11):
        loads[k].start()

    def push(src, dst, phase, dap_, rep_, into=None):
        pltpu.make_async_remote_copy(
            src_ref=src, dst_ref=dst, send_sem=send.at[phase], recv_sem=recv.at[phase] if into is None else into,
            device_id=(dap_, rep_), device_id_type=MESH,
        ).start()

    def arrived(shaped, phase):
        landed(shaped, recv.at[phase])

    def landed(shaped, sem):
        pltpu.make_async_copy(shaped, shaped, sem).wait()

    def drained(shaped, phase):
        pltpu.make_async_copy(shaped, shaped, send.at[phase]).wait()

    leaving = []

    def finish():
        for shaped, phase in leaving:
            if shaped is not None:
                drained(shaped, phase)
                continue

            @pl.when(x != rep)
            def _():
                drained(right.at[0], RIGHT1)

            @pl.when(x == rep)
            def _():
                drained(right_src, RIGHT1)

    def bias_along_x(y_):
        block = bias.at[x, y_, core]
        for step in range(1, 4):
            push(block, block, BIAS_X, device(((x + step) & 3) * 8 + y, zh, core), rep, recv_bx.at[x * 8 + y_])

    def bias_to_core(y_):
        block = bias.at[:, y_, core]
        push(block, block, BIAS_C, device(xy, zh, 1 - core), rep, recv_bc.at[y_])

    loaded(1, 4, 5)
    ln_pair = layer_norm(pair[...].reshape(4 * 128, CZ), g_pair[...])
    head_bias = dot_nt(w_bias[...], ln_pair) * LOG2E
    for a in range(4):
        bias_src[a] = head_bias[:, a * 128 : (a + 1) * 128]

    pl.semaphore_wait(barrier, 44 + jnp.where(x != rep, 1, 0))

    for step in (4, 3, 5, 2, 6, 1, 7):
        other = (zh * 4 + rep + step) & 7
        push(bias_src.at[other & 3], bias_in.at[zh * 4 + rep], BIAS1, device(xy, other >> 2, core), other & 3)
    leaving.append((bias_in.at[pl.ds(0, 7)], BIAS1))
    bias_in[zh * 4 + rep] = bias_src[rep]

    loaded(0, 2, 3)
    for s in range(2):
        tokens = layer_norm(msa[s], g_row[...])
        projected = dot(tokens, w_row[:, FEAT : 3 * FEAT]).astype(BF16)
        keys[s] = projected[:, :FEAT]
        values[s] = projected[:, FEAT:]
        for half in range(2):
            msa_halves[s, half] = msa[s, :, half * 128 : (half + 1) * 128]
            for h_ in range(2):
                for c_ in range(2):
                    queries[s, c_, half, pl.ds(h_, 32, stride=2), :] = msa_halves[
                        s, half, pl.ds(8 * h_ + 4 * c_ + rep, 32, stride=16), :
                    ]

    arrived(bias_in.at[pl.ds(0, 7)], BIAS1)
    block = jnp.concatenate(
        [jnp.concatenate([bias_in[h_ * 4 + r_] for r_ in range(4)], axis=1) for h_ in range(2)], axis=0
    )
    bias[x, y, core] = block.astype(BF16)
    for step in (4, 3, 5, 2, 6, 1, 7):
        block = bias.at[x, y, core]
        push(block, block, BIAS_Y, device(x * 8 + ((y + step) & 7), zh, core), rep, recv_by.at[y])
    bias_along_x(y)

    def row_logits(s):
        halves = [jnp.concatenate([queries[s, 0, half], queries[s, 1, half]], axis=0) for half in range(2)]
        tokens = layer_norm(jnp.concatenate(halves, axis=1), g_row[...])
        wide = dot(tokens, w_row[:, :FEAT]) * LOGIT_SCALE
        gates[s] = jax.nn.sigmoid(dot(tokens, w_row[:, 3 * FEAT :])).reshape(2, 64, FEAT)
        logits[s] = dot_nt(expand_heads(wide), keys[s]).reshape(2, 4, 8, 16, RES)

    def nearest(turn):
        away = (turn + 1) >> 1
        return (y + jnp.where((turn & 1) == 1, away, 8 - away)) & 7

    def row_softmax(y_, which):
        offset = bias[:, y_, which].astype(F32).reshape(64, RES)
        for s in range(2):
            raw = logits[s, which, :, y_].reshape(64, RES) + offset
            top = jnp.max(raw, axis=-1, keepdims=True)
            powers = jnp.exp2(raw - top)
            total = jnp.sum(powers, axis=-1, keepdims=True)
            weights[s, which, :, y_] = powers.astype(BF16).reshape(4, 16, RES)
            denom[s, which, :, y_] = jnp.broadcast_to(1.0 / total, (64, 128)).reshape(4, 16, 128)

    def row_finish(which):
        for s in range(2):
            attended = dot(weights[s, which].reshape(512, RES), values[s])
            merged = merge_heads(attended, denom[s, which].reshape(512, 128)[:, :1])
            gated = (merged * gates[s, which]).astype(BF16)
            change = dot(gated, wo_row[...])
            for half in range(2):
                staged[pl.ds(which * 4 + s * 2 + half, 64, stride=8), :] = (
                    queries[s, which, half] + change[:, half * 128 : (half + 1) * 128]
                )

    row_logits(0)
    for step in (1, 7, 2, 6, 3, 5, 4):
        source = (y + step) & 7
        landed(bias.at[0, 0, 0], recv_by.at[source])
        bias_along_x(source)
    row_logits(1)
    loaded(12)
    final_t[...] = w_fin[...].astype(F32).T.astype(BF16)

    def own_arrived(turn):
        source = nearest(turn)
        for other in range(1, 4):
            landed(bias.at[0, 0, 0], recv_bx.at[((x + other) & 3) * 8 + source])
        bias_to_core(source)
        return source

    def other_arrived(turn):
        source = nearest(turn)
        landed(bias.at[:, 0, 0], recv_bc.at[source])
        return source

    def both_queries(turn, _):
        mine_, theirs = own_arrived(turn), other_arrived(turn - 1)
        row_softmax(mine_, core)
        row_softmax(theirs, 1 - core)
        return 0

    loaded(6)
    row_softmax(own_arrived(0), core)
    lax.fori_loop(1, 8, both_queries, 0)
    row_softmax(other_arrived(7), 1 - core)
    row_finish(core)
    row_finish(1 - core)
    leaving.append((bias.at[0, pl.ds(0, 7), 0], BIAS_Y))
    leaving.append((bias.at[pl.ds(0, 3), :, 0], BIAS_X))
    leaving.append((bias.at[:, :, 0], BIAS_C))
    msa_src[...] = staged[...].astype(BF16).reshape(32, 16, 128)

    def push_msa(turn, _):
        other = far_first(turn)
        push(msa_src.at[other], msa_in.at[xy], MSA1, device(other, zh, core), rep)
        return 0

    lax.fori_loop(0, 31, push_msa, 0)
    leaving.append((msa_in.at[pl.ds(0, 31)], MSA1))
    msa_in[xy] = msa_src[xy]
    arrived(msa_in.at[pl.ds(0, 31)], MSA1)
    unpacked[...] = msa_in[...].astype(F32).reshape(512, 128)
    for target in range(4):
        parts = [
            jnp.concatenate(
                [unpacked[pl.ds(target * 4 + s * 2 + half, 32, stride=16), :] for half in range(2)], axis=1
            )
            for s in range(2)
        ]
        col_src[target] = jnp.concatenate(parts, axis=0).astype(BF16)
    for step in range(1, 4):
        other = (zc + step) & 3
        push(col_src.at[other], col_in.at[zc], MSA2, device(xy, other >> 1, other & 1), rep)
    leaving.append((col_in.at[pl.ds(0, 3)], MSA2))
    col_in[zc] = col_src[zc]
    arrived(col_in.at[pl.ds(0, 3)], MSA2)

    loaded(7, 8, 9, 10, 11)
    middle = col_in[...].astype(F32).reshape(ROWS, FEAT)
    tokens = layer_norm(middle, g_col[...])
    projected = dot(tokens, w_col[...])
    wide = expand_heads(projected[:, :FEAT] * LOGIT_SCALE)
    col_keys = projected[:, FEAT : 2 * FEAT].astype(BF16)
    col_values = projected[:, 2 * FEAT : 3 * FEAT].astype(BF16)
    col_gates = jax.nn.sigmoid(projected[:, 3 * FEAT :])
    col_logits[...] = dot_nt(wide, col_keys)

    def col_softmax(group, _):
        rows = pl.ds(pl.multiple_of(group * 128, 128), 128)
        raw = col_logits[rows, :]
        top = jnp.max(raw, axis=-1, keepdims=True)
        powers = jnp.exp2(raw - top)
        total = jnp.sum(powers, axis=-1, keepdims=True)
        col_weights[rows, :] = powers.astype(BF16)
        col_denom[rows, :] = jnp.broadcast_to(1.0 / total, (128, 128))
        return 0

    lax.fori_loop(0, 16, col_softmax, 0, unroll=2)
    attended = dot(col_weights[...], col_values)
    merged = merge_heads(attended, col_denom[...][:, :1])
    gated = (merged * col_gates).astype(BF16)
    target_rows = middle + dot(gated, wo_col[...])

    ln_opm = layer_norm(target_rows, g_opm[...])
    factors = dot_nt(w_fac[...], ln_opm)
    right_src[...] = factors[FACTOR:].astype(BF16)
    left_src[...] = (factors[:FACTOR] * (1.0 / ROWS)).astype(BF16)
    push(right_src, right.at[y, zh], RIGHT1, device(mirror, 1 - zh, core), x, recv_r1.at[zh])

    @pl.when(x != rep)
    def _():
        push(right_src, right.at[y, zh], RIGHT1, device(mirror, zh, core), x, recv_r1.at[zh])

    @pl.when(x == rep)
    def _():
        right[y, zh] = right_src[...]

    for step in range(1, 4):
        push(left_src, left.at[x, core, rep], LEFT, dap, (rep + step) & 3)
    leaving.append((None, RIGHT1))
    leaving.append((left.at[0, 0, pl.ds(0, 3)], LEFT))
    left[x, core, rep] = left_src[...]
    for m_ in range(4):
        for s in range(2):
            start = (m_ * 2 + s) * 32
            for half in range(2):
                natural[half, pl.ds(m_ * 2 + s, 32, stride=8), :] = target_rows[
                    start : start + 32, half * 128 : (half + 1) * 128
                ]
    final[rep] = jnp.concatenate([natural[0], natural[1]], axis=1).astype(BF16)
    def right_along_y(zh_):
        for step in (4, 3, 5, 2, 6, 1, 7):
            block = right.at[y, zh_]
            push(block, block, RIGHT_Y, device(x * 8 + ((y + step) & 7), zh, core), rep, recv_ry.at[y])

    def left_to_core(x_):
        block = left.at[x_, core]
        push(block, block, LEFT_C, device(xy, zh, 1 - core), rep, recv_lc.at[x_])

    def left_unpack(x_, core_):
        rows = pl.ds(pl.multiple_of((x_ * 2 + core_) * 128, 128), 128)
        block = left[x_, core_].astype(F32).reshape(128, ROWS)
        for half in range(2):
            left_f[half, rows, :] = block[:, half * 128 : (half + 1) * 128]

    arrived(left.at[0, 0, pl.ds(0, 3)], LEFT)
    for step in (2, 1, 3):
        block = left.at[x, core]
        push(block, block, LEFT_X, device(((x + step) & 3) * 8 + y, zh, core), rep, recv_lx.at[x])
    left_to_core(x)

    @pl.when(x != rep)
    def _():
        landed(right_src, recv_r1.at[zh])

    right_along_y(zh)
    landed(right_src, recv_r1.at[1 - zh])
    right_along_y(1 - zh)
    leaving.append((right.at[pl.ds(0, 7)], RIGHT_Y))
    for step in range(1, 4):
        push(final.at[rep], final.at[rep], FINAL, dap, (rep + step) & 3)
    leaving.append((final.at[pl.ds(0, 3)], FINAL))
    left_unpack(x, core)
    for step in (1, 3, 2):
        source = (x + step) & 3
        landed(left.at[0, 0], recv_lx.at[source])
        left_to_core(source)
        left_unpack(source, core)
    leaving.append((left.at[pl.ds(0, 3), 0], LEFT_X))
    leaving.append((left.at[:, 0], LEFT_C))
    for step in (0, 1, 3, 2):
        source = (x + step) & 3
        landed(left.at[0, 0], recv_lc.at[source])
        left_unpack(source, 1 - core)

    for channel in range(FACTOR):
        left_t[pl.ds(channel * 32, 32), :] = jnp.concatenate(
            [left_f[half, pl.ds(channel, 32, stride=FACTOR), :] for half in range(2)], axis=1
        ).astype(BF16)
    quarter = lax.broadcasted_iota(jnp.int32, (FACTOR, 128), 1) // 32
    for four in range(4):
        sources = (nearest(2 * four), nearest(2 * four + 1))
        for source in sources if four else sources[1:]:
            landed(right.at[0], recv_ry.at[source])
        operand = jnp.concatenate([right[source].reshape(2 * FACTOR, ROWS) for source in sources], axis=0)
        product = dot_nt(operand, left_t[...])
        for tile in range(8):
            blocks = [
                product[jq * FACTOR : (jq + 1) * FACTOR, tile * 128 : (tile + 1) * 128] for jq in range(4)
            ]
            for cq in range(4):
                moved = [
                    blocks[jq] if jq == cq else pltpu.roll(blocks[jq], (32 * (jq - cq)) % 128, 1) for jq in range(4)
                ]
                joined = jnp.where(
                    quarter < 2,
                    jnp.where(quarter == 0, moved[0], moved[1]),
                    jnp.where(quarter == 2, moved[2], moved[3]),
                )
                outer[pl.ds((tile * 4 + cq) * FACTOR, FACTOR), :] = joined.astype(BF16)
        change = dot(final_t[...], outer[...]).T
        for half, source in enumerate(sources):
            update[pl.ds(pl.multiple_of(source * 64, 64), 64), :] = change[half * 64 : (half + 1) * 64]

    for target in range(8):
        for r_ in range(4):
            result_src[target, r_] = update[pl.ds(target * 4 + r_, 16, stride=32), :].astype(BF16)
    mine = x * 2 + core
    for step in range(1, 8):
        other = (mine + step) & 7
        push(result_src.at[other], result_in.at[mine], RESULT, device((other >> 1) * 8 + y, zh, other & 1), rep)
    leaving.append((result_in.at[pl.ds(0, 7)], RESULT))
    result_in[mine] = result_src[mine]

    arrived(final.at[pl.ds(0, 3)], FINAL)
    for half in range(2):
        for r_ in range(4):
            out_msa[pl.ds(half * 4 + r_, ROWS, stride=8), :] = final[r_, :, half * 128 : (half + 1) * 128].astype(F32)

    arrived(result_in.at[pl.ds(0, 7)], RESULT)
    for source in range(8):
        for a in range(4):
            here = pl.ds(4 * (source % 2) + source // 2, 16, stride=8)
            out_pair[a, here, :] = pair[a, here, :] + result_in[source, a].astype(F32)

    finish()


def shards(
    alignment_source_tensor,
    couple_source_tensor,
    horizontal_scale_factor,
    horizontal_projection_matrix,
    couple_scale_factor,
    couple_offset_matrix,
    horizontal_final_matrix,
    vertical_scale_factor,
    vertical_projection_matrix,
    vertical_final_matrix,
    tensorial_scale_factor,
    tensorial_factor_matrix,
    tensorial_final_matrix,
):
    operands = [
        alignment_source_tensor,
        couple_source_tensor,
        horizontal_scale_factor.reshape(1, FEAT),
        horizontal_projection_matrix,
        couple_scale_factor.reshape(1, CZ),
        couple_offset_matrix.T,
        horizontal_final_matrix,
        vertical_scale_factor.reshape(1, FEAT),
        vertical_projection_matrix,
        vertical_final_matrix,
        tensorial_scale_factor.reshape(1, FEAT),
        tensorial_factor_matrix.T,
        tensorial_final_matrix,
    ]
    vmem = pl.BlockSpec(memory_space=pltpu.VMEM)
    scratch = [pltpu.VMEM(a.shape, a.dtype) for a in operands] + [
        pltpu.VMEM((4, 8, 128), F32),
        pltpu.VMEM((8, 8, 128), F32),
        pltpu.VMEM((4, 8, 2, 16, RES), BF16),
        pltpu.VMEM((2, 2, 2, 64, 128), F32),
        pltpu.VMEM((2, 2, 64, FEAT), F32),
        pltpu.VMEM((2, RES, FEAT), BF16),
        pltpu.VMEM((2, RES, FEAT), BF16),
        pltpu.VMEM((2, 2, 4, 8, 16, RES), F32),
        pltpu.VMEM((2, 2, 4, 8, 16, RES), BF16),
        pltpu.VMEM((2, 2, 4, 8, 16, 128), F32),
        pltpu.VMEM((512, 128), F32),
        pltpu.VMEM((32, 16, 128), BF16),
        pltpu.VMEM((32, 16, 128), BF16),
        pltpu.VMEM((512, 128), F32),
        pltpu.VMEM((4, 64, FEAT), BF16),
        pltpu.VMEM((4, 64, FEAT), BF16),
        pltpu.VMEM((ROWS * HEADS, ROWS), F32),
        pltpu.VMEM((ROWS * HEADS, ROWS), BF16),
        pltpu.VMEM((ROWS * HEADS, 128), F32),
        pltpu.VMEM((2, ROWS, 128), F32),
        pltpu.VMEM((4, ROWS, FEAT), BF16),
        pltpu.VMEM((FACTOR, ROWS), BF16),
        pltpu.VMEM((4, 2, 4, FACTOR, ROWS), BF16),
        pltpu.VMEM((FACTOR, ROWS), BF16),
        pltpu.VMEM((8, 2, FACTOR, ROWS), BF16),
        pltpu.VMEM((2, 32 * FACTOR, 128), F32),
        pltpu.VMEM((32 * FACTOR, ROWS), BF16),
        pltpu.VMEM((CZ, FACTOR * FACTOR), BF16),
        pltpu.VMEM((FACTOR * FACTOR, 128), BF16),
        pltpu.VMEM((512, CZ), F32),
        pltpu.VMEM((8, 4, 16, CZ), BF16),
        pltpu.VMEM((8, 4, 16, CZ), BF16),
        pltpu.VMEM((2, 2, RES, 128), F32),
        pltpu.SemaphoreType.DMA((PHASES,)),
        pltpu.SemaphoreType.DMA((PHASES,)),
        pltpu.SemaphoreType.DMA((len(operands),)),
        pltpu.SemaphoreType.DMA((8,)),
        pltpu.SemaphoreType.DMA((32,)),
        pltpu.SemaphoreType.DMA((8,)),
        pltpu.SemaphoreType.DMA((2,)),
        pltpu.SemaphoreType.DMA((8,)),
        pltpu.SemaphoreType.DMA((4,)),
        pltpu.SemaphoreType.DMA((4,)),
    ]
    out_msa, out_pair = pl.pallas_call(
        kernel,
        out_shape=(
            jax.ShapeDtypeStruct((ROWS * 8, 128), F32),
            jax.ShapeDtypeStruct((4, 128, CZ), F32),
        ),
        in_specs=[pl.BlockSpec(memory_space=pltpu.HBM)] * len(operands),
        out_specs=(vmem, vmem),
        scratch_shapes=scratch,
        compiler_params=pltpu.CompilerParams(
            collective_id=0, has_side_effects=True, vmem_limit_bytes=44 * 1024 * 1024
        ),
    )(*[pltpu.with_memory_space_constraint(a, pltpu.HBM) for a in operands])
    return jnp.swapaxes(out_msa.reshape(ROWS, 2, 4, 128), 1, 2).reshape(ROWS, 4, FEAT), out_pair


def solution(mesh):
    return jax.shard_map(
        shards,
        mesh=mesh,
        in_specs=(P("dap", None, None), P("dap", "rep", None)) + (P(),) * 11,
        out_specs=(P(None, "dap", None), P("dap", "rep", None)),
        check_vma=False,
    )
```

```python
import math

import jax
import jax.numpy as jnp
from jax import lax
from jax.experimental import pallas as pl
from jax.experimental.pallas import tpu as pltpu
from jax.sharding import PartitionSpec as P

HEADS = 8
HEAD_DIM = 32
FEAT = HEADS * HEAD_DIM
CZ = 128
ROWS = 256
RES = 512
FACTOR = 32
LOG2E = math.log2(math.e)
LOGIT_SCALE = HEAD_DIM ** (-0.5) * LOG2E
MESH = pl.DeviceIdType.MESH
F32 = jnp.float32
BF16 = jnp.bfloat16

BIAS1, BIAS_Y, BIAS_X, BIAS_C, MSA1, MSA2, LEFT, LEFT_X, LEFT_C, FINAL, RIGHT1, RIGHT_Y, RESULT = range(13)
PHASES = 13


def layer_norm(values, gain):
    average = jnp.mean(values, axis=-1, keepdims=True)
    centred = values - average
    variance = jnp.mean(centred * centred, axis=-1, keepdims=True)
    return (centred * lax.rsqrt(variance + 1e-05) * gain).astype(BF16)


def dot(a, b):
    return lax.dot_general(a, b, (((1,), (0,)), ((), ())), preferred_element_type=F32)


def dot_nt(a, b):
    return lax.dot_general(a, b, (((1,), (1,)), ((), ())), preferred_element_type=F32)


def head_mask():
    head = lax.broadcasted_iota(jnp.int32, (HEADS, FEAT), 0)
    channel = lax.broadcasted_iota(jnp.int32, (HEADS, FEAT), 1) // HEAD_DIM
    return (head == channel).astype(F32)


def expand_heads(queries):
    n = queries.shape[0]
    spread = jnp.broadcast_to(queries[:, None, :], (n, HEADS, FEAT))
    return (spread * head_mask()[None]).reshape(n * HEADS, FEAT).astype(BF16)


def merge_heads(attended, inverse):
    n = attended.shape[0] // HEADS
    scaled = (attended * inverse).reshape(n, HEADS, FEAT) * head_mask()[None]
    return jnp.sum(scaled, axis=1)


def kernel(*refs):
    given, (out_msa, out_pair), held, rest = refs[:13], refs[13:15], refs[15:28], refs[28:]
    msa, pair, g_row, w_row, g_pair, w_bias, wo_row, g_col, w_col, wo_col, g_opm, w_fac, w_fin = held
    (
        bias_src, bias_in, bias, queries, gates, keys, values, logits, weights, denom, staged, msa_src, msa_in,
        unpacked, col_src, col_in, col_logits, col_weights, col_denom, natural, final, left_src, left, right_src, right,
        left_f, left_t, final_t, outer, update, result_src, result_in, msa_halves,
        send, recv, load, recv_by, recv_bx, recv_bc, recv_r1, recv_ry, recv_lx, recv_lc, recv_m1,
    ) = rest
    loads = [pltpu.make_async_copy(given[k], held[k], load.at[k]) for k in range(13)]
    for k in (1, 5, 4):
        loads[k].start()

    def loaded(*which):
        for k in which:
            loads[k].wait()

    dap = lax.axis_index("dap")
    rep = lax.axis_index("rep")
    x = dap >> 5
    y = (dap >> 2) & 7
    xy = dap >> 2
    zc = dap & 3
    zh = zc >> 1
    core = zc & 1

    def device(xy_, zh_, core_):
        return xy_ * 4 + zh_ * 2 + core_

    barrier = pltpu.get_barrier_semaphore()

    def greet(dap_, rep_):
        pl.semaphore_signal(barrier, inc=1, device_id=(dap_, rep_), device_id_type=MESH)

    def far_first(turn):
        return (xy + turn + jnp.where(turn < 20, 12, -19)) & 31

    def greet_xy(turn, _):
        greet(device(far_first(turn), zh, core), rep)
        return 0

    mirror = rep * 8 + y
    greet(device(mirror, 1 - zh, core), x)

    @pl.when(x != rep)
    def _():
        greet(device(mirror, zh, core), x)

    lax.fori_loop(0, 31, greet_xy, 0)
    for step in (4, 3, 5, 2, 6, 1, 7):
        other = (zh * 4 + rep + step) & 7
        greet(device(xy, other >> 2, core), other & 3)
    for step in range(4):
        greet(device(((x + step) & 3) * 8 + y, zh, 1 - core), rep)
    greet(device(xy, 1 - zh, 1 - core), rep)
    for k in (0, 2, 3, 6, 12, 7, 8, 9, 10, 11):
        loads[k].start()

    def push(src, dst, phase, dap_, rep_, into=None):
        pltpu.make_async_remote_copy(
            src_ref=src, dst_ref=dst, send_sem=send.at[phase], recv_sem=recv.at[phase] if into is None else into,
            device_id=(dap_, rep_), device_id_type=MESH,
        ).start()

    def arrived(shaped, phase):
        landed(shaped, recv.at[phase])

    def landed(shaped, sem):
        pltpu.make_async_copy(shaped, shaped, sem).wait()

    def drained(shaped, phase):
        pltpu.make_async_copy(shaped, shaped, send.at[phase]).wait()

    leaving = []

    def finish():
        for shaped, phase in leaving:
            if shaped is not None:
                drained(shaped, phase)
                continue

            @pl.when(x != rep)
            def _():
                drained(right.at[0], RIGHT1)

            @pl.when(x == rep)
            def _():
                drained(right_src, RIGHT1)

    def bias_along_x(y_):
        block = bias.at[x, y_, core]
        for step in range(1, 4):
            push(block, block, BIAS_X, device(((x + step) & 3) * 8 + y, zh, core), rep, recv_bx.at[x * 8 + y_])

    def bias_to_core(y_):
        block = bias.at[:, y_, core]
        push(block, block, BIAS_C, device(xy, zh, 1 - core), rep, recv_bc.at[y_])

    loaded(1, 4, 5)
    ln_pair = layer_norm(pair[...].reshape(4 * 128, CZ), g_pair[...])
    head_bias = dot_nt(w_bias[...], ln_pair) * LOG2E
    for a in range(4):
        bias_src[a] = head_bias[:, a * 128 : (a + 1) * 128]

    pl.semaphore_wait(barrier, 44 + jnp.where(x != rep, 1, 0))

    for step in (4, 3, 5, 2, 6, 1, 7):
        other = (zh * 4 + rep + step) & 7
        push(bias_src.at[other & 3], bias_in.at[zh * 4 + rep], BIAS1, device(xy, other >> 2, core), other & 3)
    leaving.append((bias_in.at[pl.ds(0, 7)], BIAS1))
    bias_in[zh * 4 + rep] = bias_src[rep]

    loaded(0, 2, 3)
    for s in range(2):
        tokens = layer_norm(msa[s], g_row[...])
        projected = dot(tokens, w_row[:, FEAT : 3 * FEAT]).astype(BF16)
        keys[s] = projected[:, :FEAT]
        values[s] = projected[:, FEAT:]
        for half in range(2):
            msa_halves[s, half] = msa[s, :, half * 128 : (half + 1) * 128]
            for h_ in range(2):
                for c_ in range(2):
                    queries[s, c_, half, pl.ds(h_, 32, stride=2), :] = msa_halves[
                        s, half, pl.ds(8 * h_ + 4 * c_ + rep, 32, stride=16), :
                    ]

    arrived(bias_in.at[pl.ds(0, 7)], BIAS1)
    block = jnp.concatenate(
        [jnp.concatenate([bias_in[h_ * 4 + r_] for r_ in range(4)], axis=1) for h_ in range(2)], axis=0
    )
    bias[x, y, core] = block.astype(BF16)
    for step in (4, 3, 5, 2, 6, 1, 7):
        block = bias.at[x, y, core]
        push(block, block, BIAS_Y, device(x * 8 + ((y + step) & 7), zh, core), rep, recv_by.at[y])
    bias_along_x(y)

    def row_logits(s):
        halves = [jnp.concatenate([queries[s, 0, half], queries[s, 1, half]], axis=0) for half in range(2)]
        tokens = layer_norm(jnp.concatenate(halves, axis=1), g_row[...])
        wide = dot(tokens, w_row[:, :FEAT]) * LOGIT_SCALE
        gates[s] = jax.nn.sigmoid(dot(tokens, w_row[:, 3 * FEAT :])).reshape(2, 64, FEAT)
        logits[s] = dot_nt(expand_heads(wide), keys[s]).reshape(2, 4, 8, 16, RES)

    def nearest(turn):
        away = (turn + 1) >> 1
        return (y + jnp.where((turn & 1) == 1, away, 8 - away)) & 7

    def row_softmax(y_, which):
        offset = bias[:, y_, which].astype(F32).reshape(64, RES)
        for s in range(2):
            raw = logits[s, which, :, y_].reshape(64, RES) + offset
            top = jnp.max(raw, axis=-1, keepdims=True)
            powers = jnp.exp2(raw - top)
            total = jnp.sum(powers, axis=-1, keepdims=True)
            weights[s, which, :, y_] = powers.astype(BF16).reshape(4, 16, RES)
            denom[s, which, :, y_] = jnp.broadcast_to(1.0 / total, (64, 128)).reshape(4, 16, 128)

    def row_finish(which):
        for s in range(2):
            attended = dot(weights[s, which].reshape(512, RES), values[s])
            merged = merge_heads(attended, denom[s, which].reshape(512, 128)[:, :1])
            gated = (merged * gates[s, which]).astype(BF16)
            change = dot(gated, wo_row[...])
            for half in range(2):
                staged[pl.ds(which * 4 + s * 2 + half, 64, stride=8), :] = (
                    queries[s, which, half] + change[:, half * 128 : (half + 1) * 128]
                )

    row_logits(0)
    for step in (1, 7, 2, 6, 3, 5, 4):
        source = (y + step) & 7
        landed(bias.at[0, 0, 0], recv_by.at[source])
        bias_along_x(source)
    row_logits(1)
    loaded(12)
    final_t[...] = w_fin[...].astype(F32).T.astype(BF16)

    def own_arrived(turn):
        source = nearest(turn)
        for other in range(1, 4):
            landed(bias.at[0, 0, 0], recv_bx.at[((x + other) & 3) * 8 + source])
        bias_to_core(source)
        return source

    def other_arrived(turn):
        source = nearest(turn)
        landed(bias.at[:, 0, 0], recv_bc.at[source])
        return source

    def both_queries(turn, _):
        mine_, theirs = own_arrived(turn), other_arrived(turn - 1)
        row_softmax(mine_, core)
        row_softmax(theirs, 1 - core)
        return 0

    loaded(6)
    row_softmax(own_arrived(0), core)
    lax.fori_loop(1, 8, both_queries, 0)
    row_softmax(other_arrived(7), 1 - core)
    row_finish(core)
    row_finish(1 - core)
    leaving.append((bias.at[0, pl.ds(0, 7), 0], BIAS_Y))
    leaving.append((bias.at[pl.ds(0, 3), :, 0], BIAS_X))
    leaving.append((bias.at[:, :, 0], BIAS_C))
    msa_src[...] = staged[...].astype(BF16).reshape(32, 16, 128)

    def push_msa(turn, _):
        other = far_first(turn)
        push(msa_src.at[other], msa_in.at[xy], MSA1, device(other, zh, core), rep, recv_m1.at[x])
        return 0

    lax.fori_loop(0, 31, push_msa, 0)
    leaving.append((msa_in.at[pl.ds(0, 31)], MSA1))
    msa_in[xy] = msa_src[xy]
    for step in (0, 1, 3, 2):
        source = (x + step) & 3
        landed(msa_in.at[pl.ds(0, 8 if step else 7)], recv_m1.at[source])
        start = pl.multiple_of(source * 128, 128)
        unpacked[pl.ds(start, 128), :] = msa_in[pl.ds(source * 8, 8)].astype(F32).reshape(128, 128)
        for target in range(4):
            parts = [
                jnp.concatenate(
                    [unpacked[pl.ds(start + target * 4 + s * 2 + half, 8, stride=16), :] for half in range(2)], axis=1
                )
                for s in range(2)
            ]
            col_src[target, source] = jnp.concatenate(parts, axis=0).astype(BF16)
        for turn in range(1, 4):
            other = (zc + turn) & 3
            push(col_src.at[other, source], col_in.at[zc, source], MSA2, device(xy, other >> 1, other & 1), rep)
        col_in[zc, source] = col_src[zc, source]
    leaving.append((col_in.at[pl.ds(0, 3)], MSA2))
    arrived(col_in.at[pl.ds(0, 3)], MSA2)

    loaded(7, 8, 9, 10, 11)
    middle = col_in[...].astype(F32).reshape(ROWS, FEAT)
    tokens = layer_norm(middle, g_col[...])
    projected = dot(tokens, w_col[...])
    wide = expand_heads(projected[:, :FEAT] * LOGIT_SCALE)
    col_keys = projected[:, FEAT : 2 * FEAT].astype(BF16)
    col_values = projected[:, 2 * FEAT : 3 * FEAT].astype(BF16)
    col_gates = jax.nn.sigmoid(projected[:, 3 * FEAT :])
    col_logits[...] = dot_nt(wide, col_keys)

    def col_softmax(group, _):
        rows = pl.ds(pl.multiple_of(group * 128, 128), 128)
        raw = col_logits[rows, :]
        top = jnp.max(raw, axis=-1, keepdims=True)
        powers = jnp.exp2(raw - top)
        total = jnp.sum(powers, axis=-1, keepdims=True)
        col_weights[rows, :] = powers.astype(BF16)
        col_denom[rows, :] = jnp.broadcast_to(1.0 / total, (128, 128))
        return 0

    lax.fori_loop(0, 16, col_softmax, 0, unroll=2)
    attended = dot(col_weights[...], col_values)
    merged = merge_heads(attended, col_denom[...][:, :1])
    gated = (merged * col_gates).astype(BF16)
    target_rows = middle + dot(gated, wo_col[...])

    ln_opm = layer_norm(target_rows, g_opm[...])
    factors = dot_nt(w_fac[...], ln_opm)
    right_src[...] = factors[FACTOR:].astype(BF16)
    left_src[...] = (factors[:FACTOR] * (1.0 / ROWS)).astype(BF16)
    for step in range(1, 4):
        push(left_src, left.at[x, core, rep], LEFT, dap, (rep + step) & 3)
    push(right_src, right.at[y, zh], RIGHT1, device(mirror, 1 - zh, core), x, recv_r1.at[zh])

    @pl.when(x != rep)
    def _():
        push(right_src, right.at[y, zh], RIGHT1, device(mirror, zh, core), x, recv_r1.at[zh])

    @pl.when(x == rep)
    def _():
        right[y, zh] = right_src[...]

    leaving.append((None, RIGHT1))
    leaving.append((left.at[0, 0, pl.ds(0, 3)], LEFT))
    left[x, core, rep] = left_src[...]
    for block in range(32):
        m_, x_, s = block // 8, (block // 2) % 4, block % 2
        for half in range(2):
            natural[half, pl.ds(x_ * 64 + m_ * 2 + s, 8, stride=8), :] = target_rows[
                block * 8 : (block + 1) * 8, half * 128 : (half + 1) * 128
            ]
    final[rep] = jnp.concatenate([natural[0], natural[1]], axis=1).astype(BF16)
    def right_along_y(zh_):
        for step in (4, 3, 5, 2, 6, 1, 7):
            block = right.at[y, zh_]
            push(block, block, RIGHT_Y, device(x * 8 + ((y + step) & 7), zh, core), rep, recv_ry.at[y])

    def left_to_core(x_):
        block = left.at[x_, core]
        push(block, block, LEFT_C, device(xy, zh, 1 - core), rep, recv_lc.at[x_])

    def left_unpack(x_, core_):
        rows = pl.ds(pl.multiple_of((x_ * 2 + core_) * 128, 128), 128)
        block = left[x_, core_].astype(F32).reshape(128, ROWS)
        for half in range(2):
            left_f[half, rows, :] = block[:, half * 128 : (half + 1) * 128]

    arrived(left.at[0, 0, pl.ds(0, 3)], LEFT)
    for step in (2, 1, 3):
        block = left.at[x, core]
        push(block, block, LEFT_X, device(((x + step) & 3) * 8 + y, zh, core), rep, recv_lx.at[x])
    left_to_core(x)

    @pl.when(x != rep)
    def _():
        landed(right_src, recv_r1.at[zh])

    right_along_y(zh)
    landed(right_src, recv_r1.at[1 - zh])
    right_along_y(1 - zh)
    leaving.append((right.at[pl.ds(0, 7)], RIGHT_Y))
    for step in range(1, 4):
        push(final.at[rep], final.at[rep], FINAL, dap, (rep + step) & 3)
    leaving.append((final.at[pl.ds(0, 3)], FINAL))
    left_unpack(x, core)
    for step in (1, 3, 2):
        source = (x + step) & 3
        landed(left.at[0, 0], recv_lx.at[source])
        left_to_core(source)
        left_unpack(source, core)
    leaving.append((left.at[pl.ds(0, 3), 0], LEFT_X))
    leaving.append((left.at[:, 0], LEFT_C))
    for step in (0, 1, 3, 2):
        source = (x + step) & 3
        landed(left.at[0, 0], recv_lc.at[source])
        left_unpack(source, 1 - core)

    for channel in range(FACTOR):
        left_t[pl.ds(channel * 32, 32), :] = jnp.concatenate(
            [left_f[half, pl.ds(channel, 32, stride=FACTOR), :] for half in range(2)], axis=1
        ).astype(BF16)
    quarter = lax.broadcasted_iota(jnp.int32, (FACTOR, 128), 1) // 32
    for turn in range(1, 8):
        landed(right.at[0], recv_ry.at[nearest(turn)])
    right_all = right[...].reshape(16 * FACTOR, ROWS)
    for part in range(4):
        product = dot_nt(right_all, left_t[pl.ds(part * 256, 256), :])
        for tile in range(2):
            lanes = slice(tile * 128, (tile + 1) * 128)
            for four in range(4):
                blocks = [product[(four * 4 + jq) * FACTOR : (four * 4 + jq + 1) * FACTOR, lanes] for jq in range(4)]
                for cq in range(4):
                    moved = [
                        blocks[jq] if jq == cq else pltpu.roll(blocks[jq], (32 * (jq - cq)) % 128, 1) for jq in range(4)
                    ]
                    joined = jnp.where(
                        quarter < 2,
                        jnp.where(quarter == 0, moved[0], moved[1]),
                        jnp.where(quarter == 2, moved[2], moved[3]),
                    )
                    channel = part * 8 + tile * 4 + cq
                    outer[pl.ds(channel * FACTOR, FACTOR), four * 128 : (four + 1) * 128] = joined.astype(BF16)
    flat = dot(final_t[...], outer[...])
    for four in range(4):
        update[pl.ds(four * 128, 128), :] = flat[:, four * 128 : (four + 1) * 128].T

    for target in range(8):
        for r_ in range(4):
            result_src[target, r_] = update[pl.ds(target * 4 + r_, 16, stride=32), :].astype(BF16)
    mine = x * 2 + core
    for step in range(1, 8):
        other = (mine + step) & 7
        push(result_src.at[other], result_in.at[mine], RESULT, device((other >> 1) * 8 + y, zh, other & 1), rep)
    leaving.append((result_in.at[pl.ds(0, 7)], RESULT))
    result_in[mine] = result_src[mine]

    arrived(final.at[pl.ds(0, 3)], FINAL)
    for half in range(2):
        for r_ in range(4):
            out_msa[pl.ds(half * 4 + r_, ROWS, stride=8), :] = final[r_, :, half * 128 : (half + 1) * 128].astype(F32)

    arrived(result_in.at[pl.ds(0, 7)], RESULT)
    for source in range(8):
        for a in range(4):
            here = pl.ds(4 * (source % 2) + source // 2, 16, stride=8)
            out_pair[a, here, :] = pair[a, here, :] + result_in[source, a].astype(F32)

    finish()


def shards(
    alignment_source_tensor,
    couple_source_tensor,
    horizontal_scale_factor,
    horizontal_projection_matrix,
    couple_scale_factor,
    couple_offset_matrix,
    horizontal_final_matrix,
    vertical_scale_factor,
    vertical_projection_matrix,
    vertical_final_matrix,
    tensorial_scale_factor,
    tensorial_factor_matrix,
    tensorial_final_matrix,
):
    operands = [
        alignment_source_tensor,
        couple_source_tensor,
        horizontal_scale_factor.reshape(1, FEAT),
        horizontal_projection_matrix,
        couple_scale_factor.reshape(1, CZ),
        couple_offset_matrix.T,
        horizontal_final_matrix,
        vertical_scale_factor.reshape(1, FEAT),
        vertical_projection_matrix,
        vertical_final_matrix,
        tensorial_scale_factor.reshape(1, FEAT),
        tensorial_factor_matrix.T,
        tensorial_final_matrix,
    ]
    vmem = pl.BlockSpec(memory_space=pltpu.VMEM)
    scratch = [pltpu.VMEM(a.shape, a.dtype) for a in operands] + [
        pltpu.VMEM((4, 8, 128), F32),
        pltpu.VMEM((8, 8, 128), F32),
        pltpu.VMEM((4, 8, 2, 16, RES), BF16),
        pltpu.VMEM((2, 2, 2, 64, 128), F32),
        pltpu.VMEM((2, 2, 64, FEAT), F32),
        pltpu.VMEM((2, RES, FEAT), BF16),
        pltpu.VMEM((2, RES, FEAT), BF16),
        pltpu.VMEM((2, 2, 4, 8, 16, RES), F32),
        pltpu.VMEM((2, 2, 4, 8, 16, RES), BF16),
        pltpu.VMEM((2, 2, 4, 8, 16, 128), F32),
        pltpu.VMEM((512, 128), F32),
        pltpu.VMEM((32, 16, 128), BF16),
        pltpu.VMEM((32, 16, 128), BF16),
        pltpu.VMEM((512, 128), F32),
        pltpu.VMEM((4, 4, 16, FEAT), BF16),
        pltpu.VMEM((4, 4, 16, FEAT), BF16),
        pltpu.VMEM((ROWS * HEADS, ROWS), F32),
        pltpu.VMEM((ROWS * HEADS, ROWS), BF16),
        pltpu.VMEM((ROWS * HEADS, 128), F32),
        pltpu.VMEM((2, ROWS, 128), F32),
        pltpu.VMEM((4, ROWS, FEAT), BF16),
        pltpu.VMEM((FACTOR, ROWS), BF16),
        pltpu.VMEM((4, 2, 4, FACTOR, ROWS), BF16),
        pltpu.VMEM((FACTOR, ROWS), BF16),
        pltpu.VMEM((8, 2, FACTOR, ROWS), BF16),
        pltpu.VMEM((2, 32 * FACTOR, 128), F32),
        pltpu.VMEM((32 * FACTOR, ROWS), BF16),
        pltpu.VMEM((CZ, FACTOR * FACTOR), BF16),
        pltpu.VMEM((FACTOR * FACTOR, 512), BF16),
        pltpu.VMEM((512, CZ), F32),
        pltpu.VMEM((8, 4, 16, CZ), BF16),
        pltpu.VMEM((8, 4, 16, CZ), BF16),
        pltpu.VMEM((2, 2, RES, 128), F32),
        pltpu.SemaphoreType.DMA((PHASES,)),
        pltpu.SemaphoreType.DMA((PHASES,)),
        pltpu.SemaphoreType.DMA((len(operands),)),
        pltpu.SemaphoreType.DMA((8,)),
        pltpu.SemaphoreType.DMA((32,)),
        pltpu.SemaphoreType.DMA((8,)),
        pltpu.SemaphoreType.DMA((2,)),
        pltpu.SemaphoreType.DMA((8,)),
        pltpu.SemaphoreType.DMA((4,)),
        pltpu.SemaphoreType.DMA((4,)),
        pltpu.SemaphoreType.DMA((4,)),
    ]
    out_msa, out_pair = pl.pallas_call(
        kernel,
        out_shape=(
            jax.ShapeDtypeStruct((ROWS * 8, 128), F32),
            jax.ShapeDtypeStruct((4, 128, CZ), F32),
        ),
        in_specs=[pl.BlockSpec(memory_space=pltpu.HBM)] * len(operands),
        out_specs=(vmem, vmem),
        scratch_shapes=scratch,
        compiler_params=pltpu.CompilerParams(
            collective_id=0, has_side_effects=True, vmem_limit_bytes=44 * 1024 * 1024
        ),
    )(*[pltpu.with_memory_space_constraint(a, pltpu.HBM) for a in operands])
    return jnp.swapaxes(out_msa.reshape(ROWS, 2, 4, 128), 1, 2).reshape(ROWS, 4, FEAT), out_pair


def solution(mesh):
    return jax.shard_map(
        shards,
        mesh=mesh,
        in_specs=(P("dap", None, None), P("dap", "rep", None)) + (P(),) * 11,
        out_specs=(P(None, "dap", None), P("dap", "rep", None)),
        check_vma=False,
    )
```

```python
import math

import jax
import jax.numpy as jnp
from jax import lax
from jax.experimental import pallas as pl
from jax.experimental.pallas import tpu as pltpu
from jax.sharding import PartitionSpec as P

HEADS = 8
HEAD_DIM = 32
FEAT = HEADS * HEAD_DIM
CZ = 128
ROWS = 256
RES = 512
FACTOR = 32
LOG2E = math.log2(math.e)
LOGIT_SCALE = HEAD_DIM ** (-0.5) * LOG2E
MESH = pl.DeviceIdType.MESH
F32 = jnp.float32
BF16 = jnp.bfloat16

BIAS1, BIAS_Y, BIAS_X, BIAS_C, MSA1, MSA2, LEFT, LEFT_X, LEFT_C, FINAL, RIGHT1, RIGHT_Y, RESULT = range(13)
PHASES = 13
SHEET_STEPS = (10, 8, 9, 11, 6, 7, 5, 14, 13, 15, 2, 3, 1, 12, 4)


def layer_norm(values, gain):
    average = jnp.mean(values, axis=-1, keepdims=True)
    centred = values - average
    variance = jnp.mean(centred * centred, axis=-1, keepdims=True)
    return (centred * lax.rsqrt(variance + 1e-05) * gain).astype(BF16)


def dot(a, b):
    return lax.dot_general(a, b, (((1,), (0,)), ((), ())), preferred_element_type=F32)


def dot_nt(a, b):
    return lax.dot_general(a, b, (((1,), (1,)), ((), ())), preferred_element_type=F32)


def head_mask():
    head = lax.broadcasted_iota(jnp.int32, (HEADS, FEAT), 0)
    channel = lax.broadcasted_iota(jnp.int32, (HEADS, FEAT), 1) // HEAD_DIM
    return (head == channel).astype(F32)


def expand_heads(queries):
    n = queries.shape[0]
    spread = jnp.broadcast_to(queries[:, None, :], (n, HEADS, FEAT))
    return (spread * head_mask()[None]).reshape(n * HEADS, FEAT).astype(BF16)


def merge_heads(attended, inverse):
    n = attended.shape[0] // HEADS
    scaled = (attended * inverse).reshape(n, HEADS, FEAT) * head_mask()[None]
    return jnp.sum(scaled, axis=1)


def kernel(*refs):
    given, (out_msa, out_pair), held, rest = refs[:13], refs[13:15], refs[15:28], refs[28:]
    msa, pair, g_row, w_row, g_pair, w_bias, wo_row, g_col, w_col, wo_col, g_opm, w_fac, w_fin = held
    (
        bias_src, bias_in, bias, queries, gates, keys, values, logits, weights, denom, staged, msa_src, msa_in,
        unpacked, col_src, col_in, col_logits, col_weights, col_denom, natural, final, left_src, left, right_src, right,
        left_f, left_t, final_t, outer, update, result_src, result_in, msa_halves,
        send, recv, load, recv_by, recv_bx, recv_bc, recv_r1, recv_ry, recv_lx, recv_lc,
    ) = rest
    loads = [pltpu.make_async_copy(given[k], held[k], load.at[k]) for k in range(13)]
    for k in (1, 5, 4):
        loads[k].start()

    def loaded(*which):
        for k in which:
            loads[k].wait()

    dap = lax.axis_index("dap")
    rep = lax.axis_index("rep")
    x = dap >> 5
    y = (dap >> 2) & 7
    xy = dap >> 2
    zc = dap & 3
    zh = zc >> 1
    core = zc & 1

    def device(xy_, zh_, core_):
        return xy_ * 4 + zh_ * 2 + core_

    barrier = pltpu.get_barrier_semaphore()

    def greet(dap_, rep_):
        pl.semaphore_signal(barrier, inc=1, device_id=(dap_, rep_), device_id_type=MESH)

    mirror = rep * 8 + y
    greet(device(mirror, 1 - zh, core), x)

    @pl.when(x != rep)
    def _():
        greet(device(mirror, zh, core), x)

    place = x * 4 + zc

    def sheet(other):
        return device((other >> 2) * 8 + y, (other >> 1) & 1, other & 1)

    for step in SHEET_STEPS:
        greet(sheet((place + step) & 15), rep)
    for step in (4, 3, 5, 2, 6, 1, 7):
        other = (zh * 4 + rep + step) & 7
        greet(device(xy, other >> 2, core), other & 3)
    for step in (4, 3, 5, 2, 6, 1, 7):
        greet(device(x * 8 + ((y + step) & 7), zh, core), rep)
    for k in (0, 2, 3, 6, 12, 7, 8, 9, 10, 11):
        loads[k].start()

    def push(src, dst, phase, dap_, rep_, into=None):
        pltpu.make_async_remote_copy(
            src_ref=src, dst_ref=dst, send_sem=send.at[phase], recv_sem=recv.at[phase] if into is None else into,
            device_id=(dap_, rep_), device_id_type=MESH,
        ).start()

    def arrived(shaped, phase):
        landed(shaped, recv.at[phase])

    def landed(shaped, sem):
        pltpu.make_async_copy(shaped, shaped, sem).wait()

    def drained(shaped, phase):
        pltpu.make_async_copy(shaped, shaped, send.at[phase]).wait()

    leaving = []

    def finish():
        for shaped, phase in leaving:
            if shaped is not None:
                drained(shaped, phase)
                continue

            @pl.when(x != rep)
            def _():
                drained(right.at[0], RIGHT1)

            @pl.when(x == rep)
            def _():
                drained(right_src, RIGHT1)

    def bias_along_x(y_):
        block = bias.at[x, y_, core]
        for step in range(1, 4):
            push(block, block, BIAS_X, device(((x + step) & 3) * 8 + y, zh, core), rep, recv_bx.at[x * 8 + y_])

    def bias_to_core(y_):
        block = bias.at[:, y_, core]
        push(block, block, BIAS_C, device(xy, zh, 1 - core), rep, recv_bc.at[y_])

    loaded(1, 4, 5)
    ln_pair = layer_norm(pair[...].reshape(4 * 128, CZ), g_pair[...])
    head_bias = dot_nt(w_bias[...], ln_pair) * LOG2E
    for a in range(4):
        bias_src[a] = head_bias[:, a * 128 : (a + 1) * 128]

    pl.semaphore_wait(barrier, 30 + jnp.where(x != rep, 1, 0))

    for step in (4, 3, 5, 2, 6, 1, 7):
        other = (zh * 4 + rep + step) & 7
        push(bias_src.at[other & 3], bias_in.at[zh * 4 + rep], BIAS1, device(xy, other >> 2, core), other & 3)
    leaving.append((bias_in.at[pl.ds(0, 7)], BIAS1))
    bias_in[zh * 4 + rep] = bias_src[rep]

    loaded(0, 2, 3)
    for s in range(2):
        tokens = layer_norm(msa[s], g_row[...])
        projected = dot(tokens, w_row[:, FEAT : 3 * FEAT]).astype(BF16)
        keys[s] = projected[:, :FEAT]
        values[s] = projected[:, FEAT:]
        for half in range(2):
            msa_halves[s, half] = msa[s, :, half * 128 : (half + 1) * 128]
            for x_ in range(4):
                for h_ in range(2):
                    for c_ in range(2):
                        queries[s, c_, half, pl.ds(x_ * 2 + h_, 8, stride=8), :] = msa_halves[
                            s, half, pl.ds(128 * x_ + 8 * h_ + 4 * c_ + rep, 8, stride=16), :
                        ]

    arrived(bias_in.at[pl.ds(0, 7)], BIAS1)
    block = jnp.concatenate(
        [jnp.concatenate([bias_in[h_ * 4 + r_] for r_ in range(4)], axis=1) for h_ in range(2)], axis=0
    )
    bias[x, y, core] = block.astype(BF16)
    for step in (4, 3, 5, 2, 6, 1, 7):
        block = bias.at[x, y, core]
        push(block, block, BIAS_Y, device(x * 8 + ((y + step) & 7), zh, core), rep, recv_by.at[y])
    bias_along_x(y)

    def row_logits(s):
        halves = [jnp.concatenate([queries[s, 0, half], queries[s, 1, half]], axis=0) for half in range(2)]
        tokens = layer_norm(jnp.concatenate(halves, axis=1), g_row[...])
        wide = dot(tokens, w_row[:, :FEAT]) * LOGIT_SCALE
        gates[s] = jax.nn.sigmoid(dot(tokens, w_row[:, 3 * FEAT :])).reshape(2, 64, FEAT)
        logits[s] = dot_nt(expand_heads(wide), keys[s]).reshape(2, 8, 4, 16, RES)

    def nearest(turn):
        away = (turn + 1) >> 1
        return (y + jnp.where((turn & 1) == 1, away, 8 - away)) & 7

    def row_softmax(y_, which):
        offset = bias[:, y_, which].astype(F32).reshape(64, RES)
        for s in range(2):
            raw = logits[s, which, y_].reshape(64, RES) + offset
            top = jnp.max(raw, axis=-1, keepdims=True)
            powers = jnp.exp2(raw - top)
            total = jnp.sum(powers, axis=-1, keepdims=True)
            weights[s, which, y_] = powers.astype(BF16).reshape(4, 16, RES)
            denom[s, which, y_] = jnp.broadcast_to(1.0 / total, (64, 128)).reshape(4, 16, 128)

    def row_finish(which):
        for s in range(2):
            attended = dot(weights[s, which].reshape(512, RES), values[s])
            merged = merge_heads(attended, denom[s, which].reshape(512, 128)[:, :1])
            gated = (merged * gates[s, which]).astype(BF16)
            change = dot(gated, wo_row[...])
            for half in range(2):
                staged[pl.ds(which * 4 + s * 2 + half, 64, stride=8), :] = (
                    queries[s, which, half] + change[:, half * 128 : (half + 1) * 128]
                )

    row_logits(0)
    for step in (1, 7, 2, 6, 3, 5, 4):
        source = (y + step) & 7
        landed(bias.at[0, 0, 0], recv_by.at[source])
        bias_along_x(source)
    row_logits(1)
    loaded(12)
    final_t[...] = w_fin[...].astype(F32).T.astype(BF16)

    def own_arrived(turn):
        source = nearest(turn)
        for other in range(1, 4):
            landed(bias.at[0, 0, 0], recv_bx.at[((x + other) & 3) * 8 + source])
        bias_to_core(source)
        return source

    def other_arrived(turn):
        source = nearest(turn)
        landed(bias.at[:, 0, 0], recv_bc.at[source])
        return source

    def both_queries(turn, _):
        mine_, theirs = own_arrived(turn), other_arrived(turn - 1)
        row_softmax(mine_, core)
        row_softmax(theirs, 1 - core)
        return 0

    loaded(6)
    row_softmax(own_arrived(0), core)
    lax.fori_loop(1, 8, both_queries, 0)
    row_softmax(other_arrived(7), 1 - core)
    row_finish(core)
    row_finish(1 - core)
    leaving.append((bias.at[0, pl.ds(0, 7), 0], BIAS_Y))
    leaving.append((bias.at[pl.ds(0, 3), :, 0], BIAS_X))
    leaving.append((bias.at[:, :, 0], BIAS_C))
    msa_src[...] = staged[...].astype(BF16).reshape(8, 64, 128)

    for step in (4, 3, 5, 2, 6, 1, 7):
        other = (y + step) & 7
        push(msa_src.at[other], msa_in.at[y], MSA1, device(x * 8 + other, zh, core), rep)
    leaving.append((msa_in.at[pl.ds(0, 7)], MSA1))
    msa_in[y] = msa_src[y]
    arrived(msa_in.at[pl.ds(0, 7)], MSA1)
    unpacked[...] = msa_in[...].astype(F32).reshape(512, 128)
    for target in range(16):
        parts = [
            jnp.concatenate([unpacked[pl.ds(target * 4 + s * 2 + half, 8, stride=64), :] for half in range(2)], axis=1)
            for s in range(2)
        ]
        col_src[target] = jnp.concatenate(parts, axis=0).astype(BF16)
    for step in SHEET_STEPS:
        other = (place + step) & 15
        push(col_src.at[other], col_in.at[place], MSA2, sheet(other), rep)
    leaving.append((col_in.at[pl.ds(0, 15)], MSA2))
    col_in[place] = col_src[place]
    arrived(col_in.at[pl.ds(0, 15)], MSA2)

    loaded(7, 8, 9, 10, 11)
    middle = col_in[...].astype(F32).reshape(ROWS, FEAT)
    tokens = layer_norm(middle, g_col[...])
    projected = dot(tokens, w_col[...])
    wide = expand_heads(projected[:, :FEAT] * LOGIT_SCALE)
    col_keys = projected[:, FEAT : 2 * FEAT].astype(BF16)
    col_values = projected[:, 2 * FEAT : 3 * FEAT].astype(BF16)
    col_gates = jax.nn.sigmoid(projected[:, 3 * FEAT :])
    col_logits[...] = dot_nt(wide, col_keys)

    def col_softmax(group, _):
        rows = pl.ds(pl.multiple_of(group * 128, 128), 128)
        raw = col_logits[rows, :]
        top = jnp.max(raw, axis=-1, keepdims=True)
        powers = jnp.exp2(raw - top)
        total = jnp.sum(powers, axis=-1, keepdims=True)
        col_weights[rows, :] = powers.astype(BF16)
        col_denom[rows, :] = jnp.broadcast_to(1.0 / total, (128, 128))
        return 0

    lax.fori_loop(0, 16, col_softmax, 0, unroll=2)
    attended = dot(col_weights[...], col_values)
    merged = merge_heads(attended, col_denom[...][:, :1])
    gated = (merged * col_gates).astype(BF16)
    target_rows = middle + dot(gated, wo_col[...])

    ln_opm = layer_norm(target_rows, g_opm[...])
    factors = dot_nt(w_fac[...], ln_opm)
    right_src[...] = factors[FACTOR:].astype(BF16)
    left_src[...] = (factors[:FACTOR] * (1.0 / ROWS)).astype(BF16)
    for step in range(1, 4):
        push(left_src, left.at[x, core, rep], LEFT, dap, (rep + step) & 3)
    push(right_src, right.at[y, zh], RIGHT1, device(mirror, 1 - zh, core), x, recv_r1.at[zh])

    @pl.when(x != rep)
    def _():
        push(right_src, right.at[y, zh], RIGHT1, device(mirror, zh, core), x, recv_r1.at[zh])

    @pl.when(x == rep)
    def _():
        right[y, zh] = right_src[...]

    leaving.append((None, RIGHT1))
    leaving.append((left.at[0, 0, pl.ds(0, 3)], LEFT))
    left[x, core, rep] = left_src[...]
    for block in range(32):
        x_, m_, s = block // 8, (block // 2) % 4, block % 2
        for half in range(2):
            natural[half, pl.ds(x_ * 64 + m_ * 2 + s, 8, stride=8), :] = target_rows[
                block * 8 : (block + 1) * 8, half * 128 : (half + 1) * 128
            ]
    final[rep] = jnp.concatenate([natural[0], natural[1]], axis=1).astype(BF16)
    def right_along_y(zh_):
        for step in (4, 3, 5, 2, 6, 1, 7):
            block = right.at[y, zh_]
            push(block, block, RIGHT_Y, device(x * 8 + ((y + step) & 7), zh, core), rep, recv_ry.at[y])

    def left_to_core(x_):
        block = left.at[x_, core]
        push(block, block, LEFT_C, device(xy, zh, 1 - core), rep, recv_lc.at[x_])

    def left_unpack(x_, core_):
        rows = pl.ds(pl.multiple_of((x_ * 2 + core_) * 128, 128), 128)
        block = left[x_, core_].astype(F32).reshape(128, ROWS)
        for half in range(2):
            left_f[half, rows, :] = block[:, half * 128 : (half + 1) * 128]

    arrived(left.at[0, 0, pl.ds(0, 3)], LEFT)
    for step in (2, 1, 3):
        block = left.at[x, core]
        push(block, block, LEFT_X, device(((x + step) & 3) * 8 + y, zh, core), rep, recv_lx.at[x])
    left_to_core(x)

    @pl.when(x != rep)
    def _():
        landed(right_src, recv_r1.at[zh])

    right_along_y(zh)
    landed(right_src, recv_r1.at[1 - zh])
    right_along_y(1 - zh)
    leaving.append((right.at[pl.ds(0, 7)], RIGHT_Y))
    for step in range(1, 4):
        push(final.at[rep], final.at[rep], FINAL, dap, (rep + step) & 3)
    leaving.append((final.at[pl.ds(0, 3)], FINAL))
    left_unpack(x, core)
    for step in (1, 3, 2):
        source = (x + step) & 3
        landed(left.at[0, 0], recv_lx.at[source])
        left_to_core(source)
        left_unpack(source, core)
    leaving.append((left.at[pl.ds(0, 3), 0], LEFT_X))
    leaving.append((left.at[:, 0], LEFT_C))
    for step in (0, 1, 3, 2):
        source = (x + step) & 3
        landed(left.at[0, 0], recv_lc.at[source])
        left_unpack(source, 1 - core)

    for channel in range(FACTOR):
        left_t[pl.ds(channel * 32, 32), :] = jnp.concatenate(
            [left_f[half, pl.ds(channel, 32, stride=FACTOR), :] for half in range(2)], axis=1
        ).astype(BF16)
    quarter = lax.broadcasted_iota(jnp.int32, (FACTOR, 128), 1) // 32
    for turn in range(1, 8):
        landed(right.at[0], recv_ry.at[nearest(turn)])
    right_all = right[...].reshape(16 * FACTOR, ROWS)
    for part in range(4):
        product = dot_nt(right_all, left_t[pl.ds(part * 256, 256), :])
        for tile in range(2):
            lanes = slice(tile * 128, (tile + 1) * 128)
            for four in range(4):
                blocks = [product[(four * 4 + jq) * FACTOR : (four * 4 + jq + 1) * FACTOR, lanes] for jq in range(4)]
                for cq in range(4):
                    moved = [
                        blocks[jq] if jq == cq else pltpu.roll(blocks[jq], (32 * (jq - cq)) % 128, 1) for jq in range(4)
                    ]
                    joined = jnp.where(
                        quarter < 2,
                        jnp.where(quarter == 0, moved[0], moved[1]),
                        jnp.where(quarter == 2, moved[2], moved[3]),
                    )
                    channel = part * 8 + tile * 4 + cq
                    outer[pl.ds(channel * FACTOR, FACTOR), four * 128 : (four + 1) * 128] = joined.astype(BF16)
    flat = dot(final_t[...], outer[...])
    for four in range(4):
        update[pl.ds(four * 128, 128), :] = flat[:, four * 128 : (four + 1) * 128].T

    for target in range(8):
        for r_ in range(4):
            result_src[target, r_] = update[pl.ds(target * 4 + r_, 16, stride=32), :].astype(BF16)
    mine = x * 2 + core
    for step in range(1, 8):
        other = (mine + step) & 7
        push(result_src.at[other], result_in.at[mine], RESULT, device((other >> 1) * 8 + y, zh, other & 1), rep)
    leaving.append((result_in.at[pl.ds(0, 7)], RESULT))
    result_in[mine] = result_src[mine]

    arrived(final.at[pl.ds(0, 3)], FINAL)
    for half in range(2):
        for r_ in range(4):
            out_msa[pl.ds(half * 4 + r_, ROWS, stride=8), :] = final[r_, :, half * 128 : (half + 1) * 128].astype(F32)

    arrived(result_in.at[pl.ds(0, 7)], RESULT)
    for source in range(8):
        for a in range(4):
            here = pl.ds(4 * (source % 2) + source // 2, 16, stride=8)
            out_pair[a, here, :] = pair[a, here, :] + result_in[source, a].astype(F32)

    finish()


def shards(
    alignment_source_tensor,
    couple_source_tensor,
    horizontal_scale_factor,
    horizontal_projection_matrix,
    couple_scale_factor,
    couple_offset_matrix,
    horizontal_final_matrix,
    vertical_scale_factor,
    vertical_projection_matrix,
    vertical_final_matrix,
    tensorial_scale_factor,
    tensorial_factor_matrix,
    tensorial_final_matrix,
):
    operands = [
        alignment_source_tensor,
        couple_source_tensor,
        horizontal_scale_factor.reshape(1, FEAT),
        horizontal_projection_matrix,
        couple_scale_factor.reshape(1, CZ),
        couple_offset_matrix.T,
        horizontal_final_matrix,
        vertical_scale_factor.reshape(1, FEAT),
        vertical_projection_matrix,
        vertical_final_matrix,
        tensorial_scale_factor.reshape(1, FEAT),
        tensorial_factor_matrix.T,
        tensorial_final_matrix,
    ]
    vmem = pl.BlockSpec(memory_space=pltpu.VMEM)
    scratch = [pltpu.VMEM(a.shape, a.dtype) for a in operands] + [
        pltpu.VMEM((4, 8, 128), F32),
        pltpu.VMEM((8, 8, 128), F32),
        pltpu.VMEM((4, 8, 2, 16, RES), BF16),
        pltpu.VMEM((2, 2, 2, 64, 128), F32),
        pltpu.VMEM((2, 2, 64, FEAT), F32),
        pltpu.VMEM((2, RES, FEAT), BF16),
        pltpu.VMEM((2, RES, FEAT), BF16),
        pltpu.VMEM((2, 2, 8, 4, 16, RES), F32),
        pltpu.VMEM((2, 2, 8, 4, 16, RES), BF16),
        pltpu.VMEM((2, 2, 8, 4, 16, 128), F32),
        pltpu.VMEM((512, 128), F32),
        pltpu.VMEM((8, 64, 128), BF16),
        pltpu.VMEM((8, 64, 128), BF16),
        pltpu.VMEM((512, 128), F32),
        pltpu.VMEM((16, 16, FEAT), BF16),
        pltpu.VMEM((16, 16, FEAT), BF16),
        pltpu.VMEM((ROWS * HEADS, ROWS), F32),
        pltpu.VMEM((ROWS * HEADS, ROWS), BF16),
        pltpu.VMEM((ROWS * HEADS, 128), F32),
        pltpu.VMEM((2, ROWS, 128), F32),
        pltpu.VMEM((4, ROWS, FEAT), BF16),
        pltpu.VMEM((FACTOR, ROWS), BF16),
        pltpu.VMEM((4, 2, 4, FACTOR, ROWS), BF16),
        pltpu.VMEM((FACTOR, ROWS), BF16),
        pltpu.VMEM((8, 2, FACTOR, ROWS), BF16),
        pltpu.VMEM((2, 32 * FACTOR, 128), F32),
        pltpu.VMEM((32 * FACTOR, ROWS), BF16),
        pltpu.VMEM((CZ, FACTOR * FACTOR), BF16),
        pltpu.VMEM((FACTOR * FACTOR, 512), BF16),
        pltpu.VMEM((512, CZ), F32),
        pltpu.VMEM((8, 4, 16, CZ), BF16),
        pltpu.VMEM((8, 4, 16, CZ), BF16),
        pltpu.VMEM((2, 2, RES, 128), F32),
        pltpu.SemaphoreType.DMA((PHASES,)),
        pltpu.SemaphoreType.DMA((PHASES,)),
        pltpu.SemaphoreType.DMA((len(operands),)),
        pltpu.SemaphoreType.DMA((8,)),
        pltpu.SemaphoreType.DMA((32,)),
        pltpu.SemaphoreType.DMA((8,)),
        pltpu.SemaphoreType.DMA((2,)),
        pltpu.SemaphoreType.DMA((8,)),
        pltpu.SemaphoreType.DMA((4,)),
        pltpu.SemaphoreType.DMA((4,)),
    ]
    out_msa, out_pair = pl.pallas_call(
        kernel,
        out_shape=(
            jax.ShapeDtypeStruct((ROWS * 8, 128), F32),
            jax.ShapeDtypeStruct((4, 128, CZ), F32),
        ),
        in_specs=[pl.BlockSpec(memory_space=pltpu.HBM)] * len(operands),
        out_specs=(vmem, vmem),
        scratch_shapes=scratch,
        compiler_params=pltpu.CompilerParams(
            collective_id=0, has_side_effects=True, vmem_limit_bytes=44 * 1024 * 1024
        ),
    )(*[pltpu.with_memory_space_constraint(a, pltpu.HBM) for a in operands])
    return jnp.swapaxes(out_msa.reshape(ROWS, 2, 4, 128), 1, 2).reshape(ROWS, 4, FEAT), out_pair


def solution(mesh):
    return jax.shard_map(
        shards,
        mesh=mesh,
        in_specs=(P("dap", None, None), P("dap", "rep", None)) + (P(),) * 11,
        out_specs=(P(None, "dap", None), P("dap", "rep", None)),
        check_vma=False,
    )
```

```python
import math

import jax
import jax.numpy as jnp
from jax import lax
from jax.experimental import pallas as pl
from jax.experimental.pallas import tpu as pltpu
from jax.sharding import PartitionSpec as P

HEADS = 8
HEAD_DIM = 32
FEAT = HEADS * HEAD_DIM
CZ = 128
ROWS = 256
RES = 512
FACTOR = 32
LOG2E = math.log2(math.e)
LOGIT_SCALE = HEAD_DIM ** (-0.5) * LOG2E
MESH = pl.DeviceIdType.MESH
F32 = jnp.float32
BF16 = jnp.bfloat16

BIAS1, BIAS_Y, BIAS_X, BIAS_C, MSA1, MSA2, LEFT, LEFT_X, LEFT_C, FINAL, RIGHT1, RIGHT_Y, RESULT = range(13)
PHASES = 13


def layer_norm(values, gain):
    average = jnp.mean(values, axis=-1, keepdims=True)
    centred = values - average
    variance = jnp.mean(centred * centred, axis=-1, keepdims=True)
    return (centred * lax.rsqrt(variance + 1e-05) * gain).astype(BF16)


def dot(a, b):
    return lax.dot_general(a, b, (((1,), (0,)), ((), ())), preferred_element_type=F32)


def dot_nt(a, b):
    return lax.dot_general(a, b, (((1,), (1,)), ((), ())), preferred_element_type=F32)


def head_mask():
    head = lax.broadcasted_iota(jnp.int32, (HEADS, FEAT), 0)
    channel = lax.broadcasted_iota(jnp.int32, (HEADS, FEAT), 1) // HEAD_DIM
    return (head == channel).astype(F32)


def expand_heads(queries):
    n = queries.shape[0]
    spread = jnp.broadcast_to(queries[:, None, :], (n, HEADS, FEAT))
    return (spread * head_mask()[None]).reshape(n * HEADS, FEAT).astype(BF16)


def merge_heads(attended, inverse):
    n = attended.shape[0] // HEADS
    scaled = (attended * inverse).reshape(n, HEADS, FEAT) * head_mask()[None]
    return jnp.sum(scaled, axis=1)


def kernel(*refs):
    given, (out_msa, out_pair), held, rest = refs[:13], refs[13:15], refs[15:28], refs[28:]
    msa, pair, g_row, w_row, g_pair, w_bias, wo_row, g_col, w_col, wo_col, g_opm, w_fac, w_fin = held
    (
        bias_src, bias_in, bias, queries, gates, keys, values, logits, weights, denom, staged, msa_src, msa_in,
        unpacked, col_src, col_in, col_logits, col_weights, col_denom, natural, final, left_src, left, right_src, right,
        left_f, left_t, final_t, outer, update, result_src, result_in, msa_halves,
        send, recv, load, recv_by, recv_bx, recv_bc, recv_r1, recv_ry, recv_lx, recv_lc, recv_m1,
    ) = rest
    loads = [pltpu.make_async_copy(given[k], held[k], load.at[k]) for k in range(13)]
    for k in (1, 5, 4):
        loads[k].start()

    def loaded(*which):
        for k in which:
            loads[k].wait()

    dap = lax.axis_index("dap")
    rep = lax.axis_index("rep")
    x = dap >> 5
    y = (dap >> 2) & 7
    xy = dap >> 2
    zc = dap & 3
    zh = zc >> 1
    core = zc & 1

    def device(xy_, zh_, core_):
        return xy_ * 4 + zh_ * 2 + core_

    barrier = pltpu.get_barrier_semaphore()

    def greet(dap_, rep_):
        pl.semaphore_signal(barrier, inc=1, device_id=(dap_, rep_), device_id_type=MESH)

    def far_first(turn):
        return (xy + turn + jnp.where(turn < 20, 12, -19)) & 31

    def greet_xy(turn, _):
        greet(device(far_first(turn), zh, core), rep)
        return 0

    mirror = rep * 8 + y
    greet(device(mirror, 1 - zh, core), x)

    @pl.when(x != rep)
    def _():
        greet(device(mirror, zh, core), x)

    lax.fori_loop(0, 31, greet_xy, 0)
    for step in (4, 3, 5, 2, 6, 1, 7):
        other = (zh * 4 + rep + step) & 7
        greet(device(xy, other >> 2, core), other & 3)
    for step in range(4):
        greet(device(((x + step) & 3) * 8 + y, zh, 1 - core), rep)
    greet(device(xy, 1 - zh, 1 - core), rep)
    for k in (0, 2, 3, 6, 12, 7, 8, 9, 10, 11):
        loads[k].start()

    def push(src, dst, phase, dap_, rep_, into=None):
        pltpu.make_async_remote_copy(
            src_ref=src, dst_ref=dst, send_sem=send.at[phase], recv_sem=recv.at[phase] if into is None else into,
            device_id=(dap_, rep_), device_id_type=MESH,
        ).start()

    def arrived(shaped, phase):
        landed(shaped, recv.at[phase])

    def landed(shaped, sem):
        pltpu.make_async_copy(shaped, shaped, sem).wait()

    def drained(shaped, phase):
        pltpu.make_async_copy(shaped, shaped, send.at[phase]).wait()

    leaving = []

    def finish():
        for shaped, phase in leaving:
            if shaped is not None:
                drained(shaped, phase)
                continue

            @pl.when(x != rep)
            def _():
                drained(right.at[0], RIGHT1)

            @pl.when(x == rep)
            def _():
                drained(right_src, RIGHT1)

    def bias_along_x(y_):
        block = bias.at[x, y_, core]
        for step in range(1, 4):
            push(block, block, BIAS_X, device(((x + step) & 3) * 8 + y, zh, core), rep, recv_bx.at[x * 8 + y_])

    def bias_to_core(y_):
        block = bias.at[:, y_, core]
        push(block, block, BIAS_C, device(xy, zh, 1 - core), rep, recv_bc.at[y_])

    loaded(1, 4, 5)
    ln_pair = layer_norm(pair[...].reshape(4 * 128, CZ), g_pair[...])
    head_bias = dot_nt(w_bias[...], ln_pair) * LOG2E
    for a in range(4):
        bias_src[a] = head_bias[:, a * 128 : (a + 1) * 128]

    pl.semaphore_wait(barrier, 44 + jnp.where(x != rep, 1, 0))

    for step in (4, 3, 5, 2, 6, 1, 7):
        other = (zh * 4 + rep + step) & 7
        push(bias_src.at[other & 3], bias_in.at[zh * 4 + rep], BIAS1, device(xy, other >> 2, core), other & 3)
    leaving.append((bias_in.at[pl.ds(0, 7)], BIAS1))
    bias_in[zh * 4 + rep] = bias_src[rep]

    loaded(0, 2, 3)
    for s in range(2):
        tokens = layer_norm(msa[s], g_row[...])
        projected = dot(tokens, w_row[:, FEAT : 3 * FEAT]).astype(BF16)
        keys[s] = projected[:, :FEAT]
        values[s] = projected[:, FEAT:]
        for half in range(2):
            msa_halves[s, half] = msa[s, :, half * 128 : (half + 1) * 128]
            for h_ in range(2):
                for c_ in range(2):
                    queries[s, c_, half, pl.ds(h_, 32, stride=2), :] = msa_halves[
                        s, half, pl.ds(8 * h_ + 4 * c_ + rep, 32, stride=16), :
                    ]

    arrived(bias_in.at[pl.ds(0, 7)], BIAS1)
    block = jnp.concatenate(
        [jnp.concatenate([bias_in[h_ * 4 + r_] for r_ in range(4)], axis=1) for h_ in range(2)], axis=0
    )
    bias[x, y, core] = block.astype(BF16)
    for step in (4, 3, 5, 2, 6, 1, 7):
        block = bias.at[x, y, core]
        push(block, block, BIAS_Y, device(x * 8 + ((y + step) & 7), zh, core), rep, recv_by.at[y])
    bias_along_x(y)

    def row_logits(s):
        halves = [jnp.concatenate([queries[s, 0, half], queries[s, 1, half]], axis=0) for half in range(2)]
        tokens = layer_norm(jnp.concatenate(halves, axis=1), g_row[...])
        wide = dot(tokens, w_row[:, :FEAT]) * LOGIT_SCALE
        gates[s] = jax.nn.sigmoid(dot(tokens, w_row[:, 3 * FEAT :])).reshape(2, 64, FEAT)
        logits[s] = dot_nt(expand_heads(wide), keys[s]).reshape(2, 4, 8, 16, RES)

    def nearest(turn):
        away = (turn + 1) >> 1
        return (y + jnp.where((turn & 1) == 1, away, 8 - away)) & 7

    def row_softmax(y_, which):
        offset = bias[:, y_, which].astype(F32).reshape(64, RES)
        for s in range(2):
            raw = logits[s, which, :, y_].reshape(64, RES) + offset
            top = jnp.max(raw, axis=-1, keepdims=True)
            powers = jnp.exp2(raw - top)
            total = jnp.sum(powers, axis=-1, keepdims=True)
            weights[s, which, :, y_] = powers.astype(BF16).reshape(4, 16, RES)
            denom[s, which, :, y_] = jnp.broadcast_to(1.0 / total, (64, 128)).reshape(4, 16, 128)

    def row_finish(which):
        for s in range(2):
            attended = dot(weights[s, which].reshape(512, RES), values[s])
            merged = merge_heads(attended, denom[s, which].reshape(512, 128)[:, :1])
            gated = (merged * gates[s, which]).astype(BF16)
            change = dot(gated, wo_row[...])
            for half in range(2):
                staged[pl.ds(which * 4 + s * 2 + half, 64, stride=8), :] = (
                    queries[s, which, half] + change[:, half * 128 : (half + 1) * 128]
                )

    row_logits(0)
    for step in (1, 7, 2, 6, 3, 5, 4):
        source = (y + step) & 7
        landed(bias.at[0, 0, 0], recv_by.at[source])
        bias_along_x(source)
    row_logits(1)
    loaded(12)
    final_t[...] = w_fin[...].astype(F32).T.astype(BF16)

    def own_arrived(turn):
        source = nearest(turn)
        for other in range(1, 4):
            landed(bias.at[0, 0, 0], recv_bx.at[((x + other) & 3) * 8 + source])
        bias_to_core(source)
        return source

    def other_arrived(turn):
        source = nearest(turn)
        landed(bias.at[:, 0, 0], recv_bc.at[source])
        return source

    def both_queries(turn, _):
        mine_, theirs = own_arrived(turn), other_arrived(turn - 1)
        row_softmax(mine_, core)
        row_softmax(theirs, 1 - core)
        return 0

    loaded(6)
    row_softmax(own_arrived(0), core)
    lax.fori_loop(1, 8, both_queries, 0)
    row_softmax(other_arrived(7), 1 - core)
    row_finish(core)
    row_finish(1 - core)
    leaving.append((bias.at[0, pl.ds(0, 7), 0], BIAS_Y))
    leaving.append((bias.at[pl.ds(0, 3), :, 0], BIAS_X))
    leaving.append((bias.at[:, :, 0], BIAS_C))
    msa_src[...] = staged[...].astype(BF16).reshape(32, 16, 128)

    def push_msa(turn, _):
        other = far_first(turn)
        push(msa_src.at[other], msa_in.at[xy], MSA1, device(other, zh, core), rep, recv_m1.at[x])
        return 0

    lax.fori_loop(0, 31, push_msa, 0)
    leaving.append((msa_in.at[pl.ds(0, 31)], MSA1))
    msa_in[xy] = msa_src[xy]
    for step in (0, 1, 3, 2):
        source = (x + step) & 3
        landed(msa_in.at[pl.ds(0, 8 if step else 7)], recv_m1.at[source])
        start = pl.multiple_of(source * 128, 128)
        unpacked[pl.ds(start, 128), :] = msa_in[pl.ds(source * 8, 8)].astype(F32).reshape(128, 128)
        for target in range(4):
            parts = [
                jnp.concatenate(
                    [unpacked[pl.ds(start + target * 4 + s * 2 + half, 8, stride=16), :] for half in range(2)], axis=1
                )
                for s in range(2)
            ]
            col_src[target, source] = jnp.concatenate(parts, axis=0).astype(BF16)
        for turn in range(1, 4):
            other = (zc + turn) & 3
            push(col_src.at[other, source], col_in.at[zc, source], MSA2, device(xy, other >> 1, other & 1), rep)
        col_in[zc, source] = col_src[zc, source]
    leaving.append((col_in.at[pl.ds(0, 3)], MSA2))
    arrived(col_in.at[pl.ds(0, 3)], MSA2)

    loaded(7, 8, 9, 10, 11)
    middle = col_in[...].astype(F32).reshape(ROWS, FEAT)
    tokens = layer_norm(middle, g_col[...])
    projected = dot(tokens, w_col[...])
    wide = expand_heads(projected[:, :FEAT] * LOGIT_SCALE)
    col_keys = projected[:, FEAT : 2 * FEAT].astype(BF16)
    col_values = projected[:, 2 * FEAT : 3 * FEAT].astype(BF16)
    col_gates = jax.nn.sigmoid(projected[:, 3 * FEAT :])
    col_logits[...] = dot_nt(wide, col_keys)

    def col_softmax(group, _):
        rows = pl.ds(pl.multiple_of(group * 128, 128), 128)
        raw = col_logits[rows, :]
        top = jnp.max(raw, axis=-1, keepdims=True)
        powers = jnp.exp2(raw - top)
        total = jnp.sum(powers, axis=-1, keepdims=True)
        col_weights[rows, :] = powers.astype(BF16)
        col_denom[rows, :] = jnp.broadcast_to(1.0 / total, (128, 128))
        return 0

    lax.fori_loop(0, 16, col_softmax, 0, unroll=4)
    attended = dot(col_weights[...], col_values)
    merged = merge_heads(attended, col_denom[...][:, :1])
    gated = (merged * col_gates).astype(BF16)
    target_rows = middle + dot(gated, wo_col[...])

    ln_opm = layer_norm(target_rows, g_opm[...])
    factors = dot_nt(w_fac[...], ln_opm)
    right_src[...] = factors[FACTOR:].astype(BF16)
    left_src[...] = (factors[:FACTOR] * (1.0 / ROWS)).astype(BF16)
    for step in range(1, 4):
        push(left_src, left.at[x, core, rep], LEFT, dap, (rep + step) & 3)
    push(right_src, right.at[y, zh], RIGHT1, device(mirror, 1 - zh, core), x, recv_r1.at[zh])

    @pl.when(x != rep)
    def _():
        push(right_src, right.at[y, zh], RIGHT1, device(mirror, zh, core), x, recv_r1.at[zh])

    @pl.when(x == rep)
    def _():
        right[y, zh] = right_src[...]

    leaving.append((None, RIGHT1))
    leaving.append((left.at[0, 0, pl.ds(0, 3)], LEFT))
    left[x, core, rep] = left_src[...]
    for block in range(32):
        m_, x_, s = block // 8, (block // 2) % 4, block % 2
        for half in range(2):
            natural[half, pl.ds(x_ * 64 + m_ * 2 + s, 8, stride=8), :] = target_rows[
                block * 8 : (block + 1) * 8, half * 128 : (half + 1) * 128
            ]
    final[rep] = jnp.concatenate([natural[0], natural[1]], axis=1).astype(BF16)
    def right_along_y(zh_):
        for step in (4, 3, 5, 2, 6, 1, 7):
            block = right.at[y, zh_]
            push(block, block, RIGHT_Y, device(x * 8 + ((y + step) & 7), zh, core), rep, recv_ry.at[y])

    def left_to_core(x_):
        block = left.at[x_, core]
        push(block, block, LEFT_C, device(xy, zh, 1 - core), rep, recv_lc.at[x_])

    def left_unpack(x_, core_):
        rows = pl.ds(pl.multiple_of((x_ * 2 + core_) * 128, 128), 128)
        block = left[x_, core_].astype(F32).reshape(128, ROWS)
        for half in range(2):
            left_f[half, rows, :] = block[:, half * 128 : (half + 1) * 128]

    arrived(left.at[0, 0, pl.ds(0, 3)], LEFT)
    for step in (2, 1, 3):
        block = left.at[x, core]
        push(block, block, LEFT_X, device(((x + step) & 3) * 8 + y, zh, core), rep, recv_lx.at[x])
    left_to_core(x)

    @pl.when(x != rep)
    def _():
        landed(right_src, recv_r1.at[zh])

    right_along_y(zh)
    landed(right_src, recv_r1.at[1 - zh])
    right_along_y(1 - zh)
    leaving.append((right.at[pl.ds(0, 7)], RIGHT_Y))
    for step in range(1, 4):
        push(final.at[rep], final.at[rep], FINAL, dap, (rep + step) & 3)
    leaving.append((final.at[pl.ds(0, 3)], FINAL))
    left_unpack(x, core)
    for step in (1, 3, 2):
        source = (x + step) & 3
        landed(left.at[0, 0], recv_lx.at[source])
        left_to_core(source)
        left_unpack(source, core)
    leaving.append((left.at[pl.ds(0, 3), 0], LEFT_X))
    leaving.append((left.at[:, 0], LEFT_C))
    for step in (0, 1, 3, 2):
        source = (x + step) & 3
        landed(left.at[0, 0], recv_lc.at[source])
        left_unpack(source, 1 - core)

    for channel in range(FACTOR):
        left_t[pl.ds(channel * 32, 32), :] = jnp.concatenate(
            [left_f[half, pl.ds(channel, 32, stride=FACTOR), :] for half in range(2)], axis=1
        ).astype(BF16)
    quarter = lax.broadcasted_iota(jnp.int32, (FACTOR, 128), 1) // 32
    for turn in range(1, 8):
        landed(right.at[0], recv_ry.at[nearest(turn)])
    right_all = right[...].reshape(16 * FACTOR, ROWS)
    for part in range(4):
        product = dot_nt(right_all, left_t[pl.ds(part * 256, 256), :])
        for tile in range(2):
            lanes = slice(tile * 128, (tile + 1) * 128)
            for four in range(4):
                blocks = [product[(four * 4 + jq) * FACTOR : (four * 4 + jq + 1) * FACTOR, lanes] for jq in range(4)]
                for cq in range(4):
                    moved = [
                        blocks[jq] if jq == cq else pltpu.roll(blocks[jq], (32 * (jq - cq)) % 128, 1) for jq in range(4)
                    ]
                    joined = jnp.where(
                        quarter < 2,
                        jnp.where(quarter == 0, moved[0], moved[1]),
                        jnp.where(quarter == 2, moved[2], moved[3]),
                    )
                    channel = part * 8 + tile * 4 + cq
                    outer[pl.ds(channel * FACTOR, FACTOR), four * 128 : (four + 1) * 128] = joined.astype(BF16)
    flat = dot(final_t[...], outer[...])
    for four in range(4):
        update[pl.ds(four * 128, 128), :] = flat[:, four * 128 : (four + 1) * 128].T

    mine = x * 2 + core

    def result_of(target, into):
        for r_ in range(4):
            into[target, r_] = update[pl.ds(target * 4 + r_, 16, stride=32), :].astype(BF16)

    for step in (4, 5, 2, 3, 6, 7, 1):
        other = (mine + step) & 7
        result_of(other, result_src)
        push(result_src.at[other], result_in.at[mine], RESULT, device((other >> 1) * 8 + y, zh, other & 1), rep)
    leaving.append((result_in.at[pl.ds(0, 7)], RESULT))
    result_of(mine, result_in)

    arrived(final.at[pl.ds(0, 3)], FINAL)
    for half in range(2):
        for r_ in range(4):
            out_msa[pl.ds(half * 4 + r_, ROWS, stride=8), :] = final[r_, :, half * 128 : (half + 1) * 128].astype(F32)

    arrived(result_in.at[pl.ds(0, 7)], RESULT)
    for source in range(8):
        for a in range(4):
            here = pl.ds(4 * (source % 2) + source // 2, 16, stride=8)
            out_pair[a, here, :] = pair[a, here, :] + result_in[source, a].astype(F32)

    finish()


def shards(
    alignment_source_tensor,
    couple_source_tensor,
    horizontal_scale_factor,
    horizontal_projection_matrix,
    couple_scale_factor,
    couple_offset_matrix,
    horizontal_final_matrix,
    vertical_scale_factor,
    vertical_projection_matrix,
    vertical_final_matrix,
    tensorial_scale_factor,
    tensorial_factor_matrix,
    tensorial_final_matrix,
):
    operands = [
        alignment_source_tensor,
        couple_source_tensor,
        horizontal_scale_factor.reshape(1, FEAT),
        horizontal_projection_matrix,
        couple_scale_factor.reshape(1, CZ),
        couple_offset_matrix.T,
        horizontal_final_matrix,
        vertical_scale_factor.reshape(1, FEAT),
        vertical_projection_matrix,
        vertical_final_matrix,
        tensorial_scale_factor.reshape(1, FEAT),
        tensorial_factor_matrix.T,
        tensorial_final_matrix,
    ]
    vmem = pl.BlockSpec(memory_space=pltpu.VMEM)
    scratch = [pltpu.VMEM(a.shape, a.dtype) for a in operands] + [
        pltpu.VMEM((4, 8, 128), F32),
        pltpu.VMEM((8, 8, 128), F32),
        pltpu.VMEM((4, 8, 2, 16, RES), BF16),
        pltpu.VMEM((2, 2, 2, 64, 128), F32),
        pltpu.VMEM((2, 2, 64, FEAT), F32),
        pltpu.VMEM((2, RES, FEAT), BF16),
        pltpu.VMEM((2, RES, FEAT), BF16),
        pltpu.VMEM((2, 2, 4, 8, 16, RES), F32),
        pltpu.VMEM((2, 2, 4, 8, 16, RES), BF16),
        pltpu.VMEM((2, 2, 4, 8, 16, 128), F32),
        pltpu.VMEM((512, 128), F32),
        pltpu.VMEM((32, 16, 128), BF16),
        pltpu.VMEM((32, 16, 128), BF16),
        pltpu.VMEM((512, 128), F32),
        pltpu.VMEM((4, 4, 16, FEAT), BF16),
        pltpu.VMEM((4, 4, 16, FEAT), BF16),
        pltpu.VMEM((ROWS * HEADS, ROWS), F32),
        pltpu.VMEM((ROWS * HEADS, ROWS), BF16),
        pltpu.VMEM((ROWS * HEADS, 128), F32),
        pltpu.VMEM((2, ROWS, 128), F32),
        pltpu.VMEM((4, ROWS, FEAT), BF16),
        pltpu.VMEM((FACTOR, ROWS), BF16),
        pltpu.VMEM((4, 2, 4, FACTOR, ROWS), BF16),
        pltpu.VMEM((FACTOR, ROWS), BF16),
        pltpu.VMEM((8, 2, FACTOR, ROWS), BF16),
        pltpu.VMEM((2, 32 * FACTOR, 128), F32),
        pltpu.VMEM((32 * FACTOR, ROWS), BF16),
        pltpu.VMEM((CZ, FACTOR * FACTOR), BF16),
        pltpu.VMEM((FACTOR * FACTOR, 512), BF16),
        pltpu.VMEM((512, CZ), F32),
        pltpu.VMEM((8, 4, 16, CZ), BF16),
        pltpu.VMEM((8, 4, 16, CZ), BF16),
        pltpu.VMEM((2, 2, RES, 128), F32),
        pltpu.SemaphoreType.DMA((PHASES,)),
        pltpu.SemaphoreType.DMA((PHASES,)),
        pltpu.SemaphoreType.DMA((len(operands),)),
        pltpu.SemaphoreType.DMA((8,)),
        pltpu.SemaphoreType.DMA((32,)),
        pltpu.SemaphoreType.DMA((8,)),
        pltpu.SemaphoreType.DMA((2,)),
        pltpu.SemaphoreType.DMA((8,)),
        pltpu.SemaphoreType.DMA((4,)),
        pltpu.SemaphoreType.DMA((4,)),
        pltpu.SemaphoreType.DMA((4,)),
    ]
    out_msa, out_pair = pl.pallas_call(
        kernel,
        out_shape=(
            jax.ShapeDtypeStruct((ROWS * 8, 128), F32),
            jax.ShapeDtypeStruct((4, 128, CZ), F32),
        ),
        in_specs=[pl.BlockSpec(memory_space=pltpu.HBM)] * len(operands),
        out_specs=(vmem, vmem),
        scratch_shapes=scratch,
        compiler_params=pltpu.CompilerParams(
            collective_id=0, has_side_effects=True, vmem_limit_bytes=44 * 1024 * 1024
        ),
    )(*[pltpu.with_memory_space_constraint(a, pltpu.HBM) for a in operands])
    return jnp.swapaxes(out_msa.reshape(ROWS, 2, 4, 128), 1, 2).reshape(ROWS, 4, FEAT), out_pair


def solution(mesh):
    return jax.shard_map(
        shards,
        mesh=mesh,
        in_specs=(P("dap", None, None), P("dap", "rep", None)) + (P(),) * 11,
        out_specs=(P(None, "dap", None), P("dap", "rep", None)),
        check_vma=False,
    )
```

```python
import math

import jax
import jax.numpy as jnp
from jax import lax
from jax.experimental import pallas as pl
from jax.experimental.pallas import tpu as pltpu
from jax.sharding import PartitionSpec as P

HEADS = 8
HEAD_DIM = 32
FEAT = HEADS * HEAD_DIM
CZ = 128
ROWS = 256
RES = 512
FACTOR = 32
LOG2E = math.log2(math.e)
LOGIT_SCALE = HEAD_DIM ** (-0.5) * LOG2E
MESH = pl.DeviceIdType.MESH
F32 = jnp.float32
BF16 = jnp.bfloat16

BIAS1, BIAS_Y, BIAS_X, BIAS_C, MSA1, MSA2, LEFT, LEFT_X, LEFT_C, FINAL, RIGHT1, RIGHT_Y, RESULT = range(13)
PHASES = 13


def layer_norm(values, gain):
    average = jnp.mean(values, axis=-1, keepdims=True)
    centred = values - average
    variance = jnp.mean(centred * centred, axis=-1, keepdims=True)
    return (centred * lax.rsqrt(variance + 1e-05) * gain).astype(BF16)


def dot(a, b):
    return lax.dot_general(a, b, (((1,), (0,)), ((), ())), preferred_element_type=F32)


def dot_nt(a, b):
    return lax.dot_general(a, b, (((1,), (1,)), ((), ())), preferred_element_type=F32)


def head_mask():
    head = lax.broadcasted_iota(jnp.int32, (HEADS, FEAT), 0)
    channel = lax.broadcasted_iota(jnp.int32, (HEADS, FEAT), 1) // HEAD_DIM
    return (head == channel).astype(F32)


def expand_heads(queries):
    n = queries.shape[0]
    spread = jnp.broadcast_to(queries[:, None, :], (n, HEADS, FEAT))
    return (spread * head_mask()[None]).reshape(n * HEADS, FEAT).astype(BF16)


def merge_heads(attended, inverse):
    n = attended.shape[0] // HEADS
    scaled = (attended * inverse).reshape(n, HEADS, FEAT) * head_mask()[None]
    return jnp.sum(scaled, axis=1)


def kernel(*refs):
    given, (out_msa, out_pair), held, rest = refs[:13], refs[13:15], refs[15:28], refs[28:]
    msa, pair, g_row, w_row, g_pair, w_bias, wo_row, g_col, w_col, wo_col, g_opm, w_fac, w_fin = held
    (
        bias_src, bias_in, bias, queries, gates, keys, values, logits, weights, denom, staged, msa_src, msa_in,
        unpacked, col_src, col_in, col_logits, col_weights, col_denom, natural, final, left_src, left, right_src, right,
        left_f, left_t, final_t, outer, update, result_src, result_in, msa_halves,
        send, recv, load, recv_by, recv_bx, recv_bc, recv_r1, recv_ry, recv_lx, recv_lc, recv_m1,
    ) = rest
    loads = [pltpu.make_async_copy(given[k], held[k], load.at[k]) for k in range(13)]
    for k in (1, 5, 4):
        loads[k].start()

    def loaded(*which):
        for k in which:
            loads[k].wait()

    dap = lax.axis_index("dap")
    rep = lax.axis_index("rep")
    x = dap >> 5
    y = (dap >> 2) & 7
    xy = dap >> 2
    zc = dap & 3
    zh = zc >> 1
    core = zc & 1

    def device(xy_, zh_, core_):
        return xy_ * 4 + zh_ * 2 + core_

    barrier = pltpu.get_barrier_semaphore()

    def greet(dap_, rep_):
        pl.semaphore_signal(barrier, inc=1, device_id=(dap_, rep_), device_id_type=MESH)

    def far_first(turn):
        return (xy + turn + jnp.where(turn < 20, 12, -19)) & 31

    def greet_xy(turn, _):
        greet(device(far_first(turn), zh, core), rep)
        return 0

    mirror = rep * 8 + y
    greet(device(mirror, 1 - zh, core), x)

    @pl.when(x != rep)
    def _():
        greet(device(mirror, zh, core), x)

    lax.fori_loop(0, 31, greet_xy, 0)
    for step in (4, 3, 5, 2, 6, 1, 7):
        other = (zh * 4 + rep + step) & 7
        greet(device(xy, other >> 2, core), other & 3)
    for step in range(4):
        greet(device(((x + step) & 3) * 8 + y, zh, 1 - core), rep)
    greet(device(xy, 1 - zh, 1 - core), rep)
    for k in (0, 2, 3, 6, 12, 7, 8, 9, 10, 11):
        loads[k].start()

    def push(src, dst, phase, dap_, rep_, into=None):
        pltpu.make_async_remote_copy(
            src_ref=src, dst_ref=dst, send_sem=send.at[phase], recv_sem=recv.at[phase] if into is None else into,
            device_id=(dap_, rep_), device_id_type=MESH,
        ).start()

    def arrived(shaped, phase):
        landed(shaped, recv.at[phase])

    def landed(shaped, sem):
        pltpu.make_async_copy(shaped, shaped, sem).wait()

    def drained(shaped, phase):
        pltpu.make_async_copy(shaped, shaped, send.at[phase]).wait()

    leaving = []

    def finish():
        for shaped, phase in leaving:
            if shaped is not None:
                drained(shaped, phase)
                continue

            @pl.when(x != rep)
            def _():
                drained(right.at[0], RIGHT1)

            @pl.when(x == rep)
            def _():
                drained(right_src, RIGHT1)

    def bias_along_x(y_):
        block = bias.at[x, y_, core]
        for step in range(1, 4):
            push(block, block, BIAS_X, device(((x + step) & 3) * 8 + y, zh, core), rep, recv_bx.at[x * 8 + y_])

    def bias_to_core(y_):
        block = bias.at[:, y_, core]
        push(block, block, BIAS_C, device(xy, zh, 1 - core), rep, recv_bc.at[y_])

    loaded(1, 4, 5)
    ln_pair = layer_norm(pair[...].reshape(4 * 128, CZ), g_pair[...])
    head_bias = dot_nt(w_bias[...], ln_pair) * LOG2E
    for a in range(4):
        bias_src[a] = head_bias[:, a * 128 : (a + 1) * 128]

    pl.semaphore_wait(barrier, 44 + jnp.where(x != rep, 1, 0))

    for step in (4, 3, 5, 2, 6, 1, 7):
        other = (zh * 4 + rep + step) & 7
        push(bias_src.at[other & 3], bias_in.at[zh * 4 + rep], BIAS1, device(xy, other >> 2, core), other & 3)
    leaving.append((bias_in.at[pl.ds(0, 7)], BIAS1))
    bias_in[zh * 4 + rep] = bias_src[rep]

    loaded(0, 2, 3)
    for s in range(2):
        tokens = layer_norm(msa[s], g_row[...])
        projected = dot(tokens, w_row[:, FEAT : 3 * FEAT]).astype(BF16)
        keys[s] = projected[:, :FEAT]
        values[s] = projected[:, FEAT:]
        for half in range(2):
            msa_halves[s, half] = msa[s, :, half * 128 : (half + 1) * 128]
            for h_ in range(2):
                for c_ in range(2):
                    queries[s, c_, half, pl.ds(h_, 32, stride=2), :] = msa_halves[
                        s, half, pl.ds(8 * h_ + 4 * c_ + rep, 32, stride=16), :
                    ]

    arrived(bias_in.at[pl.ds(0, 7)], BIAS1)
    block = jnp.concatenate(
        [jnp.concatenate([bias_in[h_ * 4 + r_] for r_ in range(4)], axis=1) for h_ in range(2)], axis=0
    )
    bias[x, y, core] = block.astype(BF16)
    for step in (4, 3, 5, 2, 6, 1, 7):
        block = bias.at[x, y, core]
        push(block, block, BIAS_Y, device(x * 8 + ((y + step) & 7), zh, core), rep, recv_by.at[y])
    bias_along_x(y)

    def row_logits(s):
        halves = [jnp.concatenate([queries[s, 0, half], queries[s, 1, half]], axis=0) for half in range(2)]
        tokens = layer_norm(jnp.concatenate(halves, axis=1), g_row[...])
        wide = dot(tokens, w_row[:, :FEAT]) * LOGIT_SCALE
        gates[s] = jax.nn.sigmoid(dot(tokens, w_row[:, 3 * FEAT :])).reshape(2, 64, FEAT)
        logits[s] = dot_nt(expand_heads(wide), keys[s]).reshape(2, 4, 8, 16, RES)

    def nearest(turn):
        away = (turn + 1) >> 1
        return (y + jnp.where((turn & 1) == 1, away, 8 - away)) & 7

    def row_softmax(y_, which):
        offset = bias[:, y_, which].astype(F32).reshape(64, RES)
        for s in range(2):
            raw = logits[s, which, :, y_].reshape(64, RES) + offset
            top = jnp.max(raw, axis=-1, keepdims=True)
            powers = jnp.exp2(raw - top)
            total = jnp.sum(powers, axis=-1, keepdims=True)
            weights[s, which, :, y_] = powers.astype(BF16).reshape(4, 16, RES)
            denom[s, which, :, y_] = jnp.broadcast_to(1.0 / total, (64, 128)).reshape(4, 16, 128)

    def row_finish():
        for s in range(2):
            attended = dot(weights[s].reshape(1024, RES), values[s])
            merged = merge_heads(attended, denom[s].reshape(1024, 128)[:, :1])
            gated = (merged * gates[s].reshape(128, FEAT)).astype(BF16)
            change = dot(gated, wo_row[...])
            for which in range(2):
                for half in range(2):
                    staged[pl.ds(which * 4 + s * 2 + half, 64, stride=8), :] = (
                        queries[s, which, half]
                        + change[which * 64 : (which + 1) * 64, half * 128 : (half + 1) * 128]
                    )

    row_logits(0)
    for step in (1, 7, 2, 6, 3, 5, 4):
        source = (y + step) & 7
        landed(bias.at[0, 0, 0], recv_by.at[source])
        bias_along_x(source)
    row_logits(1)
    loaded(12)
    final_t[...] = w_fin[...].astype(F32).T.astype(BF16)

    def own_arrived(turn):
        source = nearest(turn)
        for other in range(1, 4):
            landed(bias.at[0, 0, 0], recv_bx.at[((x + other) & 3) * 8 + source])
        bias_to_core(source)
        return source

    def other_arrived(turn):
        source = nearest(turn)
        landed(bias.at[:, 0, 0], recv_bc.at[source])
        return source

    def both_queries(turn, _):
        mine_, theirs = own_arrived(turn), other_arrived(turn - 1)
        row_softmax(mine_, core)
        row_softmax(theirs, 1 - core)
        return 0

    loaded(6)
    row_softmax(own_arrived(0), core)
    lax.fori_loop(1, 8, both_queries, 0)
    row_softmax(other_arrived(7), 1 - core)
    row_finish()
    leaving.append((bias.at[0, pl.ds(0, 7), 0], BIAS_Y))
    leaving.append((bias.at[pl.ds(0, 3), :, 0], BIAS_X))
    leaving.append((bias.at[:, :, 0], BIAS_C))
    msa_src[...] = staged[...].astype(BF16).reshape(32, 16, 128)

    def push_msa(turn, _):
        other = far_first(turn)
        push(msa_src.at[other], msa_in.at[xy], MSA1, device(other, zh, core), rep, recv_m1.at[x])
        return 0

    lax.fori_loop(0, 31, push_msa, 0)
    leaving.append((msa_in.at[pl.ds(0, 31)], MSA1))
    msa_in[xy] = msa_src[xy]
    for step in (0, 1, 3, 2):
        source = (x + step) & 3
        landed(msa_in.at[pl.ds(0, 8 if step else 7)], recv_m1.at[source])
        start = pl.multiple_of(source * 128, 128)
        unpacked[pl.ds(start, 128), :] = msa_in[pl.ds(source * 8, 8)].astype(F32).reshape(128, 128)
        for target in range(4):
            parts = [
                jnp.concatenate(
                    [unpacked[pl.ds(start + target * 4 + s * 2 + half, 8, stride=16), :] for half in range(2)], axis=1
                )
                for s in range(2)
            ]
            col_src[target, source] = jnp.concatenate(parts, axis=0).astype(BF16)
        for turn in range(1, 4):
            other = (zc + turn) & 3
            push(col_src.at[other, source], col_in.at[zc, source], MSA2, device(xy, other >> 1, other & 1), rep)
        col_in[zc, source] = col_src[zc, source]
    leaving.append((col_in.at[pl.ds(0, 3)], MSA2))
    arrived(col_in.at[pl.ds(0, 3)], MSA2)

    loaded(7, 8, 9, 10, 11)
    middle = col_in[...].astype(F32).reshape(ROWS, FEAT)
    tokens = layer_norm(middle, g_col[...])
    projected = dot(tokens, w_col[...])
    wide = expand_heads(projected[:, :FEAT] * LOGIT_SCALE)
    col_keys = projected[:, FEAT : 2 * FEAT].astype(BF16)
    col_values = projected[:, 2 * FEAT : 3 * FEAT].astype(BF16)
    col_gates = jax.nn.sigmoid(projected[:, 3 * FEAT :])
    col_logits[...] = dot_nt(wide, col_keys)

    def col_softmax(group, _):
        rows = pl.ds(pl.multiple_of(group * 128, 128), 128)
        raw = col_logits[rows, :]
        top = jnp.max(raw, axis=-1, keepdims=True)
        powers = jnp.exp2(raw - top)
        total = jnp.sum(powers, axis=-1, keepdims=True)
        col_weights[rows, :] = powers.astype(BF16)
        col_denom[rows, :] = jnp.broadcast_to(1.0 / total, (128, 128))
        return 0

    lax.fori_loop(0, 16, col_softmax, 0, unroll=8)
    attended = dot(col_weights[...], col_values)
    merged = merge_heads(attended, col_denom[...][:, :1])
    gated = (merged * col_gates).astype(BF16)
    target_rows = middle + dot(gated, wo_col[...])

    ln_opm = layer_norm(target_rows, g_opm[...])
    factors = dot_nt(w_fac[...], ln_opm)
    right_src[...] = factors[FACTOR:].astype(BF16)
    left_src[...] = (factors[:FACTOR] * (1.0 / ROWS)).astype(BF16)
    for step in range(1, 4):
        push(left_src, left.at[x, core, rep], LEFT, dap, (rep + step) & 3)
    push(right_src, right.at[y, zh], RIGHT1, device(mirror, 1 - zh, core), x, recv_r1.at[zh])

    @pl.when(x != rep)
    def _():
        push(right_src, right.at[y, zh], RIGHT1, device(mirror, zh, core), x, recv_r1.at[zh])

    @pl.when(x == rep)
    def _():
        right[y, zh] = right_src[...]

    leaving.append((None, RIGHT1))
    leaving.append((left.at[0, 0, pl.ds(0, 3)], LEFT))
    left[x, core, rep] = left_src[...]
    for block in range(32):
        m_, x_, s = block // 8, (block // 2) % 4, block % 2
        for half in range(2):
            natural[half, pl.ds(x_ * 64 + m_ * 2 + s, 8, stride=8), :] = target_rows[
                block * 8 : (block + 1) * 8, half * 128 : (half + 1) * 128
            ]
    final[rep] = jnp.concatenate([natural[0], natural[1]], axis=1).astype(BF16)
    def right_along_y(zh_):
        for step in (4, 3, 5, 2, 6, 1, 7):
            block = right.at[y, zh_]
            push(block, block, RIGHT_Y, device(x * 8 + ((y + step) & 7), zh, core), rep, recv_ry.at[y])

    def left_to_core(x_):
        block = left.at[x_, core]
        push(block, block, LEFT_C, device(xy, zh, 1 - core), rep, recv_lc.at[x_])

    def left_unpack(x_, core_):
        rows = pl.ds(pl.multiple_of((x_ * 2 + core_) * 128, 128), 128)
        block = left[x_, core_].astype(F32).reshape(128, ROWS)
        for half in range(2):
            left_f[half, rows, :] = block[:, half * 128 : (half + 1) * 128]

    arrived(left.at[0, 0, pl.ds(0, 3)], LEFT)
    for step in (2, 1, 3):
        block = left.at[x, core]
        push(block, block, LEFT_X, device(((x + step) & 3) * 8 + y, zh, core), rep, recv_lx.at[x])
    left_to_core(x)

    @pl.when(x != rep)
    def _():
        landed(right_src, recv_r1.at[zh])

    right_along_y(zh)
    landed(right_src, recv_r1.at[1 - zh])
    right_along_y(1 - zh)
    leaving.append((right.at[pl.ds(0, 7)], RIGHT_Y))
    for step in range(1, 4):
        push(final.at[rep], final.at[rep], FINAL, dap, (rep + step) & 3)
    leaving.append((final.at[pl.ds(0, 3)], FINAL))
    left_unpack(x, core)
    for step in (1, 3, 2):
        source = (x + step) & 3
        landed(left.at[0, 0], recv_lx.at[source])
        left_to_core(source)
        left_unpack(source, core)
    leaving.append((left.at[pl.ds(0, 3), 0], LEFT_X))
    leaving.append((left.at[:, 0], LEFT_C))
    for step in (0, 1, 3, 2):
        source = (x + step) & 3
        landed(left.at[0, 0], recv_lc.at[source])
        left_unpack(source, 1 - core)

    for channel in range(FACTOR):
        left_t[pl.ds(channel * 32, 32), :] = jnp.concatenate(
            [left_f[half, pl.ds(channel, 32, stride=FACTOR), :] for half in range(2)], axis=1
        ).astype(BF16)
    quarter = lax.broadcasted_iota(jnp.int32, (FACTOR, 128), 1) // 32
    for turn in range(1, 8):
        landed(right.at[0], recv_ry.at[nearest(turn)])
    right_all = right[...].reshape(16 * FACTOR, ROWS)
    for part in range(4):
        product = dot_nt(right_all, left_t[pl.ds(part * 256, 256), :])
        for tile in range(2):
            lanes = slice(tile * 128, (tile + 1) * 128)
            for four in range(4):
                blocks = [product[(four * 4 + jq) * FACTOR : (four * 4 + jq + 1) * FACTOR, lanes] for jq in range(4)]
                for cq in range(4):
                    moved = [
                        blocks[jq] if jq == cq else pltpu.roll(blocks[jq], (32 * (jq - cq)) % 128, 1) for jq in range(4)
                    ]
                    joined = jnp.where(
                        quarter < 2,
                        jnp.where(quarter == 0, moved[0], moved[1]),
                        jnp.where(quarter == 2, moved[2], moved[3]),
                    )
                    channel = part * 8 + tile * 4 + cq
                    outer[pl.ds(channel * FACTOR, FACTOR), four * 128 : (four + 1) * 128] = joined.astype(BF16)
    flat = dot(final_t[...], outer[...])
    for four in range(4):
        update[pl.ds(four * 128, 128), :] = flat[:, four * 128 : (four + 1) * 128].T

    mine = x * 2 + core

    def result_of(target, into):
        for r_ in range(4):
            into[target, r_] = update[pl.ds(target * 4 + r_, 16, stride=32), :].astype(BF16)

    for step in (4, 5, 2, 3, 6, 7, 1):
        other = (mine + step) & 7
        result_of(other, result_src)
        push(result_src.at[other], result_in.at[mine], RESULT, device((other >> 1) * 8 + y, zh, other & 1), rep)
    leaving.append((result_in.at[pl.ds(0, 7)], RESULT))
    result_of(mine, result_in)

    arrived(final.at[pl.ds(0, 3)], FINAL)
    for half in range(2):
        for r_ in range(4):
            out_msa[pl.ds(half * 4 + r_, ROWS, stride=8), :] = final[r_, :, half * 128 : (half + 1) * 128].astype(F32)

    arrived(result_in.at[pl.ds(0, 7)], RESULT)
    for source in range(8):
        for a in range(4):
            here = pl.ds(4 * (source % 2) + source // 2, 16, stride=8)
            out_pair[a, here, :] = pair[a, here, :] + result_in[source, a].astype(F32)

    finish()


def shards(
    alignment_source_tensor,
    couple_source_tensor,
    horizontal_scale_factor,
    horizontal_projection_matrix,
    couple_scale_factor,
    couple_offset_matrix,
    horizontal_final_matrix,
    vertical_scale_factor,
    vertical_projection_matrix,
    vertical_final_matrix,
    tensorial_scale_factor,
    tensorial_factor_matrix,
    tensorial_final_matrix,
):
    operands = [
        alignment_source_tensor,
        couple_source_tensor,
        horizontal_scale_factor.reshape(1, FEAT),
        horizontal_projection_matrix,
        couple_scale_factor.reshape(1, CZ),
        couple_offset_matrix.T,
        horizontal_final_matrix,
        vertical_scale_factor.reshape(1, FEAT),
        vertical_projection_matrix,
        vertical_final_matrix,
        tensorial_scale_factor.reshape(1, FEAT),
        tensorial_factor_matrix.T,
        tensorial_final_matrix,
    ]
    vmem = pl.BlockSpec(memory_space=pltpu.VMEM)
    scratch = [pltpu.VMEM(a.shape, a.dtype) for a in operands] + [
        pltpu.VMEM((4, 8, 128), F32),
        pltpu.VMEM((8, 8, 128), F32),
        pltpu.VMEM((4, 8, 2, 16, RES), BF16),
        pltpu.VMEM((2, 2, 2, 64, 128), F32),
        pltpu.VMEM((2, 2, 64, FEAT), F32),
        pltpu.VMEM((2, RES, FEAT), BF16),
        pltpu.VMEM((2, RES, FEAT), BF16),
        pltpu.VMEM((2, 2, 4, 8, 16, RES), F32),
        pltpu.VMEM((2, 2, 4, 8, 16, RES), BF16),
        pltpu.VMEM((2, 2, 4, 8, 16, 128), F32),
        pltpu.VMEM((512, 128), F32),
        pltpu.VMEM((32, 16, 128), BF16),
        pltpu.VMEM((32, 16, 128), BF16),
        pltpu.VMEM((512, 128), F32),
        pltpu.VMEM((4, 4, 16, FEAT), BF16),
        pltpu.VMEM((4, 4, 16, FEAT), BF16),
        pltpu.VMEM((ROWS * HEADS, ROWS), F32),
        pltpu.VMEM((ROWS * HEADS, ROWS), BF16),
        pltpu.VMEM((ROWS * HEADS, 128), F32),
        pltpu.VMEM((2, ROWS, 128), F32),
        pltpu.VMEM((4, ROWS, FEAT), BF16),
        pltpu.VMEM((FACTOR, ROWS), BF16),
        pltpu.VMEM((4, 2, 4, FACTOR, ROWS), BF16),
        pltpu.VMEM((FACTOR, ROWS), BF16),
        pltpu.VMEM((8, 2, FACTOR, ROWS), BF16),
        pltpu.VMEM((2, 32 * FACTOR, 128), F32),
        pltpu.VMEM((32 * FACTOR, ROWS), BF16),
        pltpu.VMEM((CZ, FACTOR * FACTOR), BF16),
        pltpu.VMEM((FACTOR * FACTOR, 512), BF16),
        pltpu.VMEM((512, CZ), F32),
        pltpu.VMEM((8, 4, 16, CZ), BF16),
        pltpu.VMEM((8, 4, 16, CZ), BF16),
        pltpu.VMEM((2, 2, RES, 128), F32),
        pltpu.SemaphoreType.DMA((PHASES,)),
        pltpu.SemaphoreType.DMA((PHASES,)),
        pltpu.SemaphoreType.DMA((len(operands),)),
        pltpu.SemaphoreType.DMA((8,)),
        pltpu.SemaphoreType.DMA((32,)),
        pltpu.SemaphoreType.DMA((8,)),
        pltpu.SemaphoreType.DMA((2,)),
        pltpu.SemaphoreType.DMA((8,)),
        pltpu.SemaphoreType.DMA((4,)),
        pltpu.SemaphoreType.DMA((4,)),
        pltpu.SemaphoreType.DMA((4,)),
    ]
    out_msa, out_pair = pl.pallas_call(
        kernel,
        out_shape=(
            jax.ShapeDtypeStruct((ROWS * 8, 128), F32),
            jax.ShapeDtypeStruct((4, 128, CZ), F32),
        ),
        in_specs=[pl.BlockSpec(memory_space=pltpu.HBM)] * len(operands),
        out_specs=(vmem, vmem),
        scratch_shapes=scratch,
        compiler_params=pltpu.CompilerParams(
            collective_id=0, has_side_effects=True, vmem_limit_bytes=44 * 1024 * 1024
        ),
    )(*[pltpu.with_memory_space_constraint(a, pltpu.HBM) for a in operands])
    return jnp.swapaxes(out_msa.reshape(ROWS, 2, 4, 128), 1, 2).reshape(ROWS, 4, FEAT), out_pair


def solution(mesh):
    return jax.shard_map(
        shards,
        mesh=mesh,
        in_specs=(P("dap", None, None), P("dap", "rep", None)) + (P(),) * 11,
        out_specs=(P(None, "dap", None), P("dap", "rep", None)),
        check_vma=False,
    )
```
